128 devices in a mesh: replica: 8 (over y, core), tensor: 16 (over x, z).
Axes of the slice: x: 4, y: 4, z: 4, core: 2. Of those that a mesh axis runs over, the one named last changes fastest.
Arguments:
- queries: bfloat16 [512, 2, 8192], P(('replica', 'tensor')), may hold values from -200 to 200
- cached_key_rows: bfloat16 [512, 2, 64, 1024], P(('replica', 'tensor')), may hold values from -7 to 7
- cached_value_rows: bfloat16 [512, 2, 64, 1024], P(('replica', 'tensor')), may hold values from -6 to 6
- current_token_key: bfloat16 [512, 2, 1024], P(('replica', 'tensor')), may hold values from -7 to 7
- current_token_value: bfloat16 [512, 2, 1024], P(('replica', 'tensor')), may hold values from -6 to 6
- lengths: int32 [512], P(('replica', 'tensor')), may hold values from 1 to 64, as said below
- residual: bfloat16 [512, 2, 8192], P(('replica', 'tensor')), may hold values from -250 to 250
- output_projection_weight: bfloat16 [8192, 8192], P('tensor'), may hold values from -0.0625 to 0.0625
- request_adapter_index: int32 [512], P('replica'), may hold values from 0 to 383, as said below
- lowrank_down_factors: bfloat16 [384, 16, 8192], P('replica', None, 'tensor'), may hold values from -0.0625 to 0.0625
- lowrank_up_factors: bfloat16 [384, 16, 8192], P('replica', None, 'tensor'), may hold values from -1.5 to 1.5
- final_norm_scale: bfloat16 [8192], replicated, may hold values from 0.5 to 1.5
- vocabulary_head_matrix: bfloat16 [8192, 98304], P(None, ('replica', 'tensor')), may hold values from -2 to 2
Outputs:
- contrast: float32 [512, 98304], P(None, ('replica', 'tensor'))
The draws below stay inside these ranges and needn't reach their ends.
Inputs may be any that keep to these rules, and one draw needn't show every extreme that they name: `lengths`: at least one request has exactly 64 cached positions. `request_adapter_index`: adapter id // 48 is the replica group that holds the adapter; among the 64 requests of one replica group at most 16 name adapters of one holding group, and in every draw one holding group is named by exactly 16 requests of every replica group.
All inputs are finite; a program needn't handle non-finite values.
Results may differ from the reference program's by a relative error of at most 0.0023.
Values may be sent and summed in bfloat16 or wider, within the bound.
No kernel may reach another device: no remote copies, remote signals or barrier semaphores. Data moves between devices by JAX's collectives and lax.ppermute only.
A program may use at most 128 MiB of HBM per device.

```python
import math
import jax
import jax.numpy as jnp
from jax import lax

MODEL_WIDTH = 8192
HEADS = 64
KVH = 8
HD = 128
ADAPTER_RANK = 16
CTX = 64
ADAPT_GRP = 48
R_GRP = 64
ROWS = 512
CAP = 16
ADAPTER_TOTAL = 384
VOCAB = 98304
N_REPLICA = 8


def shared_keys(key):
    return jnp.clip(jax.random.normal(jax.random.fold_in(key, 901), (ROWS, 2, KVH * HD), jnp.float32), -6.0, 6.0)


def draw_current_token_key(key, part):
    common = shared_keys(key)
    return common.astype(jnp.bfloat16)


def draw_queries(key, part):
    key = jax.random.fold_in(key, 11)
    base = jnp.clip(jax.random.normal(key, (ROWS, 2, HEADS, HD), jnp.float32), -6.0, 6.0)
    return base.reshape(ROWS, 2, HEADS * HD).astype(jnp.bfloat16)


def draw_cached_key_rows(key, part):
    key = jax.random.fold_in(key, 13)
    base = jnp.clip(jax.random.normal(key, (ROWS, 2, CTX, KVH * HD), jnp.float32), -6.0, 6.0)
    return base.astype(jnp.bfloat16)


def draw_residual(key, part):
    key = jax.random.fold_in(key, 17)
    base = jnp.clip(jax.random.normal(key, (ROWS, 2, MODEL_WIDTH), jnp.float32), -6.0, 6.0)
    return base.astype(jnp.bfloat16)


def draw_vocabulary_head_matrix(key, part):
    key = jax.random.fold_in(key, 19)
    column = jnp.arange(VOCAB)
    spread = jnp.exp(jax.random.uniform(jax.random.fold_in(key, 1), (VOCAB,), jnp.float32, -0.25, 0.25))
    scale = 3.0 * (1.0 + 0.5 * column.astype(jnp.float32) / VOCAB) * spread / jnp.sqrt(jnp.float32(MODEL_WIDTH))
    weight = jnp.clip(jax.random.normal(key, (MODEL_WIDTH, VOCAB), jnp.float32), -6.0, 6.0) * scale[None, :]
    return weight.astype(jnp.bfloat16)


def draw_lengths(key, part):
    key = jax.random.fold_in(key, 23)
    base = jax.random.randint(key, (ROWS,), 1, CTX + 1)
    longest = jax.random.randint(jax.random.fold_in(key, 1), (), 0, ROWS)
    return jnp.where(jnp.arange(ROWS) == longest, CTX, base).astype(jnp.int32)


def draw_request_adapter_index(key, part):
    key = jax.random.fold_in(key, 29)
    hottest = jax.random.randint(jax.random.fold_in(key, 1), (), 0, N_REPLICA)
    others = (hottest + 1 + jnp.arange(N_REPLICA - 1)) % N_REPLICA
    spare = jnp.repeat(others, CAP)
    group_keys = jax.random.split(jax.random.fold_in(key, 2), N_REPLICA)

    def one_group(subkey):
        picked = jax.random.permutation(jax.random.fold_in(subkey, 1), spare)[:R_GRP - CAP]
        owners = jnp.concatenate([jnp.zeros((CAP,), jnp.int32) + hottest, picked.astype(jnp.int32)])
        return jax.random.permutation(jax.random.fold_in(subkey, 2), owners)
    owners = jax.vmap(one_group)(group_keys).reshape(ROWS)
    inner = jax.random.randint(jax.random.fold_in(key, 3), (ROWS,), 0, ADAPT_GRP)
    return (owners * ADAPT_GRP + inner).astype(jnp.int32)


def block_levels(key, dims, pieces, smallest, high):
    def one(position, shards_of):
        steps = jax.random.uniform(jax.random.fold_in(jax.random.fold_in(key, 6), position), (shards_of,), jnp.float32, smallest / len(pieces), high / len(pieces))
        return jnp.repeat(jnp.exp(steps), dims[position] // shards_of).reshape((-1,) + (1,) * (len(dims) - position - 1))

    level = one(*pieces[0])
    for cut in pieces[1:]:
        level = level * one(*cut)
    return level


def noise(rng, shape, scale, limit, cuts=(), held_as=jnp.bfloat16):
    level = block_levels(rng, shape, cuts, -0.22, 0.18) if cuts else 1.0
    array = jax.random.normal(rng, shape, jnp.float32) * scale * level
    return jnp.minimum(jnp.maximum(array, -limit), limit).astype(held_as)


def setup_inputs(seed: int = 0) -> dict:
    key_of = jax.random.split(jax.random.key(seed), 14)
    return {
        "queries": draw_queries(jax.random.fold_in(key_of[13], 71), 0),
        "cached_key_rows": draw_cached_key_rows(jax.random.fold_in(key_of[13], 71), 0),
        "cached_value_rows": noise(key_of[2], (ROWS, 2, CTX, KVH * HD), 1.0, 6.0, ((0, 128),)),
        "current_token_key": draw_current_token_key(jax.random.fold_in(key_of[13], 71), 0),
        "current_token_value": noise(key_of[4], (ROWS, 2, KVH * HD), 1.0, 6.0, ((0, 128),)),
        "lengths": draw_lengths(jax.random.fold_in(key_of[13], 71), 0),
        "residual": draw_residual(jax.random.fold_in(key_of[13], 71), 0),
        "output_projection_weight": noise(key_of[7], (MODEL_WIDTH, MODEL_WIDTH), MODEL_WIDTH ** -0.5, 0.0625, ((0, 16),)),
        "request_adapter_index": draw_request_adapter_index(jax.random.fold_in(key_of[13], 71), 0),
        "lowrank_down_factors": noise(key_of[9], (ADAPTER_TOTAL, ADAPTER_RANK, MODEL_WIDTH), MODEL_WIDTH ** -0.5, 0.0625, ((0, 8), (2, 16))),
        "lowrank_up_factors": noise(key_of[10], (ADAPTER_TOTAL, ADAPTER_RANK, MODEL_WIDTH), ADAPTER_RANK ** -0.5, 1.5, ((0, 8), (2, 16))),
        "final_norm_scale": jnp.clip(1.0 + 0.1 * jax.random.normal(key_of[11], (MODEL_WIDTH,), jnp.float32), 0.5, 1.5).astype(jnp.bfloat16),
        "vocabulary_head_matrix": draw_vocabulary_head_matrix(jax.random.fold_in(key_of[13], 71), 0),
    }


BETA = 0.5
LOWRANK_SCALE = 2.0
EPS = 1e-05
HIGH_PRECISION = lax.Precision.HIGHEST

def attend(queries, cached_key_rows, cached_value_rows, current_token_key, current_token_value, lengths):
    count = queries.shape[0]
    group = HEADS // KVH
    scale = 1.0 / math.sqrt(HD)
    query = queries.reshape(count, 2, KVH, group, HD).astype(jnp.float32)
    keys = cached_key_rows.reshape(count, 2, -1, KVH, HD).astype(jnp.float32)
    values = cached_value_rows.reshape(count, 2, -1, KVH, HD).astype(jnp.float32)
    fresh_key = current_token_key.reshape(count, 2, KVH, HD).astype(jnp.float32)
    fresh_value = current_token_value.reshape(count, 2, KVH, HD).astype(jnp.float32)
    scores = jnp.einsum('rbkgd,rbpkd->rbkgp', query, keys, precision=HIGH_PRECISION) * scale
    own_score = jnp.einsum('rbkgd,rbkd->rbkg', query, fresh_key, precision=HIGH_PRECISION) * scale
    places = jnp.arange(keys.shape[2], dtype=jnp.int32)
    valid = (places[None, :] < lengths[:, None])[:, None, None, None, :]
    highest = jnp.maximum(lax.optimization_barrier(jnp.max(jnp.where(valid, scores, -1e+30), axis=-1)), own_score)
    powers = jnp.where(valid, jnp.exp(scores - highest[..., None]), 0.0)
    fresh = jnp.exp(own_score - highest)
    summed = lax.optimization_barrier(jnp.sum(powers, axis=-1)) + fresh
    weights = (powers / summed[..., None]).astype(jnp.bfloat16)
    fresh_weight = (fresh / summed).astype(jnp.bfloat16)
    mixed = jnp.einsum('rbkgp,rbpkd->rbkgd', weights.astype(jnp.float32), values, precision=HIGH_PRECISION)
    mixed = mixed + fresh_weight.astype(jnp.float32)[..., None] * fresh_value[:, :, :, None, :]
    return mixed.reshape(count, 2, HEADS * HD).astype(jnp.bfloat16)

def normalize(hidden, gain):
    values = hidden.astype(jnp.float32)
    square = lax.optimization_barrier(jnp.mean(values * values, axis=-1, keepdims=True))
    return (values * lax.rsqrt(square + EPS) * gain.astype(jnp.float32)).astype(jnp.bfloat16)

def reference(queries, cached_key_rows, cached_value_rows, current_token_key, current_token_value, lengths, residual, output_projection_weight, request_adapter_index, lowrank_down_factors, lowrank_up_factors, final_norm_scale, vocabulary_head_matrix):
    attended = attend(queries, cached_key_rows, cached_value_rows, current_token_key, current_token_value, lengths)
    mixed = jnp.dot(attended.reshape(ROWS * 2, MODEL_WIDTH), output_projection_weight, preferred_element_type=jnp.float32).reshape(ROWS, 2, MODEL_WIDTH)
    expert_in = attended[:, 0, :].astype(jnp.float32)
    down_factor_rows = jnp.take(lowrank_down_factors, request_adapter_index, axis=0).astype(jnp.float32)
    rank_activation = jnp.einsum('rf,rkf->rk', expert_in, down_factor_rows, precision=HIGH_PRECISION)
    up_factor_rows = jnp.take(lowrank_up_factors, request_adapter_index, axis=0).astype(jnp.float32)
    lowrank_update = LOWRANK_SCALE * jnp.einsum('vc,vcm->vm', rank_activation, up_factor_rows, precision=HIGH_PRECISION)
    mixed = mixed.at[:, 0, :].add(lowrank_update)
    hidden = (residual.astype(jnp.float32) + mixed).astype(jnp.bfloat16)
    normed = normalize(hidden, final_norm_scale)
    logits = jnp.dot(normed.reshape(ROWS * 2, MODEL_WIDTH), vocabulary_head_matrix, preferred_element_type=jnp.float32).reshape(ROWS, 2, VOCAB)
    highest = lax.optimization_barrier(jnp.max(logits, axis=-1))
    summed = lax.optimization_barrier(jnp.sum(jnp.exp(logits - highest[..., None]), axis=-1))
    norm_log = highest + jnp.log(summed)
    logprob = logits - norm_log[..., None]
    return (1.0 + BETA) * logprob[:, 0, :] - BETA * logprob[:, 1, :]
```

```python
import math

import jax
import jax.numpy as jnp
import numpy as np
from jax import lax
from jax.experimental import pallas as pl
from jax.experimental.pallas import tpu as pltpu
from jax.sharding import Mesh
from jax.sharding import PartitionSpec as P

WIDTH = 8192
HD = 128
CTX = 64
RANK = 16
HELD = 48
REQ = 64
TEN = 16
COLS = WIDTH // TEN
VOC = 768
NY = 4
BETA = 0.5
LOWRANK_SCALE = 2.0
EPS = 1e-05
MIB = 1 << 20
LAST = (((1,), (1,)), ((), ()))
F32 = jnp.float32
BF16 = jnp.bfloat16


def params(mib):
    return pltpu.CompilerParams(vmem_limit_bytes=mib * MIB)


GROUPS = 4


def attention_kernel(len_ref, q_ref, k_ref, v_ref, ck_ref, cv_ref, res_ref, o_ref, q_s, r_s, ck_s, cv_s):
    scale = 1.0 / math.sqrt(HD)
    for r in range(4):
        q_s[2 * r : 2 * r + 2, :] = q_ref[r].astype(F32)
        r_s[2 * r : 2 * r + 2, :] = res_ref[r].astype(F32)
        ck_s[2 * r : 2 * r + 2, :] = ck_ref[r].astype(F32)
        cv_s[2 * r : 2 * r + 2, :] = cv_ref[r].astype(F32)
    row = lax.broadcasted_iota(jnp.int32, (64, 8 * CTX), 0)
    col = lax.broadcasted_iota(jnp.int32, (64, 8 * CTX), 1)
    owner = col // CTX
    limit = jnp.zeros((64, 8 * CTX), jnp.int32)
    for r in range(4):
        limit = jnp.where(owner // 2 == r, len_ref[r], limit)
    valid = (row % 8 == owner) & (col % CTX < limit)
    for g in range(GROUPS):
        lanes = slice(g * HD, (g + 1) * HD)
        base = g * 8 * HD
        q = jnp.concatenate([q_s[:, base + h * HD : base + (h + 1) * HD] for h in range(8)], axis=0)
        keys = k_ref[:, :, :, lanes].reshape(8 * CTX, HD)
        values = v_ref[:, :, :, lanes].reshape(8 * CTX, HD)
        scores = lax.dot_general(q.astype(BF16), keys, LAST, preferred_element_type=F32) * scale
        fresh_key = jnp.concatenate([ck_s[:, lanes]] * 8, axis=0)
        fresh_value = jnp.concatenate([cv_s[:, lanes]] * 8, axis=0)
        own = jnp.sum(q * fresh_key, axis=1, keepdims=True) * scale
        highest = jnp.max(jnp.where(valid, scores, -1e30), axis=1, keepdims=True)
        highest = jnp.maximum(highest, own)
        powers = jnp.where(valid, jnp.exp(scores - highest), 0.0)
        fresh = jnp.exp(own - highest)
        summed = jnp.sum(powers, axis=1, keepdims=True) + fresh
        weights = (powers / summed).astype(BF16)
        fresh_weight = (fresh / summed).astype(BF16).astype(F32)
        mixed = jnp.dot(weights, values, preferred_element_type=F32) + fresh_weight * fresh_value
        for h in range(8):
            both = jnp.concatenate(
                [mixed[h * 8 : (h + 1) * 8, :], r_s[:, base + h * HD : base + (h + 1) * HD]], axis=0
            )
            o_ref[2 * g + h // 4, :, (h % 4) * HD : (h % 4 + 1) * HD] = both.astype(BF16)


def attention(queries, keys, values, fresh_key, fresh_value, lengths, residual):
    wide = pl.BlockSpec((4, 2, GROUPS * 1024), lambda g: (0, 0, g))
    cache = pl.BlockSpec((4, 2, CTX, GROUPS * HD), lambda g: (0, 0, 0, g))
    narrow = pl.BlockSpec((4, 2, GROUPS * HD), lambda g: (0, 0, g))
    return pl.pallas_call(
        attention_kernel,
        grid=(8 // GROUPS,),
        in_specs=[
            pl.BlockSpec(memory_space=pltpu.SMEM),
            wide,
            cache,
            cache,
            narrow,
            narrow,
            wide,
        ],
        out_specs=pl.BlockSpec((2 * GROUPS, 16, COLS), lambda g: (g, 0, 0)),
        out_shape=jax.ShapeDtypeStruct((TEN, 16, COLS), BF16),
        scratch_shapes=[
            pltpu.VMEM((8, GROUPS * 1024), F32),
            pltpu.VMEM((8, GROUPS * 1024), F32),
            pltpu.VMEM((8, GROUPS * HD), F32),
            pltpu.VMEM((8, GROUPS * HD), F32),
        ],
        compiler_params=params(56),
        cost_estimate=pl.CostEstimate(flops=3 * 10**8, bytes_accessed=3 * MIB, transcendentals=262144),
    )(lengths, queries, keys, values, fresh_key, fresh_value, residual)


def start_rows(slot_ref, tables, rows_s, sem):
    held = tables[0].shape[0]

    def one(r, carry):
        slot = slot_ref[r]
        for n, table_ref in enumerate(tables):

            @pl.when((slot >= n * held) & (slot < (n + 1) * held))
            def _():
                pltpu.make_async_copy(table_ref.at[slot - n * held], rows_s.at[r], sem).start()

        return carry

    lax.fori_loop(0, REQ, one, 0, unroll=4)


def wait_rows(tables, rows_s, sem):
    pltpu.make_async_copy(tables[0].at[pl.ds(0, REQ)], rows_s, sem).wait()


def own_lanes(rows, lanes, first):
    row = lax.broadcasted_iota(jnp.int32, (rows, lanes), 0)
    lane = lax.broadcasted_iota(jnp.int32, (rows, lanes), 1)
    return row == 2 * (lane // RANK + first)


def attended_rows(got_ref):
    return got_ref[...].astype(F32)[:, 0:8, :].reshape(128, COLS).astype(BF16)


WIDE = 4


def projection_kernel(got_ref, w_ref, o_ref, att_s):
    @pl.when(pl.program_id(0) == 0)
    def _():
        att_s[...] = attended_rows(got_ref)

    for t in range(WIDE):
        part = jnp.dot(
            att_s[...], w_ref[:, t * COLS : (t + 1) * COLS], preferred_element_type=F32
        )
        o_ref[t] = part.astype(BF16)


def projection(got, weight):
    return pl.pallas_call(
        projection_kernel,
        grid=(TEN // WIDE,),
        in_specs=[
            pl.BlockSpec((TEN, 16, COLS), lambda j: (0, 0, 0)),
            pl.BlockSpec((COLS, WIDE * COLS), lambda j: (0, j)),
        ],
        out_specs=pl.BlockSpec((WIDE, 128, COLS), lambda j: (j, 0, 0)),
        out_shape=jax.ShapeDtypeStruct((TEN, 128, COLS), BF16),
        scratch_shapes=[pltpu.VMEM((128, COLS), BF16)],
        compiler_params=params(56),
        cost_estimate=pl.CostEstimate(flops=11 * 10**8, bytes_accessed=11 * MIB, transcendentals=0),
    )(got, weight)


def rank_kernel(idx_ref, got_ref, table_ref, o_ref, rows_s, sem):
    start_rows(idx_ref, [table_ref], rows_s, sem)
    attended = attended_rows(got_ref)
    wait_rows([table_ref], rows_s, sem)
    rows = rows_s[...].reshape(REQ * RANK, COLS)
    product = lax.dot_general(attended, rows, LAST, preferred_element_type=F32)
    mask = own_lanes(128, REQ * RANK, 0)
    o_ref[...] = jnp.sum(jnp.where(mask, product, 0.0), axis=0, keepdims=True)


def rank_sums(index, got, table):
    near = pl.BlockSpec(memory_space=pltpu.VMEM)
    return pl.pallas_call(
        rank_kernel,
        in_specs=[
            pl.BlockSpec(memory_space=pltpu.SMEM),
            near,
            pl.BlockSpec(memory_space=pl.ANY),
        ],
        out_specs=near,
        out_shape=jax.ShapeDtypeStruct((1, REQ * RANK), F32),
        scratch_shapes=[pltpu.VMEM((REQ, RANK, COLS), BF16), pltpu.SemaphoreType.DMA],
        compiler_params=params(56),
        cost_estimate=pl.CostEstimate(flops=14 * 10**7, bytes_accessed=2 * MIB, transcendentals=0),
    )(index, got, table)


def hidden_kernel(
    slot_ref, sums_ref, k0_ref, k1_ref, k2_ref, k3_ref, got_ref, gain_ref, own_ref, sib_ref,
    oa_ref, ob_ref, rows_s, hid_s, sem,
):
    tables = [own_ref, sib_ref]
    start_rows(slot_ref, tables, rows_s, sem)
    total = sums_ref[0].astype(F32)
    for t in range(1, TEN):
        total = total + sums_ref[t].astype(F32)
    rank = (k0_ref[...] + k1_ref[...]) + (k2_ref[...] + k3_ref[...])
    base = got_ref[...].astype(F32)[:, 8:16, :].reshape(128, COLS)
    spread = jnp.where(own_lanes(128, REQ * RANK, 0), rank, 0.0)
    high = spread.astype(BF16)
    low = (spread - high.astype(F32)).astype(BF16)
    wait_rows(tables, rows_s, sem)
    rows = rows_s[...].reshape(REQ * RANK, COLS)
    delta = jnp.dot(high, rows, preferred_element_type=F32)
    delta = delta + jnp.dot(low, rows, preferred_element_type=F32)
    hidden = (base + (total + LOWRANK_SCALE * delta)).astype(BF16).astype(F32)
    scaled = hidden * gain_ref[...].astype(F32)
    for j in range(COLS // HD):
        lanes = slice(j * HD, (j + 1) * HD)
        hid_s[j] = scaled[:, lanes]
        o_ref = oa_ref if j * HD < HALF else ob_ref
        lanes = slice(j * HD % HALF, j * HD % HALF + HD)
        for kind in range(2):
            rows = hid_s[j, pl.ds(kind, REQ, stride=2), :]
            o_ref[kind * REQ : (kind + 1) * REQ, lanes] = rows.astype(BF16)


HALF = COLS // 2


def hidden_slice(slots, sums, rank, got, gain, own, sib):
    near = pl.BlockSpec(memory_space=pltpu.VMEM)
    far = pl.BlockSpec(memory_space=pl.ANY)
    return pl.pallas_call(
        hidden_kernel,
        in_specs=[pl.BlockSpec(memory_space=pltpu.SMEM)] + [near] * 7 + [far] * 2,
        out_specs=[near, near],
        out_shape=[jax.ShapeDtypeStruct((128, HALF), BF16)] * 2,
        scratch_shapes=[
            pltpu.VMEM((REQ, RANK, COLS), BF16),
            pltpu.VMEM((COLS // HD, 128, HD), F32),
            pltpu.SemaphoreType.DMA,
        ],
        compiler_params=params(16),
        cost_estimate=pl.CostEstimate(flops=3 * 10**8, bytes_accessed=4 * MIB, transcendentals=0),
    )(slots, sums, *rank, got, gain, own, sib)


TILE = 256
TILES = 2 * VOC // TILE


def tensor_index(at, first, second):
    along_x = jnp.where(at[3] == 0, first, second)
    along_z = jnp.where(at[3] == 0, second, first)
    return lax.rem(at[1] + along_x, 4) * 4 + lax.rem(at[2] + along_z, 4)


def head_kernel(pieces, first, last, at_ref, inv_ref, *refs):
    count = 1 + max(piece[0] for piece in pieces)
    x_refs, wo_ref, ws_ref, refs = refs[:count], refs[count], refs[count + 1], refs[count + 2 :]
    if not first:
        sums_ref, square_ref, refs = refs[0], refs[1], refs[2:]
    if last:
        uo_ref, us_ref, lse_ref, x_s, w_s, acc_s, sq_s, x_sem, w_sem, in_sem, q_sem = refs
    else:
        out_ref, squares_ref, x_s, w_s, acc_s, sq_s, x_sem, w_sem, in_sem, q_sem, out_sem = refs

    for n, (which, block, offsets, absolute) in enumerate(pieces):
        lanes = pl.ds(n * HALF, HALF)
        for y in range(NY):
            if absolute:
                source = x_refs[which].at[y, block]
                place = y
            else:
                source = x_refs[which].at[block, y]
                place = lax.rem(at_ref[0] + y, NY)
            pltpu.make_async_copy(source, x_s.at[place, :, lanes], x_sem).start()
    starts = []
    for _, block, offsets, absolute in pieces:
        index = block if absolute else tensor_index(at_ref, *offsets)
        starts.append(pl.multiple_of(index * COLS + (HALF if absolute else 0), HALF))
    for tile in range(TILES):
        w_ref = wo_ref if tile < TILES // 2 else ws_ref
        columns = pl.ds(tile % (TILES // 2) * TILE, TILE)
        for n, start in enumerate(starts):
            pltpu.make_async_copy(
                w_ref.at[pl.ds(start, HALF), columns],
                w_s.at[tile, pl.ds(n * HALF, HALF), :],
                w_sem.at[tile],
            ).start()
        if not first:
            pltpu.make_async_copy(sums_ref.at[tile], acc_s.at[tile], in_sem.at[tile]).start()
    if not first:
        pltpu.make_async_copy(square_ref, sq_s, q_sem).start()
        pltpu.make_async_copy(square_ref, sq_s, q_sem).wait()
    pltpu.make_async_copy(x_s, x_s, x_sem).wait()

    def one(tile, carry):
        pltpu.make_async_copy(w_s.at[tile], w_s.at[tile], w_sem.at[tile]).wait()
        x = x_s[...].reshape(512, len(pieces) * HALF)
        part = jnp.dot(x, w_s[tile], preferred_element_type=F32)
        if first:
            acc_s[tile] = part
        else:
            pltpu.make_async_copy(sums_ref.at[tile], acc_s.at[tile], in_sem.at[tile]).wait()
            acc_s[tile] += part
        if not last:
            pltpu.make_async_copy(acc_s.at[tile], out_ref.at[tile], out_sem.at[tile]).start()
        return carry

    lax.fori_loop(0, TILES, one, 0)

    square = jnp.zeros((512, HD), F32) if first else sq_s[...]
    for n, start in enumerate(starts):
        for j in range(HALF // HD):
            piece = x_s[:, :, n * HALF + j * HD : n * HALF + (j + 1) * HD].reshape(512, HD).astype(F32)
            inverse = inv_ref[:, pl.ds(pl.multiple_of(start + j * HD, HD), HD)]
            square = square + piece * piece * inverse
    if not last:
        sq_s[...] = square
        pltpu.make_async_copy(sq_s, squares_ref, q_sem).start()
        pltpu.make_async_copy(sq_s, squares_ref, q_sem).wait()
        for tile in range(TILES):
            pltpu.make_async_copy(acc_s.at[tile], out_ref.at[tile], out_sem.at[tile]).wait()
        return

    mean = jnp.sum(square, axis=1, keepdims=True) * (1.0 / WIDTH)
    factor = lax.rsqrt(mean + EPS)
    peak = acc_s[0]
    for tile in range(1, TILES):
        peak = jnp.maximum(peak, acc_s[tile])
    peak = jnp.max(peak, axis=1, keepdims=True) * factor
    total = jnp.exp(acc_s[0] * factor - peak)
    for tile in range(1, TILES):
        total = total + jnp.exp(acc_s[tile] * factor - peak)
    lse = peak + jnp.log(jnp.sum(total, axis=1, keepdims=True))
    sq_s[...] = jnp.broadcast_to(lse, (512, HD))
    lse_ref[...] = jnp.transpose(sq_s[...])[0:1, :]
    for y in range(NY):
        a, b, c = y * 128, y * 128 + REQ, y * 128 + 128
        expert = (1.0 + BETA) * factor[a:b]
        amateur = BETA * factor[b:c]
        for tile in range(TILES):
            u_ref = uo_ref if tile < TILES // 2 else us_ref
            lanes = slice(tile % (TILES // 2) * TILE, (tile % (TILES // 2) + 1) * TILE)
            u_ref[y * REQ : (y + 1) * REQ, lanes] = (
                expert * acc_s[tile, a:b, :] - amateur * acc_s[tile, b:c, :]
            )


def head_part(place, arrays, pieces, inverse, w_own, w_sib, sums=None, last=False):
    first = sums is None
    depth = len(pieces) * HALF
    near = pl.BlockSpec(memory_space=pltpu.VMEM)
    far = pl.BlockSpec(memory_space=pl.ANY)
    partial = [(TILES, 512, TILE), (512, HD)]
    shapes = [(NY * REQ, VOC), (NY * REQ, VOC), (1, 512)] if last else partial
    dma = pltpu.SemaphoreType.DMA
    return pl.pallas_call(
        lambda *refs: head_kernel(pieces, first, last, *refs),
        in_specs=[pl.BlockSpec(memory_space=pltpu.SMEM), near]
        + [far] * (len(arrays) + 2 + (0 if first else 2)),
        out_specs=[near] * 3 if last else [far] * 2,
        out_shape=[jax.ShapeDtypeStruct(shape, F32) for shape in shapes],
        scratch_shapes=[
            pltpu.VMEM((NY, 128, depth), BF16),
            pltpu.VMEM((TILES, depth, TILE), BF16),
            pltpu.VMEM((TILES, 512, TILE), F32),
            pltpu.VMEM((512, HD), F32),
            dma,
            dma((TILES,)),
            dma((TILES,)),
            dma,
        ]
        + ([] if last else [dma((TILES,))]),
        compiler_params=params(56),
        cost_estimate=pl.CostEstimate(
            flops=2 * 512 * depth * 2 * VOC,
            bytes_accessed=depth * 4096 + (3 if first else 6) * MIB,
            transcendentals=786432 if last else 0,
        ),
    )(place, inverse, *arrays, w_own, w_sib, *(sums or ()))


def contrast_kernel(core_ref, uo_ref, us_ref, no_ref, ns_ref, o_ref):
    core = core_ref[0]
    for u_ref, n_ref, parity in ((uo_ref, no_ref, core), (us_ref, ns_ref, 1 - core)):
        column = jnp.transpose(jnp.broadcast_to(n_ref[...], (HD, 512)))
        for y in range(NY):
            a, b, c = y * 128, y * 128 + REQ, y * 128 + 128
            shift = (1.0 + BETA) * column[a:b] - BETA * column[b:c]
            rows = pl.ds(pl.multiple_of((2 * y + parity) * REQ, REQ), REQ)
            for j in range(VOC // HD):
                lanes = slice(j * HD, (j + 1) * HD)
                o_ref[rows, lanes] = u_ref[y * REQ : (y + 1) * REQ, lanes] - shift


def contrast(core, u_own, u_sib, norm_own, norm_sib):
    near = pl.BlockSpec(memory_space=pltpu.VMEM)
    return pl.pallas_call(
        contrast_kernel,
        in_specs=[pl.BlockSpec(memory_space=pltpu.SMEM)] + [near] * 4,
        out_specs=near,
        out_shape=jax.ShapeDtypeStruct((512, VOC), F32),
        compiler_params=params(16),
        cost_estimate=pl.CostEstimate(flops=10**6, bytes_accessed=4 * MIB, transcendentals=65536),
    )(core, u_own, u_sib, norm_own, norm_sib)


TENSOR = ("x", "z")
SWAP = [(0, 1), (1, 0)]


def combine(lse):
    peak = lse[0]
    for part in lse[1:]:
        peak = jnp.maximum(peak, part)
    total = jnp.exp(lse[0] - peak)
    for part in lse[1:]:
        total = total + jnp.exp(part - peak)
    return peak + jnp.log(total)


def from_offset(array, axis, offset):
    return lax.ppermute(array, axis, [((i + offset) % 4, i) for i in range(4)])


def from_core_offset(array, axes, offset):
    pairs = []
    for c in range(2):
        for x in range(4):
            for z in range(4):
                far_x = (x + offset) % 4 if axes[c] == "x" else x
                far_z = (z + offset) % 4 if axes[c] == "z" else z
                pairs.append((c * 16 + far_x * 4 + far_z, c * 16 + x * 4 + z))
    return lax.ppermute(array, ("c", "x", "z"), pairs)


FIRST = ("x", "z")
SECOND = ("z", "x")


def opposite(after, before, axes):
    half = after.shape[0] // 2
    return from_core_offset(after[:half], axes, 1), from_core_offset(before[half:], axes, 3)


def per_device(
    queries,
    cached_key_rows,
    cached_value_rows,
    current_token_key,
    current_token_value,
    lengths,
    residual,
    output_projection_weight,
    request_adapter_index,
    lowrank_down_factors,
    lowrank_up_factors,
    final_norm_scale,
    vocabulary_head_matrix,
):
    core = lax.axis_index("c").astype(jnp.int32).reshape(1)
    place = jnp.stack([lax.axis_index(axis) for axis in ("y", "x", "z", "c")]).astype(jnp.int32)
    head_sib = lax.ppermute(vocabulary_head_matrix, "c", SWAP)
    down = lax.all_gather(lowrank_down_factors, ("y", "c"), axis=0, tiled=True)
    up_after = from_offset(lowrank_up_factors, "y", 1)
    up_before = from_offset(lowrank_up_factors, "y", 3)
    owner = request_adapter_index // HELD
    slots = ((owner // 2 - place[0]) % NY) * HELD + request_adapter_index % HELD
    slots = slots + jnp.where(owner % 2 == place[3], 0, NY * HELD)
    gain = lax.dynamic_slice(final_norm_scale, (lax.axis_index(TENSOR) * COLS,), (COLS,))
    inverse = 1.0 / final_norm_scale.astype(F32)
    inverse = (inverse * inverse).reshape(1, WIDTH)

    sent = attention(
        queries,
        cached_key_rows,
        cached_value_rows,
        current_token_key,
        current_token_value,
        lengths,
        residual,
    )
    got = lax.all_to_all(sent, TENSOR, split_axis=0, concat_axis=0, tiled=True)
    partial = projection(got, output_projection_weight)
    up_after, up_before, partial = lax.optimization_barrier((up_after, up_before, partial))
    sums = lax.all_to_all(partial, TENSOR, split_axis=0, concat_axis=0, tiled=True)
    half = HELD // 2
    up_own = jnp.concatenate(
        [
            lowrank_up_factors,
            up_after,
            from_offset(up_after[:half], "y", 1),
            from_offset(up_before[half:], "y", 3),
            up_before,
        ],
        axis=0,
    )
    up_sib = lax.ppermute(up_own, "c", SWAP)
    rank = rank_sums(request_adapter_index, got, down)
    rank = sum([from_offset(rank, "x", d) for d in range(1, 4)], rank)
    rank = [rank] + [from_offset(rank, "z", d) for d in range(1, 4)]
    own, rest = hidden_slice(slots, sums, rank, got, gain.reshape(1, COLS), up_own, up_sib)

    gathered = lax.all_gather(rest, ("y", "x", "z"), axis=0, tiled=False)
    gathered = gathered.reshape(NY, TEN, 128, HALF)
    plane = jnp.stack([own] + [from_offset(own, "y", d) for d in range(1, 4)])
    after = from_core_offset(plane, FIRST, 1)
    before = from_core_offset(plane, FIRST, 3)
    far = opposite(after, before, FIRST)
    mine = jnp.stack([plane, after, jnp.concatenate(far, axis=0), before])
    after = from_core_offset(mine, SECOND, 1)
    before = from_core_offset(mine, SECOND, 3)
    weights = (inverse, vocabulary_head_matrix, head_sib)
    pieces = [(0, n, (n, 0), False) for n in range(4)]
    partial = head_part(place, [mine], pieces, *weights)
    after, before, *partial = lax.optimization_barrier((after, before, *partial))
    far = opposite(after, before, SECOND)
    pieces = [(n // 4, n % 4, (n % 4, 1 + 2 * (n // 4)), False) for n in range(8)]
    partial = head_part(place, [after, before], pieces, *weights, sums=partial)
    pieces = [(n // 2, n % 2, (n, 2), False) for n in range(4)]
    partial = head_part(place, far, pieces, *weights, sums=partial)
    pieces = [(0, n, None, True) for n in range(TEN)]
    u_own, u_send, lse = head_part(place, [gathered], pieces, *weights, sums=partial, last=True)
    for axis in ("y", "x", "z"):
        lse = combine([lse] + [from_offset(lse, axis, d) for d in range(1, 4)])
        if axis == "y":
            u_send, lse = lax.optimization_barrier((u_send, lse))
            u_sib = lax.ppermute(u_send, "c", SWAP)
    return contrast(core, u_own, u_sib, lse, lax.ppermute(lse, "c", SWAP))


def solution(mesh):
    fine = Mesh(np.asarray(mesh.devices).reshape(NY, 2, 4, 4), ("y", "c", "x", "z"))
    every = ("y", "c", "x", "z")
    group = ("y", "c")
    in_specs = (
        P(every, None, None),
        P(every, None, None, None),
        P(every, None, None, None),
        P(every, None, None),
        P(every, None, None),
        P(every),
        P(every, None, None),
        P(TENSOR, None),
        P(group),
        P(group, None, TENSOR),
        P(group, None, TENSOR),
        P(),
        P(None, every),
    )
    return jax.shard_map(
        per_device, mesh=fine, in_specs=in_specs, out_specs=P(None, every), check_vma=False
    )
```

```python
import math

import jax
import jax.numpy as jnp
import numpy as np
from jax import lax
from jax.experimental import pallas as pl
from jax.experimental.pallas import tpu as pltpu
from jax.sharding import Mesh
from jax.sharding import PartitionSpec as P

WIDTH = 8192
HD = 128
CTX = 64
RANK = 16
HELD = 48
REQ = 64
TEN = 16
COLS = WIDTH // TEN
VOC = 768
NY = 4
BETA = 0.5
LOWRANK_SCALE = 2.0
EPS = 1e-05
MIB = 1 << 20
LAST = (((1,), (1,)), ((), ()))
F32 = jnp.float32
BF16 = jnp.bfloat16


def params(mib):
    return pltpu.CompilerParams(vmem_limit_bytes=mib * MIB)


GROUPS = 4


def attention_kernel(len_ref, q_ref, k_ref, v_ref, ck_ref, cv_ref, res_ref, o_ref, q_s, r_s, ck_s, cv_s):
    scale = 1.0 / math.sqrt(HD)
    for r in range(4):
        q_s[2 * r : 2 * r + 2, :] = q_ref[r].astype(F32)
        r_s[2 * r : 2 * r + 2, :] = res_ref[r].astype(F32)
        ck_s[2 * r : 2 * r + 2, :] = ck_ref[r].astype(F32)
        cv_s[2 * r : 2 * r + 2, :] = cv_ref[r].astype(F32)
    row = lax.broadcasted_iota(jnp.int32, (64, 8 * CTX), 0)
    col = lax.broadcasted_iota(jnp.int32, (64, 8 * CTX), 1)
    owner = col // CTX
    limit = jnp.zeros((64, 8 * CTX), jnp.int32)
    for r in range(4):
        limit = jnp.where(owner // 2 == r, len_ref[r], limit)
    valid = (row % 8 == owner) & (col % CTX < limit)
    for g in range(GROUPS):
        lanes = slice(g * HD, (g + 1) * HD)
        base = g * 8 * HD
        q = jnp.concatenate([q_s[:, base + h * HD : base + (h + 1) * HD] for h in range(8)], axis=0)
        keys = k_ref[:, :, :, lanes].reshape(8 * CTX, HD)
        values = v_ref[:, :, :, lanes].reshape(8 * CTX, HD)
        scores = lax.dot_general(q.astype(BF16), keys, LAST, preferred_element_type=F32) * scale
        fresh_key = jnp.concatenate([ck_s[:, lanes]] * 8, axis=0)
        fresh_value = jnp.concatenate([cv_s[:, lanes]] * 8, axis=0)
        own = jnp.sum(q * fresh_key, axis=1, keepdims=True) * scale
        highest = jnp.max(jnp.where(valid, scores, -1e30), axis=1, keepdims=True)
        highest = jnp.maximum(highest, own)
        powers = jnp.where(valid, jnp.exp(scores - highest), 0.0)
        fresh = jnp.exp(own - highest)
        summed = jnp.sum(powers, axis=1, keepdims=True) + fresh
        weights = (powers / summed).astype(BF16)
        fresh_weight = (fresh / summed).astype(BF16).astype(F32)
        mixed = jnp.dot(weights, values, preferred_element_type=F32) + fresh_weight * fresh_value
        for h in range(8):
            both = jnp.concatenate(
                [mixed[h * 8 : (h + 1) * 8, :], r_s[:, base + h * HD : base + (h + 1) * HD]], axis=0
            )
            o_ref[2 * g + h // 4, :, (h % 4) * HD : (h % 4 + 1) * HD] = both.astype(BF16)


def attention(queries, keys, values, fresh_key, fresh_value, lengths, residual):
    wide = pl.BlockSpec((4, 2, GROUPS * 1024), lambda g: (0, 0, g))
    cache = pl.BlockSpec((4, 2, CTX, GROUPS * HD), lambda g: (0, 0, 0, g))
    narrow = pl.BlockSpec((4, 2, GROUPS * HD), lambda g: (0, 0, g))
    return pl.pallas_call(
        attention_kernel,
        grid=(8 // GROUPS,),
        in_specs=[
            pl.BlockSpec(memory_space=pltpu.SMEM),
            wide,
            cache,
            cache,
            narrow,
            narrow,
            wide,
        ],
        out_specs=pl.BlockSpec((2 * GROUPS, 16, COLS), lambda g: (g, 0, 0)),
        out_shape=jax.ShapeDtypeStruct((TEN, 16, COLS), BF16),
        scratch_shapes=[
            pltpu.VMEM((8, GROUPS * 1024), F32),
            pltpu.VMEM((8, GROUPS * 1024), F32),
            pltpu.VMEM((8, GROUPS * HD), F32),
            pltpu.VMEM((8, GROUPS * HD), F32),
        ],
        compiler_params=params(56),
        cost_estimate=pl.CostEstimate(flops=3 * 10**8, bytes_accessed=3 * MIB, transcendentals=262144),
    )(lengths, queries, keys, values, fresh_key, fresh_value, residual)


def start_rows(slot_ref, tables, rows_s, sem):
    held = tables[0].shape[0]

    def one(r, carry):
        slot = slot_ref[r]
        for n, table_ref in enumerate(tables):

            @pl.when((slot >= n * held) & (slot < (n + 1) * held))
            def _():
                pltpu.make_async_copy(table_ref.at[slot - n * held], rows_s.at[r], sem).start()

        return carry

    lax.fori_loop(0, REQ, one, 0, unroll=4)


def wait_rows(table_ref, rows_s, sem):
    pltpu.make_async_copy(table_ref.at[pl.ds(0, REQ)], rows_s, sem).wait()


def own_lanes(rows, lanes, pitch):
    row = lax.broadcasted_iota(jnp.int32, (rows, lanes), 0)
    lane = lax.broadcasted_iota(jnp.int32, (rows, lanes), 1)
    return row == pitch * (lane // RANK)


def attended_rows(got_ref):
    return got_ref[...].astype(F32)[:, 0:8, :].reshape(128, COLS).astype(BF16)


WIDE = 4


def projection_kernel(got_ref, w_ref, o_ref, att_s):
    @pl.when(pl.program_id(0) == 0)
    def _():
        att_s[...] = attended_rows(got_ref)

    for t in range(WIDE):
        part = jnp.dot(
            att_s[...], w_ref[:, t * COLS : (t + 1) * COLS], preferred_element_type=F32
        )
        o_ref[t] = part.astype(BF16)


def projection(got, weight):
    return pl.pallas_call(
        projection_kernel,
        grid=(TEN // WIDE,),
        in_specs=[
            pl.BlockSpec((TEN, 16, COLS), lambda j: (0, 0, 0)),
            pl.BlockSpec((COLS, WIDE * COLS), lambda j: (0, j)),
        ],
        out_specs=pl.BlockSpec((WIDE, 128, COLS), lambda j: (j, 0, 0)),
        out_shape=jax.ShapeDtypeStruct((TEN, 128, COLS), BF16),
        scratch_shapes=[pltpu.VMEM((128, COLS), BF16)],
        compiler_params=params(56),
        cost_estimate=pl.CostEstimate(flops=11 * 10**8, bytes_accessed=11 * MIB, transcendentals=0),
    )(got, weight)


def rank_kernel(idx_ref, got_ref, table_ref, o_ref, rows_s, sem):
    start_rows(idx_ref, [table_ref], rows_s, sem)
    attended = attended_rows(got_ref)
    wait_rows(table_ref, rows_s, sem)
    rows = rows_s[...].reshape(REQ * RANK, COLS)
    product = lax.dot_general(attended, rows, LAST, preferred_element_type=F32)
    mask = own_lanes(128, REQ * RANK, 2)
    o_ref[...] = jnp.sum(jnp.where(mask, product, 0.0), axis=0, keepdims=True)


def rank_sums(index, got, table):
    near = pl.BlockSpec(memory_space=pltpu.VMEM)
    return pl.pallas_call(
        rank_kernel,
        in_specs=[
            pl.BlockSpec(memory_space=pltpu.SMEM),
            near,
            pl.BlockSpec(memory_space=pl.ANY),
        ],
        out_specs=near,
        out_shape=jax.ShapeDtypeStruct((1, REQ * RANK), F32),
        scratch_shapes=[pltpu.VMEM((REQ, RANK, COLS), BF16), pltpu.SemaphoreType.DMA],
        compiler_params=params(56),
        cost_estimate=pl.CostEstimate(flops=14 * 10**7, bytes_accessed=2 * MIB, transcendentals=0),
    )(index, got, table)


def sum_kernel(sums_ref, got_ref, gain_ref, expert_ref, amateur_ref, hid_s):
    total = sums_ref[0].astype(F32)
    for t in range(1, TEN):
        total = total + sums_ref[t].astype(F32)
    total = total + got_ref[...].astype(F32)[:, 8:16, :].reshape(128, COLS)
    for j in range(COLS // HD):
        lanes = slice(j * HD, (j + 1) * HD)
        hid_s[j] = total[:, lanes]
        expert_ref[:, lanes] = hid_s[j, pl.ds(0, REQ, stride=2), :]
        hidden = hid_s[j, pl.ds(1, REQ, stride=2), :].astype(BF16).astype(F32)
        amateur_ref[:, lanes] = (hidden * gain_ref[:, lanes].astype(F32)).astype(BF16)


def summed_rows(sums, got, gain):
    near = pl.BlockSpec(memory_space=pltpu.VMEM)
    return pl.pallas_call(
        sum_kernel,
        in_specs=[near] * 3,
        out_specs=[near, near],
        out_shape=[
            jax.ShapeDtypeStruct((REQ, COLS), F32),
            jax.ShapeDtypeStruct((REQ, COLS), BF16),
        ],
        scratch_shapes=[pltpu.VMEM((COLS // HD, 128, HD), F32)],
        compiler_params=params(16),
        cost_estimate=pl.CostEstimate(flops=2 * 10**6, bytes_accessed=3 * MIB, transcendentals=0),
    )(sums, got, gain)


def expert_kernel(
    slot_ref, base_ref, k0_ref, k1_ref, k2_ref, k3_ref, gain_ref, own_ref, sib_ref, o_ref, rows_s, sem
):
    start_rows(slot_ref, [own_ref, sib_ref], rows_s, sem)
    rank = (k0_ref[...] + k1_ref[...]) + (k2_ref[...] + k3_ref[...])
    spread = jnp.where(own_lanes(REQ, REQ * RANK, 1), rank, 0.0)
    high = spread.astype(BF16)
    low = (spread - high.astype(F32)).astype(BF16)
    wait_rows(own_ref, rows_s, sem)
    rows = rows_s[...].reshape(REQ * RANK, COLS)
    delta = jnp.dot(high, rows, preferred_element_type=F32)
    delta = delta + jnp.dot(low, rows, preferred_element_type=F32)
    hidden = (base_ref[...] + LOWRANK_SCALE * delta).astype(BF16).astype(F32)
    o_ref[...] = (hidden * gain_ref[...].astype(F32)).astype(BF16)


def expert_rows(slots, base, rank, gain, own, sib):
    near = pl.BlockSpec(memory_space=pltpu.VMEM)
    return pl.pallas_call(
        expert_kernel,
        in_specs=[pl.BlockSpec(memory_space=pltpu.SMEM)]
        + [near] * 6
        + [pl.BlockSpec(memory_space=pl.ANY)] * 2,
        out_specs=near,
        out_shape=jax.ShapeDtypeStruct((REQ, COLS), BF16),
        scratch_shapes=[pltpu.VMEM((REQ, RANK, COLS), BF16), pltpu.SemaphoreType.DMA],
        compiler_params=params(56),
        cost_estimate=pl.CostEstimate(flops=3 * 10**8, bytes_accessed=2 * MIB, transcendentals=0),
    )(slots, base, *rank, gain, own, sib)


def tensor_index(at, first, second):
    along_x = jnp.where(at[3] == 0, first, second)
    along_z = jnp.where(at[3] == 0, second, first)
    return lax.rem(at[1] + along_x, 4) * 4 + lax.rem(at[2] + along_z, 4)


ROWS = NY * REQ
PAIR = 2 * COLS
BOTH = 2 * VOC


def head_kernel(pieces, first, last, amateur, at_ref, inv_ref, *refs):
    count = 1 + max(piece[0] for piece in pieces)
    x_refs, wo_ref, ws_ref, refs = refs[:count], refs[count], refs[count + 1], refs[count + 2 :]
    if not first:
        sums_ref, square_ref, refs = refs[0], refs[1], refs[2:]
    if last:
        other_ref, other_lse_ref, uo_ref, us_ref, lse_ref = refs[:5]
        x_s, w_s, acc_s, sq_s, x_sem, w_sem, in_sem, q_sem, other_s, o_sem = refs[5:]
    else:
        out_ref, squares_ref, x_s, w_s, acc_s, sq_s, x_sem, w_sem, in_sem, q_sem = refs

    starts = []
    for n, (which, block, offsets) in enumerate(pieces):
        index = block if offsets is None else tensor_index(at_ref, *offsets)
        start = pl.multiple_of(index * COLS, COLS)
        starts.append(start)
        run, part = n // 2, pl.ds(n % 2 * COLS, COLS)
        for y in range(NY):
            if offsets is None:
                source = x_refs[which].at[y, block]
                place = y
            else:
                source = x_refs[which].at[block, y]
                place = lax.rem(at_ref[0] + y, NY)
            pltpu.make_async_copy(source, x_s.at[run, place, :, part], x_sem.at[run]).start()
        for side, w_ref in enumerate((wo_ref, ws_ref)):
            pltpu.make_async_copy(
                w_ref.at[pl.ds(start, COLS), :],
                w_s.at[run, part, pl.ds(side * VOC, VOC)],
                w_sem.at[run],
            ).start()
    if not first:
        pltpu.make_async_copy(sums_ref, acc_s, in_sem).start()
        pltpu.make_async_copy(square_ref, sq_s, q_sem).start()
        pltpu.make_async_copy(square_ref, sq_s, q_sem).wait()
        pltpu.make_async_copy(sums_ref, acc_s, in_sem).wait()
    else:
        acc_s[...] = jnp.zeros((ROWS, BOTH), F32)
        sq_s[...] = jnp.zeros((ROWS, HD), F32)
    if last:
        pltpu.make_async_copy(other_ref, other_s, o_sem).start()

    def one(run, carry):
        pltpu.make_async_copy(x_s.at[run], x_s.at[run], x_sem.at[run]).wait()
        pltpu.make_async_copy(w_s.at[run], w_s.at[run], w_sem.at[run]).wait()
        x = x_s[run].reshape(ROWS, PAIR)
        acc_s[...] += jnp.dot(x, w_s[run], preferred_element_type=F32)
        return carry

    lax.fori_loop(0, len(pieces) // 2, one, 0)

    square = sq_s[...]
    for n, start in enumerate(starts):
        for j in range(COLS // HD):
            lanes = slice(n % 2 * COLS + j * HD, n % 2 * COLS + (j + 1) * HD)
            piece = x_s[n // 2, :, :, lanes].reshape(ROWS, HD).astype(F32)
            inverse = inv_ref[:, pl.ds(pl.multiple_of(start + j * HD, HD), HD)]
            square = square + piece * piece * inverse
    if not (last or amateur):
        sq_s[...] = square
        pltpu.make_async_copy(sq_s, squares_ref, q_sem).start()
        pltpu.make_async_copy(acc_s, out_ref, in_sem).start()
        pltpu.make_async_copy(sq_s, squares_ref, q_sem).wait()
        pltpu.make_async_copy(acc_s, out_ref, in_sem).wait()
        return

    factor = lax.rsqrt(jnp.sum(square, axis=1, keepdims=True) * (1.0 / WIDTH) + EPS)
    logits = acc_s[...] * factor
    peak = jnp.max(logits, axis=1, keepdims=True)
    lse = peak + jnp.log(jnp.sum(jnp.exp(logits - peak), axis=1, keepdims=True))
    sq_s[...] = jnp.broadcast_to(lse, (ROWS, HD))
    lse = jnp.transpose(sq_s[...])[0:1, :]
    if amateur:
        acc_s[...] = logits
        squares_ref[...] = lse
        pltpu.make_async_copy(acc_s, out_ref, in_sem).start()
        pltpu.make_async_copy(acc_s, out_ref, in_sem).wait()
        return
    lse_ref[:, 0:ROWS] = lse
    lse_ref[:, ROWS:] = other_lse_ref[...]
    pltpu.make_async_copy(other_ref, other_s, o_sem).wait()
    mixed = (1.0 + BETA) * logits - BETA * other_s[...]
    uo_ref[...] = mixed[:, :VOC]
    us_ref[...] = mixed[:, VOC:]


def head_part(place, arrays, pieces, inverse, w_own, w_sib, sums=None, other=None, amateur=False):
    first, last = sums is None, other is not None
    depth = len(pieces) * COLS
    runs = len(pieces) // 2
    near = pl.BlockSpec(memory_space=pltpu.VMEM)
    far = pl.BlockSpec(memory_space=pl.ANY)
    if last:
        shapes, out_specs = [(ROWS, VOC), (ROWS, VOC), (1, 2 * ROWS)], [near] * 3
    elif amateur:
        shapes, out_specs = [(ROWS, BOTH), (1, ROWS)], [far, near]
    else:
        shapes, out_specs = [(ROWS, BOTH), (ROWS, HD)], [far, far]
    dma = pltpu.SemaphoreType.DMA
    return pl.pallas_call(
        lambda *refs: head_kernel(pieces, first, last, amateur, *refs),
        in_specs=[pl.BlockSpec(memory_space=pltpu.SMEM), near]
        + [far] * (len(arrays) + 2 + (0 if first else 2))
        + ([far, near] if last else []),
        out_specs=out_specs,
        out_shape=[jax.ShapeDtypeStruct(shape, F32) for shape in shapes],
        scratch_shapes=[
            pltpu.VMEM((runs, NY, REQ, PAIR), BF16),
            pltpu.VMEM((runs, PAIR, BOTH), BF16),
            pltpu.VMEM((ROWS, BOTH), F32),
            pltpu.VMEM((ROWS, HD), F32),
            dma((runs,)),
            dma((runs,)),
            dma,
            dma,
        ]
        + ([pltpu.VMEM((ROWS, BOTH), F32), dma] if last else []),
        compiler_params=params(56),
        cost_estimate=pl.CostEstimate(
            flops=ROWS * depth,
            bytes_accessed=depth * 64,
            transcendentals=0,
        ),
    )(place, inverse, *arrays, w_own, w_sib, *(sums or ()), *(other or ()))


def contrast_kernel(core_ref, uo_ref, us_ref, no_ref, ns_ref, o_ref):
    core = core_ref[0]
    for u_ref, n_ref, parity in ((uo_ref, no_ref, core), (us_ref, ns_ref, 1 - core)):
        column = jnp.transpose(jnp.broadcast_to(n_ref[...], (HD, 512)))
        for y in range(NY):
            a, b = y * REQ, ROWS + y * REQ
            shift = (1.0 + BETA) * column[a : a + REQ] - BETA * column[b : b + REQ]
            rows = pl.ds(pl.multiple_of((2 * y + parity) * REQ, REQ), REQ)
            for j in range(VOC // HD):
                lanes = slice(j * HD, (j + 1) * HD)
                o_ref[rows, lanes] = u_ref[y * REQ : (y + 1) * REQ, lanes] - shift


def contrast(core, u_own, u_sib, norm_own, norm_sib):
    near = pl.BlockSpec(memory_space=pltpu.VMEM)
    return pl.pallas_call(
        contrast_kernel,
        in_specs=[pl.BlockSpec(memory_space=pltpu.SMEM)] + [near] * 4,
        out_specs=near,
        out_shape=jax.ShapeDtypeStruct((512, VOC), F32),
        compiler_params=params(16),
        cost_estimate=pl.CostEstimate(flops=10**6, bytes_accessed=4 * MIB, transcendentals=65536),
    )(core, u_own, u_sib, norm_own, norm_sib)


TENSOR = ("x", "z")
SWAP = [(0, 1), (1, 0)]


def combine(lse):
    peak = lse[0]
    for part in lse[1:]:
        peak = jnp.maximum(peak, part)
    total = jnp.exp(lse[0] - peak)
    for part in lse[1:]:
        total = total + jnp.exp(part - peak)
    return peak + jnp.log(total)


def from_offset(array, axis, offset):
    return lax.ppermute(array, axis, [((i + offset) % 4, i) for i in range(4)])


def from_core_offset(array, axes, offset):
    pairs = []
    for c in range(2):
        for x in range(4):
            for z in range(4):
                far_x = (x + offset) % 4 if axes[c] == "x" else x
                far_z = (z + offset) % 4 if axes[c] == "z" else z
                pairs.append((c * 16 + far_x * 4 + far_z, c * 16 + x * 4 + z))
    return lax.ppermute(array, ("c", "x", "z"), pairs)


FIRST = ("x", "z")
SECOND = ("z", "x")


def opposite(after, before, axes):
    half = after.shape[0] // 2
    return from_core_offset(after[:half], axes, 1), from_core_offset(before[half:], axes, 3)


def per_device(
    queries,
    cached_key_rows,
    cached_value_rows,
    current_token_key,
    current_token_value,
    lengths,
    residual,
    output_projection_weight,
    request_adapter_index,
    lowrank_down_factors,
    lowrank_up_factors,
    final_norm_scale,
    vocabulary_head_matrix,
):
    core = lax.axis_index("c").astype(jnp.int32).reshape(1)
    place = jnp.stack([lax.axis_index(axis) for axis in ("y", "x", "z", "c")]).astype(jnp.int32)
    head_sib = lax.ppermute(vocabulary_head_matrix, "c", SWAP)
    down = lax.all_gather(lowrank_down_factors, ("y", "c"), axis=0, tiled=True)
    owner = request_adapter_index // HELD
    slots = ((owner // 2 - place[0]) % NY) * HELD + request_adapter_index % HELD
    slots = slots + jnp.where(owner % 2 == place[3], 0, NY * HELD)
    up_after = from_offset(lowrank_up_factors, "y", 1)
    up_before = from_offset(lowrank_up_factors, "y", 3)
    gain = lax.dynamic_slice(final_norm_scale, (lax.axis_index(TENSOR) * COLS,), (COLS,))
    gain = gain.reshape(1, COLS)
    inverse = 1.0 / final_norm_scale.astype(F32)
    inverse = (inverse * inverse).reshape(1, WIDTH)

    sent = attention(
        queries,
        cached_key_rows,
        cached_value_rows,
        current_token_key,
        current_token_value,
        lengths,
        residual,
    )
    got = lax.all_to_all(sent, TENSOR, split_axis=0, concat_axis=0, tiled=True)
    partial = projection(got, output_projection_weight)
    up_after, up_before, partial = lax.optimization_barrier((up_after, up_before, partial))
    sums = lax.all_to_all(partial, TENSOR, split_axis=0, concat_axis=0, tiled=True)
    rank = rank_sums(request_adapter_index, got, down)
    half = HELD // 2
    up_far = (from_offset(up_after[:half], "y", 1), from_offset(up_before[half:], "y", 3))
    up_own = jnp.concatenate([lowrank_up_factors, up_after, *up_far, up_before], axis=0)
    up_own, sums = lax.optimization_barrier((up_own, sums))
    up_sib = lax.ppermute(up_own, "c", SWAP)
    base, amateur = summed_rows(sums, got, gain)
    gathered = lax.all_gather(amateur, ("y", "x", "z"), axis=0, tiled=False)
    gathered = gathered.reshape(NY, TEN, REQ, COLS)
    rank, base = lax.optimization_barrier((rank, base))
    rank = sum([from_offset(rank, "x", d) for d in range(1, 4)], rank)
    rank = [rank] + [from_offset(rank, "z", d) for d in range(1, 4)]
    expert = expert_rows(slots, base, rank, gain, up_own, up_sib)

    plane = jnp.stack([expert] + [from_offset(expert, "y", d) for d in range(1, 4)])
    after = from_core_offset(plane, FIRST, 1)
    before = from_core_offset(plane, FIRST, 3)
    mine = jnp.stack([plane, after, from_core_offset(plane, FIRST, 2), before])
    after = from_core_offset(mine, SECOND, 1)
    before = from_core_offset(mine, SECOND, 3)
    weights = (inverse, vocabulary_head_matrix, head_sib)
    pieces = [(0, n, (n, 0)) for n in range(4)]
    partial = head_part(place, [mine], pieces, *weights)
    after, before, *partial = lax.optimization_barrier((after, before, *partial))
    far = opposite(after, before, SECOND)
    pieces = [(n // 4, n % 4, (n % 4, 1 + 2 * (n // 4))) for n in range(8)]
    partial = head_part(place, [after, before], pieces, *weights, sums=partial)
    gathered, *partial = lax.optimization_barrier((gathered, *partial))
    pieces = [(0, n, None) for n in range(TEN)]
    other = head_part(place, [gathered], pieces, *weights, amateur=True)
    pieces = [(n // 2, n % 2, (n, 2)) for n in range(4)]
    u_own, u_send, lse = head_part(place, far, pieces, *weights, sums=partial, other=other)
    for axis in ("y", "x", "z"):
        lse = combine([lse] + [from_offset(lse, axis, d) for d in range(1, 4)])
        if axis == "y":
            u_send, lse = lax.optimization_barrier((u_send, lse))
            u_sib = lax.ppermute(u_send, "c", SWAP)
    return contrast(core, u_own, u_sib, lse, lax.ppermute(lse, "c", SWAP))


def solution(mesh):
    fine = Mesh(np.asarray(mesh.devices).reshape(NY, 2, 4, 4), ("y", "c", "x", "z"))
    every = ("y", "c", "x", "z")
    group = ("y", "c")
    in_specs = (
        P(every, None, None),
        P(every, None, None, None),
        P(every, None, None, None),
        P(every, None, None),
        P(every, None, None),
        P(every),
        P(every, None, None),
        P(TENSOR, None),
        P(group),
        P(group, None, TENSOR),
        P(group, None, TENSOR),
        P(),
        P(None, every),
    )
    return jax.shard_map(
        per_device, mesh=fine, in_specs=in_specs, out_specs=P(None, every), check_vma=False
    )
```

```python
import math

import jax
import jax.numpy as jnp
import numpy as np
from jax import lax
from jax.experimental import pallas as pl
from jax.experimental.pallas import tpu as pltpu
from jax.sharding import Mesh
from jax.sharding import PartitionSpec as P

WIDTH = 8192
HD = 128
CTX = 64
RANK = 16
HELD = 48
REQ = 64
TEN = 16
COLS = WIDTH // TEN
VOC = 768
NY = 4
BETA = 0.5
LOWRANK_SCALE = 2.0
EPS = 1e-05
MIB = 1 << 20
LAST = (((1,), (1,)), ((), ()))
F32 = jnp.float32
BF16 = jnp.bfloat16


def params(mib):
    return pltpu.CompilerParams(vmem_limit_bytes=mib * MIB)


GROUPS = 4


def attention_kernel(len_ref, q_ref, k_ref, v_ref, ck_ref, cv_ref, res_ref, o_ref, q_s, r_s, ck_s, cv_s):
    scale = 1.0 / math.sqrt(HD)
    for r in range(4):
        q_s[2 * r : 2 * r + 2, :] = q_ref[r].astype(F32)
        r_s[2 * r : 2 * r + 2, :] = res_ref[r].astype(F32)
        ck_s[2 * r : 2 * r + 2, :] = ck_ref[r].astype(F32)
        cv_s[2 * r : 2 * r + 2, :] = cv_ref[r].astype(F32)
    row = lax.broadcasted_iota(jnp.int32, (64, 8 * CTX), 0)
    col = lax.broadcasted_iota(jnp.int32, (64, 8 * CTX), 1)
    owner = col // CTX
    limit = jnp.zeros((64, 8 * CTX), jnp.int32)
    for r in range(4):
        limit = jnp.where(owner // 2 == r, len_ref[r], limit)
    valid = (row % 8 == owner) & (col % CTX < limit)
    for g in range(GROUPS):
        lanes = slice(g * HD, (g + 1) * HD)
        base = g * 8 * HD
        q = jnp.concatenate([q_s[:, base + h * HD : base + (h + 1) * HD] for h in range(8)], axis=0)
        keys = k_ref[:, :, :, lanes].reshape(8 * CTX, HD)
        values = v_ref[:, :, :, lanes].reshape(8 * CTX, HD)
        scores = lax.dot_general(q.astype(BF16), keys, LAST, preferred_element_type=F32) * scale
        fresh_key = jnp.concatenate([ck_s[:, lanes]] * 8, axis=0)
        fresh_value = jnp.concatenate([cv_s[:, lanes]] * 8, axis=0)
        own = jnp.sum(q * fresh_key, axis=1, keepdims=True) * scale
        highest = jnp.max(jnp.where(valid, scores, -1e30), axis=1, keepdims=True)
        highest = jnp.maximum(highest, own)
        powers = jnp.where(valid, jnp.exp(scores - highest), 0.0)
        fresh = jnp.exp(own - highest)
        summed = jnp.sum(powers, axis=1, keepdims=True) + fresh
        weights = (powers / summed).astype(BF16)
        fresh_weight = (fresh / summed).astype(BF16).astype(F32)
        mixed = jnp.dot(weights, values, preferred_element_type=F32) + fresh_weight * fresh_value
        for h in range(8):
            both = jnp.concatenate(
                [mixed[h * 8 : (h + 1) * 8, :], r_s[:, base + h * HD : base + (h + 1) * HD]], axis=0
            )
            o_ref[2 * g + h // 4, :, (h % 4) * HD : (h % 4 + 1) * HD] = both.astype(BF16)


def attention(queries, keys, values, fresh_key, fresh_value, lengths, residual):
    wide = pl.BlockSpec((4, 2, GROUPS * 1024), lambda g: (0, 0, g))
    cache = pl.BlockSpec((4, 2, CTX, GROUPS * HD), lambda g: (0, 0, 0, g))
    narrow = pl.BlockSpec((4, 2, GROUPS * HD), lambda g: (0, 0, g))
    return pl.pallas_call(
        attention_kernel,
        grid=(8 // GROUPS,),
        in_specs=[
            pl.BlockSpec(memory_space=pltpu.SMEM),
            wide,
            cache,
            cache,
            narrow,
            narrow,
            wide,
        ],
        out_specs=pl.BlockSpec((2 * GROUPS, 16, COLS), lambda g: (g, 0, 0)),
        out_shape=jax.ShapeDtypeStruct((TEN, 16, COLS), BF16),
        scratch_shapes=[
            pltpu.VMEM((8, GROUPS * 1024), F32),
            pltpu.VMEM((8, GROUPS * 1024), F32),
            pltpu.VMEM((8, GROUPS * HD), F32),
            pltpu.VMEM((8, GROUPS * HD), F32),
        ],
        compiler_params=params(56),
        cost_estimate=pl.CostEstimate(flops=3 * 10**8, bytes_accessed=3 * MIB, transcendentals=262144),
    )(lengths, queries, keys, values, fresh_key, fresh_value, residual)


def start_rows(slot_ref, tables, rows_s, sem):
    held = tables[0].shape[0]

    def one(r, carry):
        slot = slot_ref[r]
        for n, table_ref in enumerate(tables):

            @pl.when((slot >= n * held) & (slot < (n + 1) * held))
            def _():
                pltpu.make_async_copy(table_ref.at[slot - n * held], rows_s.at[r], sem).start()

        return carry

    lax.fori_loop(0, REQ, one, 0, unroll=4)


def wait_rows(table_ref, rows_s, sem):
    pltpu.make_async_copy(table_ref.at[pl.ds(0, REQ)], rows_s, sem).wait()


def own_lanes(rows, lanes, pitch):
    row = lax.broadcasted_iota(jnp.int32, (rows, lanes), 0)
    lane = lax.broadcasted_iota(jnp.int32, (rows, lanes), 1)
    return row == pitch * (lane // RANK)


def attended_rows(got_ref):
    return got_ref[...].astype(F32)[:, 0:8, :].reshape(128, COLS)


def split_kinds(rows, kinds_s):
    kinds = [[], []]
    for j in range(COLS // HD):
        kinds_s[j] = rows[:, j * HD : (j + 1) * HD]
        for kind in range(2):
            kinds[kind].append(kinds_s[j, pl.ds(kind, REQ, stride=2), :])
    return [jnp.concatenate(parts, axis=1) for parts in kinds]


WIDE = 4


def projection_kernel(got_ref, w_ref, expert_ref, amateur_ref, att_s, kinds_s):
    @pl.when(pl.program_id(0) == 0)
    def _():
        att_s[...] = jnp.concatenate(split_kinds(attended_rows(got_ref), kinds_s), axis=0).astype(BF16)

    for t in range(WIDE):
        part = jnp.dot(
            att_s[...], w_ref[:, t * COLS : (t + 1) * COLS], preferred_element_type=F32
        )
        expert_ref[t] = part[:REQ].astype(BF16)
        amateur_ref[t] = part[REQ:].astype(BF16)


def projection(got, weight):
    return pl.pallas_call(
        projection_kernel,
        grid=(TEN // WIDE,),
        in_specs=[
            pl.BlockSpec((TEN, 16, COLS), lambda j: (0, 0, 0)),
            pl.BlockSpec((COLS, WIDE * COLS), lambda j: (0, j)),
        ],
        out_specs=[pl.BlockSpec((WIDE, REQ, COLS), lambda j: (j, 0, 0))] * 2,
        out_shape=[jax.ShapeDtypeStruct((TEN, REQ, COLS), BF16)] * 2,
        scratch_shapes=[
            pltpu.VMEM((128, COLS), BF16),
            pltpu.VMEM((COLS // HD, 128, HD), F32),
        ],
        compiler_params=params(56),
        cost_estimate=pl.CostEstimate(flops=11 * 10**8, bytes_accessed=11 * MIB, transcendentals=0),
    )(got, weight)


def rank_kernel(idx_ref, got_ref, table_ref, o_ref, rows_s, sem):
    start_rows(idx_ref, [table_ref], rows_s, sem)
    attended = attended_rows(got_ref).astype(BF16)
    wait_rows(table_ref, rows_s, sem)
    rows = rows_s[...].reshape(REQ * RANK, COLS)
    product = lax.dot_general(attended, rows, LAST, preferred_element_type=F32)
    mask = own_lanes(128, REQ * RANK, 2)
    o_ref[...] = jnp.sum(jnp.where(mask, product, 0.0), axis=0, keepdims=True)


def rank_sums(index, got, table):
    near = pl.BlockSpec(memory_space=pltpu.VMEM)
    return pl.pallas_call(
        rank_kernel,
        in_specs=[
            pl.BlockSpec(memory_space=pltpu.SMEM),
            near,
            pl.BlockSpec(memory_space=pl.ANY),
        ],
        out_specs=near,
        out_shape=jax.ShapeDtypeStruct((1, REQ * RANK), F32),
        scratch_shapes=[pltpu.VMEM((REQ, RANK, COLS), BF16), pltpu.SemaphoreType.DMA],
        compiler_params=params(56),
        cost_estimate=pl.CostEstimate(flops=14 * 10**7, bytes_accessed=2 * MIB, transcendentals=0),
    )(index, got, table)


def add_all(sums_ref):
    total = sums_ref[0].astype(F32)
    for t in range(1, TEN):
        total = total + sums_ref[t].astype(F32)
    return total


def residual_rows(got_ref):
    return got_ref[...].astype(F32)[:, 8:16, :].reshape(128, COLS)


def amateur_kernel(sums_ref, got_ref, gain_ref, o_ref, kinds_s):
    base = split_kinds(residual_rows(got_ref), kinds_s)[1]
    hidden = (base + add_all(sums_ref)).astype(BF16).astype(F32)
    o_ref[...] = (hidden * gain_ref[...].astype(F32)).astype(BF16)


def amateur_rows(sums, got, gain):
    near = pl.BlockSpec(memory_space=pltpu.VMEM)
    return pl.pallas_call(
        amateur_kernel,
        in_specs=[near] * 3,
        out_specs=near,
        out_shape=jax.ShapeDtypeStruct((REQ, COLS), BF16),
        scratch_shapes=[pltpu.VMEM((COLS // HD, 128, HD), F32)],
        compiler_params=params(16),
        cost_estimate=pl.CostEstimate(flops=10**6, bytes_accessed=2 * MIB, transcendentals=0),
    )(sums, got, gain)


def expert_kernel(
    slot_ref, sums_ref, got_ref, k0_ref, k1_ref, k2_ref, k3_ref, gain_ref, own_ref, sib_ref,
    o_ref, rows_s, kinds_s, sem,
):
    start_rows(slot_ref, [own_ref, sib_ref], rows_s, sem)
    base = split_kinds(residual_rows(got_ref), kinds_s)[0] + add_all(sums_ref)
    rank = (k0_ref[...] + k1_ref[...]) + (k2_ref[...] + k3_ref[...])
    spread = jnp.where(own_lanes(REQ, REQ * RANK, 1), rank, 0.0)
    high = spread.astype(BF16)
    low = (spread - high.astype(F32)).astype(BF16)
    wait_rows(own_ref, rows_s, sem)
    rows = rows_s[...].reshape(REQ * RANK, COLS)
    delta = jnp.dot(high, rows, preferred_element_type=F32)
    delta = delta + jnp.dot(low, rows, preferred_element_type=F32)
    hidden = (base + LOWRANK_SCALE * delta).astype(BF16).astype(F32)
    o_ref[...] = (hidden * gain_ref[...].astype(F32)).astype(BF16)


def expert_rows(slots, sums, got, rank, gain, own, sib):
    near = pl.BlockSpec(memory_space=pltpu.VMEM)
    return pl.pallas_call(
        expert_kernel,
        in_specs=[pl.BlockSpec(memory_space=pltpu.SMEM)]
        + [near] * 7
        + [pl.BlockSpec(memory_space=pl.ANY)] * 2,
        out_specs=near,
        out_shape=jax.ShapeDtypeStruct((REQ, COLS), BF16),
        scratch_shapes=[
            pltpu.VMEM((REQ, RANK, COLS), BF16),
            pltpu.VMEM((COLS // HD, 128, HD), F32),
            pltpu.SemaphoreType.DMA,
        ],
        compiler_params=params(56),
        cost_estimate=pl.CostEstimate(flops=3 * 10**8, bytes_accessed=2 * MIB, transcendentals=0),
    )(slots, sums, got, *rank, gain, own, sib)


def tensor_index(at, first, second):
    along_x = jnp.where(at[3] == 0, first, second)
    along_z = jnp.where(at[3] == 0, second, first)
    return lax.rem(at[1] + along_x, 4) * 4 + lax.rem(at[2] + along_z, 4)


ROWS = NY * REQ
PAIR = 2 * COLS
BOTH = 2 * VOC


def head_kernel(pieces, first, last, amateur, at_ref, inv_ref, *refs):
    count = 1 + max(piece[0] for piece in pieces)
    x_refs, wo_ref, ws_ref, refs = refs[:count], refs[count], refs[count + 1], refs[count + 2 :]
    if not first:
        sums_ref, square_ref, refs = refs[0], refs[1], refs[2:]
    if last:
        other_ref, other_lse_ref, uo_ref, us_ref, lse_ref = refs[:5]
        x_s, w_s, acc_s, sq_s, x_sem, w_sem, in_sem, q_sem, other_s, o_sem = refs[5:]
    else:
        out_ref, squares_ref, x_s, w_s, acc_s, sq_s, x_sem, w_sem, in_sem, q_sem = refs

    starts = []
    for n, (which, block, offsets) in enumerate(pieces):
        index = block if offsets is None else tensor_index(at_ref, *offsets)
        start = pl.multiple_of(index * COLS, COLS)
        starts.append(start)
        run, part = n // 2, pl.ds(n % 2 * COLS, COLS)
        for y in range(NY):
            if offsets is None:
                source = x_refs[which].at[y, block]
                place = y
            else:
                source = x_refs[which].at[block, y]
                place = lax.rem(at_ref[0] + y, NY)
            pltpu.make_async_copy(source, x_s.at[run, place, :, part], x_sem.at[run]).start()
        for side, w_ref in enumerate((wo_ref, ws_ref)):
            pltpu.make_async_copy(
                w_ref.at[pl.ds(start, COLS), :],
                w_s.at[run, part, pl.ds(side * VOC, VOC)],
                w_sem.at[run],
            ).start()
    if not first:
        pltpu.make_async_copy(sums_ref, acc_s, in_sem).start()
        pltpu.make_async_copy(square_ref, sq_s, q_sem).start()
        pltpu.make_async_copy(square_ref, sq_s, q_sem).wait()
        pltpu.make_async_copy(sums_ref, acc_s, in_sem).wait()
    else:
        acc_s[...] = jnp.zeros((ROWS, BOTH), F32)
        sq_s[...] = jnp.zeros((ROWS, HD), F32)
    if last:
        pltpu.make_async_copy(other_ref, other_s, o_sem).start()

    def one(run, carry):
        pltpu.make_async_copy(x_s.at[run], x_s.at[run], x_sem.at[run]).wait()
        pltpu.make_async_copy(w_s.at[run], w_s.at[run], w_sem.at[run]).wait()
        x = x_s[run].reshape(ROWS, PAIR)
        acc_s[...] += jnp.dot(x, w_s[run], preferred_element_type=F32)
        return carry

    lax.fori_loop(0, len(pieces) // 2, one, 0)

    square = sq_s[...]
    for n, start in enumerate(starts):
        for j in range(COLS // HD):
            lanes = slice(n % 2 * COLS + j * HD, n % 2 * COLS + (j + 1) * HD)
            piece = x_s[n // 2, :, :, lanes].reshape(ROWS, HD).astype(F32)
            inverse = inv_ref[:, pl.ds(pl.multiple_of(start + j * HD, HD), HD)]
            square = square + piece * piece * inverse
    if not (last or amateur):
        sq_s[...] = square
        pltpu.make_async_copy(sq_s, squares_ref, q_sem).start()
        pltpu.make_async_copy(acc_s, out_ref, in_sem).start()
        pltpu.make_async_copy(sq_s, squares_ref, q_sem).wait()
        pltpu.make_async_copy(acc_s, out_ref, in_sem).wait()
        return

    factor = lax.rsqrt(jnp.sum(square, axis=1, keepdims=True) * (1.0 / WIDTH) + EPS)
    logits = acc_s[...] * factor
    peak = jnp.max(logits, axis=1, keepdims=True)
    lse = peak + jnp.log(jnp.sum(jnp.exp(logits - peak), axis=1, keepdims=True))
    sq_s[...] = jnp.broadcast_to(lse, (ROWS, HD))
    lse = jnp.transpose(sq_s[...])[0:1, :]
    if amateur:
        acc_s[...] = logits
        squares_ref[...] = lse
        pltpu.make_async_copy(acc_s, out_ref, in_sem).start()
        pltpu.make_async_copy(acc_s, out_ref, in_sem).wait()
        return
    lse_ref[:, 0:ROWS] = lse
    lse_ref[:, ROWS:] = other_lse_ref[...]
    pltpu.make_async_copy(other_ref, other_s, o_sem).wait()
    mixed = (1.0 + BETA) * logits - BETA * other_s[...]
    uo_ref[...] = mixed[:, :VOC]
    us_ref[...] = mixed[:, VOC:]


def head_part(place, arrays, pieces, inverse, w_own, w_sib, sums=None, other=None, amateur=False):
    first, last = sums is None, other is not None
    depth = len(pieces) * COLS
    runs = len(pieces) // 2
    near = pl.BlockSpec(memory_space=pltpu.VMEM)
    far = pl.BlockSpec(memory_space=pl.ANY)
    if last:
        shapes, out_specs = [(ROWS, VOC), (ROWS, VOC), (1, 2 * ROWS)], [near] * 3
    elif amateur:
        shapes, out_specs = [(ROWS, BOTH), (1, ROWS)], [far, near]
    else:
        shapes, out_specs = [(ROWS, BOTH), (ROWS, HD)], [far, far]
    dma = pltpu.SemaphoreType.DMA
    return pl.pallas_call(
        lambda *refs: head_kernel(pieces, first, last, amateur, *refs),
        in_specs=[pl.BlockSpec(memory_space=pltpu.SMEM), near]
        + [far] * (len(arrays) + 2 + (0 if first else 2))
        + ([far, near] if last else []),
        out_specs=out_specs,
        out_shape=[jax.ShapeDtypeStruct(shape, F32) for shape in shapes],
        scratch_shapes=[
            pltpu.VMEM((runs, NY, REQ, PAIR), BF16),
            pltpu.VMEM((runs, PAIR, BOTH), BF16),
            pltpu.VMEM((ROWS, BOTH), F32),
            pltpu.VMEM((ROWS, HD), F32),
            dma((runs,)),
            dma((runs,)),
            dma,
            dma,
        ]
        + ([pltpu.VMEM((ROWS, BOTH), F32), dma] if last else []),
        compiler_params=params(56),
        cost_estimate=pl.CostEstimate(
            flops=ROWS * depth,
            bytes_accessed=depth * 64,
            transcendentals=0,
        ),
    )(place, inverse, *arrays, w_own, w_sib, *(sums or ()), *(other or ()))


def contrast_kernel(core_ref, uo_ref, us_ref, no_ref, ns_ref, o_ref):
    core = core_ref[0]
    for u_ref, n_ref, parity in ((uo_ref, no_ref, core), (us_ref, ns_ref, 1 - core)):
        column = jnp.transpose(jnp.broadcast_to(n_ref[...], (HD, 512)))
        for y in range(NY):
            a, b = y * REQ, ROWS + y * REQ
            shift = (1.0 + BETA) * column[a : a + REQ] - BETA * column[b : b + REQ]
            rows = pl.ds(pl.multiple_of((2 * y + parity) * REQ, REQ), REQ)
            for j in range(VOC // HD):
                lanes = slice(j * HD, (j + 1) * HD)
                o_ref[rows, lanes] = u_ref[y * REQ : (y + 1) * REQ, lanes] - shift


def contrast(core, u_own, u_sib, norm_own, norm_sib):
    near = pl.BlockSpec(memory_space=pltpu.VMEM)
    return pl.pallas_call(
        contrast_kernel,
        in_specs=[pl.BlockSpec(memory_space=pltpu.SMEM)] + [near] * 4,
        out_specs=near,
        out_shape=jax.ShapeDtypeStruct((512, VOC), F32),
        compiler_params=params(16),
        cost_estimate=pl.CostEstimate(flops=10**6, bytes_accessed=4 * MIB, transcendentals=65536),
    )(core, u_own, u_sib, norm_own, norm_sib)


TENSOR = ("x", "z")
SWAP = [(0, 1), (1, 0)]


def combine(lse):
    peak = lse[0]
    for part in lse[1:]:
        peak = jnp.maximum(peak, part)
    total = jnp.exp(lse[0] - peak)
    for part in lse[1:]:
        total = total + jnp.exp(part - peak)
    return peak + jnp.log(total)


def from_offset(array, axis, offset):
    return lax.ppermute(array, axis, [((i + offset) % 4, i) for i in range(4)])


def from_core_offset(array, axes, offset):
    pairs = []
    for c in range(2):
        for x in range(4):
            for z in range(4):
                far_x = (x + offset) % 4 if axes[c] == "x" else x
                far_z = (z + offset) % 4 if axes[c] == "z" else z
                pairs.append((c * 16 + far_x * 4 + far_z, c * 16 + x * 4 + z))
    return lax.ppermute(array, ("c", "x", "z"), pairs)


FIRST = ("x", "z")
SECOND = ("z", "x")


def opposite(after, before, axes):
    half = after.shape[0] // 2
    return from_core_offset(after[:half], axes, 1), from_core_offset(before[half:], axes, 3)


def per_device(
    queries,
    cached_key_rows,
    cached_value_rows,
    current_token_key,
    current_token_value,
    lengths,
    residual,
    output_projection_weight,
    request_adapter_index,
    lowrank_down_factors,
    lowrank_up_factors,
    final_norm_scale,
    vocabulary_head_matrix,
):
    core = lax.axis_index("c").astype(jnp.int32).reshape(1)
    place = jnp.stack([lax.axis_index(axis) for axis in ("y", "x", "z", "c")]).astype(jnp.int32)
    head_sib = lax.ppermute(vocabulary_head_matrix, "c", SWAP)
    down = lax.all_gather(lowrank_down_factors, ("y", "c"), axis=0, tiled=True)
    owner = request_adapter_index // HELD
    slots = ((owner // 2 - place[0]) % NY) * HELD + request_adapter_index % HELD
    slots = slots + jnp.where(owner % 2 == place[3], 0, NY * HELD)
    up_after = from_offset(lowrank_up_factors, "y", 1)
    up_before = from_offset(lowrank_up_factors, "y", 3)
    gain = lax.dynamic_slice(final_norm_scale, (lax.axis_index(TENSOR) * COLS,), (COLS,))
    gain = gain.reshape(1, COLS)
    inverse = 1.0 / final_norm_scale.astype(F32)
    inverse = (inverse * inverse).reshape(1, WIDTH)

    sent = attention(
        queries,
        cached_key_rows,
        cached_value_rows,
        current_token_key,
        current_token_value,
        lengths,
        residual,
    )
    got = lax.all_to_all(sent, TENSOR, split_axis=0, concat_axis=0, tiled=True)
    expert, amateur = projection(got, output_projection_weight)
    amateur = lax.all_to_all(amateur, TENSOR, split_axis=0, concat_axis=0, tiled=True)
    sums = lax.all_to_all(expert, TENSOR, split_axis=0, concat_axis=0, tiled=True)
    amateur = amateur_rows(amateur, got, gain)
    up_after, up_before, amateur = lax.optimization_barrier((up_after, up_before, amateur))
    gathered = lax.all_gather(amateur, ("y", "x", "z"), axis=0, tiled=False)
    gathered = gathered.reshape(NY, TEN, REQ, COLS)
    half = HELD // 2
    up_far = (from_offset(up_after[:half], "y", 1), from_offset(up_before[half:], "y", 3))
    up_own = jnp.concatenate([lowrank_up_factors, up_after, *up_far, up_before], axis=0)
    up_own, sums = lax.optimization_barrier((up_own, sums))
    up_sib = lax.ppermute(up_own, "c", SWAP)
    rank = rank_sums(request_adapter_index, got, down)
    rank, sums = lax.optimization_barrier((rank, sums))
    rank = sum([from_offset(rank, "x", d) for d in range(1, 4)], rank)
    rank = [rank] + [from_offset(rank, "z", d) for d in range(1, 4)]
    expert = expert_rows(slots, sums, got, rank, gain, up_own, up_sib)

    plane = jnp.stack([expert] + [from_offset(expert, "y", d) for d in range(1, 4)])
    after = from_core_offset(plane, FIRST, 1)
    before = from_core_offset(plane, FIRST, 3)
    mine = jnp.stack([plane, after, from_core_offset(plane, FIRST, 2), before])
    after = from_core_offset(mine, SECOND, 1)
    before = from_core_offset(mine, SECOND, 3)
    weights = (inverse, vocabulary_head_matrix, head_sib)
    pieces = [(0, n, (n, 0)) for n in range(4)]
    partial = head_part(place, [mine], pieces, *weights)
    pieces = [(0, n, None) for n in range(TEN)]
    other = head_part(place, [gathered], pieces, *weights, amateur=True)
    after, before, *rest = lax.optimization_barrier((after, before, *partial, *other))
    partial, other = rest[:2], rest[2:]
    far = opposite(after, before, SECOND)
    pieces = [(n // 4, n % 4, (n % 4, 1 + 2 * (n // 4))) for n in range(8)]
    partial = head_part(place, [after, before], pieces, *weights, sums=partial)
    pieces = [(n // 2, n % 2, (n, 2)) for n in range(4)]
    u_own, u_send, lse = head_part(place, far, pieces, *weights, sums=partial, other=other)
    for axis in ("y", "x", "z"):
        lse = combine([lse] + [from_offset(lse, axis, d) for d in range(1, 4)])
        if axis == "y":
            u_send, lse = lax.optimization_barrier((u_send, lse))
            u_sib = lax.ppermute(u_send, "c", SWAP)
    return contrast(core, u_own, u_sib, lse, lax.ppermute(lse, "c", SWAP))


def solution(mesh):
    fine = Mesh(np.asarray(mesh.devices).reshape(NY, 2, 4, 4), ("y", "c", "x", "z"))
    every = ("y", "c", "x", "z")
    group = ("y", "c")
    in_specs = (
        P(every, None, None),
        P(every, None, None, None),
        P(every, None, None, None),
        P(every, None, None),
        P(every, None, None),
        P(every),
        P(every, None, None),
        P(TENSOR, None),
        P(group),
        P(group, None, TENSOR),
        P(group, None, TENSOR),
        P(),
        P(None, every),
    )
    return jax.shard_map(
        per_device, mesh=fine, in_specs=in_specs, out_specs=P(None, every), check_vma=False
    )
```

```python
import math

import jax
import jax.numpy as jnp
import numpy as np
from jax import lax
from jax.experimental import pallas as pl
from jax.experimental.pallas import tpu as pltpu
from jax.sharding import Mesh
from jax.sharding import PartitionSpec as P

WIDTH = 8192
HD = 128
CTX = 64
RANK = 16
HELD = 48
REQ = 64
TEN = 16
COLS = WIDTH // TEN
VOC = 768
NY = 4
BETA = 0.5
LOWRANK_SCALE = 2.0
EPS = 1e-05
MIB = 1 << 20
LAST = (((1,), (1,)), ((), ()))
F32 = jnp.float32
BF16 = jnp.bfloat16


def params(mib):
    return pltpu.CompilerParams(vmem_limit_bytes=mib * MIB)


GROUPS = 4


def attention_kernel(len_ref, q_ref, k_ref, v_ref, ck_ref, cv_ref, res_ref, o_ref, q_s, r_s, ck_s, cv_s):
    scale = 1.0 / math.sqrt(HD)
    for r in range(4):
        q_s[2 * r : 2 * r + 2, :] = q_ref[r].astype(F32)
        r_s[2 * r : 2 * r + 2, :] = res_ref[r].astype(F32)
        ck_s[2 * r : 2 * r + 2, :] = ck_ref[r].astype(F32)
        cv_s[2 * r : 2 * r + 2, :] = cv_ref[r].astype(F32)
    row = lax.broadcasted_iota(jnp.int32, (64, 8 * CTX), 0)
    col = lax.broadcasted_iota(jnp.int32, (64, 8 * CTX), 1)
    owner = col // CTX
    limit = jnp.zeros((64, 8 * CTX), jnp.int32)
    for r in range(4):
        limit = jnp.where(owner // 2 == r, len_ref[r], limit)
    valid = (row % 8 == owner) & (col % CTX < limit)
    for g in range(GROUPS):
        lanes = slice(g * HD, (g + 1) * HD)
        base = g * 8 * HD
        q = jnp.concatenate([q_s[:, base + h * HD : base + (h + 1) * HD] for h in range(8)], axis=0)
        keys = k_ref[:, :, :, lanes].reshape(8 * CTX, HD)
        values = v_ref[:, :, :, lanes].reshape(8 * CTX, HD)
        scores = lax.dot_general(q.astype(BF16), keys, LAST, preferred_element_type=F32) * scale
        fresh_key = jnp.concatenate([ck_s[:, lanes]] * 8, axis=0)
        fresh_value = jnp.concatenate([cv_s[:, lanes]] * 8, axis=0)
        own = jnp.sum(q * fresh_key, axis=1, keepdims=True) * scale
        highest = jnp.max(jnp.where(valid, scores, -1e30), axis=1, keepdims=True)
        highest = jnp.maximum(highest, own)
        powers = jnp.where(valid, jnp.exp(scores - highest), 0.0)
        fresh = jnp.exp(own - highest)
        summed = jnp.sum(powers, axis=1, keepdims=True) + fresh
        weights = (powers / summed).astype(BF16)
        fresh_weight = (fresh / summed).astype(BF16).astype(F32)
        mixed = jnp.dot(weights, values, preferred_element_type=F32) + fresh_weight * fresh_value
        for h in range(8):
            both = jnp.concatenate(
                [mixed[h * 8 : (h + 1) * 8, :], r_s[:, base + h * HD : base + (h + 1) * HD]], axis=0
            )
            o_ref[2 * g + h // 4, :, (h % 4) * HD : (h % 4 + 1) * HD] = both.astype(BF16)


def attention(queries, keys, values, fresh_key, fresh_value, lengths, residual):
    wide = pl.BlockSpec((4, 2, GROUPS * 1024), lambda g: (0, 0, g))
    cache = pl.BlockSpec((4, 2, CTX, GROUPS * HD), lambda g: (0, 0, 0, g))
    narrow = pl.BlockSpec((4, 2, GROUPS * HD), lambda g: (0, 0, g))
    return pl.pallas_call(
        attention_kernel,
        grid=(8 // GROUPS,),
        in_specs=[
            pl.BlockSpec(memory_space=pltpu.SMEM),
            wide,
            cache,
            cache,
            narrow,
            narrow,
            wide,
        ],
        out_specs=pl.BlockSpec((2 * GROUPS, 16, COLS), lambda g: (g, 0, 0)),
        out_shape=jax.ShapeDtypeStruct((TEN, 16, COLS), BF16),
        scratch_shapes=[
            pltpu.VMEM((8, GROUPS * 1024), F32),
            pltpu.VMEM((8, GROUPS * 1024), F32),
            pltpu.VMEM((8, GROUPS * HD), F32),
            pltpu.VMEM((8, GROUPS * HD), F32),
        ],
        compiler_params=params(56),
        cost_estimate=pl.CostEstimate(flops=3 * 10**8, bytes_accessed=3 * MIB, transcendentals=262144),
    )(lengths, queries, keys, values, fresh_key, fresh_value, residual)


def start_rows(slot_ref, tables, rows_s, sem):
    held = tables[0].shape[0]

    def one(r, carry):
        slot = slot_ref[r]
        for n, table_ref in enumerate(tables):

            @pl.when((slot >= n * held) & (slot < (n + 1) * held))
            def _():
                pltpu.make_async_copy(table_ref.at[slot - n * held], rows_s.at[r], sem).start()

        return carry

    lax.fori_loop(0, REQ, one, 0, unroll=4)


def wait_rows(table_ref, rows_s, sem):
    pltpu.make_async_copy(table_ref.at[pl.ds(0, REQ)], rows_s, sem).wait()


def own_lanes(rows, lanes, pitch, first=0):
    row = lax.broadcasted_iota(jnp.int32, (rows, lanes), 0)
    lane = lax.broadcasted_iota(jnp.int32, (rows, lanes), 1)
    return row == pitch * (lane // RANK + first)


def attended_rows(got_ref):
    return got_ref[...].astype(F32)[:, 0:8, :].reshape(128, COLS)


def split_kinds(rows, kinds_s):
    kinds = [[], []]
    for j in range(COLS // HD):
        kinds_s[j] = rows[:, j * HD : (j + 1) * HD]
        for kind in range(2):
            kinds[kind].append(kinds_s[j, pl.ds(kind, REQ, stride=2), :])
    return [jnp.concatenate(parts, axis=1) for parts in kinds]


WIDE = 4
SENT = REQ + 16


def projection_kernel(got_ref, w_ref, expert_ref, amateur_ref, att_s, kinds_s):
    @pl.when(pl.program_id(0) == 0)
    def _():
        att_s[...] = jnp.concatenate(split_kinds(attended_rows(got_ref), kinds_s), axis=0).astype(BF16)

    for t in range(WIDE):
        part = jnp.dot(
            att_s[...], w_ref[:, t * COLS : (t + 1) * COLS], preferred_element_type=F32
        )
        expert_ref[t, 0:REQ, :] = part[:REQ].astype(BF16)
        amateur_ref[t] = part[REQ:].astype(BF16)


def projection(got, weight):
    return pl.pallas_call(
        projection_kernel,
        grid=(TEN // WIDE,),
        in_specs=[
            pl.BlockSpec((TEN, 16, COLS), lambda j: (0, 0, 0)),
            pl.BlockSpec((COLS, WIDE * COLS), lambda j: (0, j)),
        ],
        out_specs=[pl.BlockSpec((WIDE, rows, COLS), lambda j: (j, 0, 0)) for rows in (SENT, REQ)],
        out_shape=[jax.ShapeDtypeStruct((TEN, rows, COLS), BF16) for rows in (SENT, REQ)],
        scratch_shapes=[
            pltpu.VMEM((128, COLS), BF16),
            pltpu.VMEM((COLS // HD, 128, HD), F32),
        ],
        compiler_params=params(56),
        cost_estimate=pl.CostEstimate(flops=11 * 10**8, bytes_accessed=11 * MIB, transcendentals=0),
    )(got, weight)


def rank_kernel(idx_ref, got_ref, table_ref, partial_ref, o_ref, rows_s, block_s, sem, out_sem):
    start_rows(idx_ref, [table_ref], rows_s, sem)
    attended = attended_rows(got_ref).astype(BF16)
    wait_rows(table_ref, rows_s, sem)
    rows = rows_s[...].reshape(REQ * RANK, COLS)
    product = lax.dot_general(attended, rows, LAST, preferred_element_type=F32)
    mask = own_lanes(128, REQ * RANK, 2)
    rank = jnp.sum(jnp.where(mask, product, 0.0), axis=0, keepdims=True)
    place = lax.broadcasted_iota(jnp.int32, (16, COLS), 0)
    block = jnp.zeros((16, COLS), F32)
    for n in range(2):
        half = rank[:, n * COLS : (n + 1) * COLS]
        high = half.astype(BF16).astype(F32)
        block = jnp.where(place == n, high, block)
        block = jnp.where(place == n + 2, half - high, block)
    block_s[...] = block.astype(BF16)
    copies = [
        pltpu.make_async_copy(block_s, o_ref.at[t, pl.ds(REQ, 16), :], out_sem.at[t])
        for t in range(TEN)
    ]
    for copy in copies:
        copy.start()
    for copy in copies:
        copy.wait()


def with_rank_sums(index, got, table, partial):
    far = pl.BlockSpec(memory_space=pl.ANY)
    return pl.pallas_call(
        rank_kernel,
        in_specs=[
            pl.BlockSpec(memory_space=pltpu.SMEM),
            pl.BlockSpec(memory_space=pltpu.VMEM),
            far,
            far,
        ],
        out_specs=far,
        out_shape=jax.ShapeDtypeStruct(partial.shape, BF16),
        input_output_aliases={3: 0},
        scratch_shapes=[
            pltpu.VMEM((REQ, RANK, COLS), BF16),
            pltpu.VMEM((16, COLS), BF16),
            pltpu.SemaphoreType.DMA,
            pltpu.SemaphoreType.DMA((TEN,)),
        ],
        compiler_params=params(56),
        cost_estimate=pl.CostEstimate(flops=14 * 10**7, bytes_accessed=2 * MIB, transcendentals=0),
    )(index, got, table, partial)


def add_all(sums_ref, first, last):
    total = sums_ref[0, first:last, :].astype(F32)
    for t in range(1, TEN):
        total = total + sums_ref[t, first:last, :].astype(F32)
    return total


def residual_rows(got_ref):
    return got_ref[...].astype(F32)[:, 8:16, :].reshape(128, COLS)


def amateur_kernel(sums_ref, got_ref, gain_ref, o_ref, kinds_s):
    base = split_kinds(residual_rows(got_ref), kinds_s)[1]
    hidden = (base + add_all(sums_ref, 0, REQ)).astype(BF16).astype(F32)
    o_ref[...] = (hidden * gain_ref[...].astype(F32)).astype(BF16)


def amateur_rows(sums, got, gain):
    near = pl.BlockSpec(memory_space=pltpu.VMEM)
    return pl.pallas_call(
        amateur_kernel,
        in_specs=[near] * 3,
        out_specs=near,
        out_shape=jax.ShapeDtypeStruct((REQ, COLS), BF16),
        scratch_shapes=[pltpu.VMEM((COLS // HD, 128, HD), F32)],
        compiler_params=params(16),
        cost_estimate=pl.CostEstimate(flops=10**6, bytes_accessed=2 * MIB, transcendentals=0),
    )(sums, got, gain)


def expert_kernel(
    slot_ref, sums_ref, got_ref, gain_ref, own_ref, sib_ref, o_ref, rows_s, kinds_s, sem
):
    start_rows(slot_ref, [own_ref, sib_ref], rows_s, sem)
    base = split_kinds(residual_rows(got_ref), kinds_s)[0] + add_all(sums_ref, 0, REQ)
    rank = add_all(sums_ref, REQ, SENT)
    wait_rows(own_ref, rows_s, sem)
    rows = rows_s[...].reshape(REQ * RANK, COLS)
    delta = jnp.zeros((REQ, COLS), F32)
    for n in range(2):
        vector = rank[n : n + 1, :] + rank[n + 2 : n + 3, :]
        spread = jnp.where(own_lanes(REQ, COLS, 1, n * (COLS // RANK)), vector, 0.0)
        high = spread.astype(BF16)
        low = (spread - high.astype(F32)).astype(BF16)
        part = rows[n * COLS : (n + 1) * COLS, :]
        delta = delta + jnp.dot(high, part, preferred_element_type=F32)
        delta = delta + jnp.dot(low, part, preferred_element_type=F32)
    hidden = (base + LOWRANK_SCALE * delta).astype(BF16).astype(F32)
    o_ref[...] = (hidden * gain_ref[...].astype(F32)).astype(BF16)


def expert_rows(slots, sums, got, gain, own, sib):
    near = pl.BlockSpec(memory_space=pltpu.VMEM)
    return pl.pallas_call(
        expert_kernel,
        in_specs=[pl.BlockSpec(memory_space=pltpu.SMEM)]
        + [near] * 3
        + [pl.BlockSpec(memory_space=pl.ANY)] * 2,
        out_specs=near,
        out_shape=jax.ShapeDtypeStruct((REQ, COLS), BF16),
        scratch_shapes=[
            pltpu.VMEM((REQ, RANK, COLS), BF16),
            pltpu.VMEM((COLS // HD, 128, HD), F32),
            pltpu.SemaphoreType.DMA,
        ],
        compiler_params=params(56),
        cost_estimate=pl.CostEstimate(flops=3 * 10**8, bytes_accessed=2 * MIB, transcendentals=0),
    )(slots, sums, got, gain, own, sib)


def tensor_index(at, first, second):
    along_x = jnp.where(at[3] == 0, first, second)
    along_z = jnp.where(at[3] == 0, second, first)
    return lax.rem(at[1] + along_x, 4) * 4 + lax.rem(at[2] + along_z, 4)


ROWS = NY * REQ
PAIR = 2 * COLS
BOTH = 2 * VOC


def head_kernel(pieces, first, last, amateur, at_ref, inv_ref, *refs):
    count = 1 + max(piece[0] for piece in pieces)
    x_refs, wo_ref, ws_ref, refs = refs[:count], refs[count], refs[count + 1], refs[count + 2 :]
    if not first:
        sums_ref, square_ref, refs = refs[0], refs[1], refs[2:]
    if last:
        other_ref, other_lse_ref, uo_ref, us_ref, lse_ref = refs[:5]
        x_s, w_s, acc_s, sq_s, x_sem, w_sem, in_sem, q_sem, other_s, o_sem = refs[5:]
    else:
        out_ref, squares_ref, x_s, w_s, acc_s, sq_s, x_sem, w_sem, in_sem, q_sem = refs

    starts = []
    for n, (which, block, offsets) in enumerate(pieces):
        index = block if offsets is None else tensor_index(at_ref, *offsets)
        start = pl.multiple_of(index * COLS, COLS)
        starts.append(start)
        run, part = n // 2, pl.ds(n % 2 * COLS, COLS)
        for y in range(NY):
            if offsets is None:
                source = x_refs[which].at[y, block]
                place = y
            else:
                source = x_refs[which].at[block, y]
                place = lax.rem(at_ref[0] + y, NY)
            pltpu.make_async_copy(source, x_s.at[run, place, :, part], x_sem.at[run]).start()
        for side, w_ref in enumerate((wo_ref, ws_ref)):
            pltpu.make_async_copy(
                w_ref.at[pl.ds(start, COLS), :],
                w_s.at[run, part, pl.ds(side * VOC, VOC)],
                w_sem.at[run],
            ).start()
    if not first:
        pltpu.make_async_copy(sums_ref, acc_s, in_sem).start()
        pltpu.make_async_copy(square_ref, sq_s, q_sem).start()
        pltpu.make_async_copy(square_ref, sq_s, q_sem).wait()
        pltpu.make_async_copy(sums_ref, acc_s, in_sem).wait()
    else:
        acc_s[...] = jnp.zeros((ROWS, BOTH), F32)
        sq_s[...] = jnp.zeros((ROWS, HD), F32)
    if last:
        pltpu.make_async_copy(other_ref, other_s, o_sem).start()

    def one(run, carry):
        pltpu.make_async_copy(x_s.at[run], x_s.at[run], x_sem.at[run]).wait()
        pltpu.make_async_copy(w_s.at[run], w_s.at[run], w_sem.at[run]).wait()
        x = x_s[run].reshape(ROWS, PAIR)
        acc_s[...] += jnp.dot(x, w_s[run], preferred_element_type=F32)
        return carry

    lax.fori_loop(0, len(pieces) // 2, one, 0)

    square = sq_s[...]
    for n, start in enumerate(starts):
        for j in range(COLS // HD):
            lanes = slice(n % 2 * COLS + j * HD, n % 2 * COLS + (j + 1) * HD)
            piece = x_s[n // 2, :, :, lanes].reshape(ROWS, HD).astype(F32)
            inverse = inv_ref[:, pl.ds(pl.multiple_of(start + j * HD, HD), HD)]
            square = square + piece * piece * inverse
    if not (last or amateur):
        sq_s[...] = square
        pltpu.make_async_copy(sq_s, squares_ref, q_sem).start()
        pltpu.make_async_copy(acc_s, out_ref, in_sem).start()
        pltpu.make_async_copy(sq_s, squares_ref, q_sem).wait()
        pltpu.make_async_copy(acc_s, out_ref, in_sem).wait()
        return

    factor = lax.rsqrt(jnp.sum(square, axis=1, keepdims=True) * (1.0 / WIDTH) + EPS)
    logits = acc_s[...] * factor
    peak = jnp.max(logits, axis=1, keepdims=True)
    lse = peak + jnp.log(jnp.sum(jnp.exp(logits - peak), axis=1, keepdims=True))
    sq_s[...] = jnp.broadcast_to(lse, (ROWS, HD))
    lse = jnp.transpose(sq_s[...])[0:1, :]
    if amateur:
        acc_s[...] = logits
        squares_ref[...] = lse
        pltpu.make_async_copy(acc_s, out_ref, in_sem).start()
        pltpu.make_async_copy(acc_s, out_ref, in_sem).wait()
        return
    lse_ref[:, 0:ROWS] = lse
    lse_ref[:, ROWS:] = other_lse_ref[...]
    pltpu.make_async_copy(other_ref, other_s, o_sem).wait()
    mixed = (1.0 + BETA) * logits - BETA * other_s[...]
    uo_ref[...] = mixed[:, :VOC]
    us_ref[...] = mixed[:, VOC:]


def head_part(place, arrays, pieces, inverse, w_own, w_sib, sums=None, other=None, amateur=False):
    first, last = sums is None, other is not None
    depth = len(pieces) * COLS
    runs = len(pieces) // 2
    near = pl.BlockSpec(memory_space=pltpu.VMEM)
    far = pl.BlockSpec(memory_space=pl.ANY)
    if last:
        shapes, out_specs = [(ROWS, VOC), (ROWS, VOC), (1, 2 * ROWS)], [near] * 3
    elif amateur:
        shapes, out_specs = [(ROWS, BOTH), (1, ROWS)], [far, near]
    else:
        shapes, out_specs = [(ROWS, BOTH), (ROWS, HD)], [far, far]
    dma = pltpu.SemaphoreType.DMA
    return pl.pallas_call(
        lambda *refs: head_kernel(pieces, first, last, amateur, *refs),
        in_specs=[pl.BlockSpec(memory_space=pltpu.SMEM), near]
        + [far] * (len(arrays) + 2 + (0 if first else 2))
        + ([far, near] if last else []),
        out_specs=out_specs,
        out_shape=[jax.ShapeDtypeStruct(shape, F32) for shape in shapes],
        scratch_shapes=[
            pltpu.VMEM((runs, NY, REQ, PAIR), BF16),
            pltpu.VMEM((runs, PAIR, BOTH), BF16),
            pltpu.VMEM((ROWS, BOTH), F32),
            pltpu.VMEM((ROWS, HD), F32),
            dma((runs,)),
            dma((runs,)),
            dma,
            dma,
        ]
        + ([pltpu.VMEM((ROWS, BOTH), F32), dma] if last else []),
        compiler_params=params(56),
        cost_estimate=pl.CostEstimate(
            flops=ROWS * depth,
            bytes_accessed=depth * 64,
            transcendentals=0,
        ),
    )(place, inverse, *arrays, w_own, w_sib, *(sums or ()), *(other or ()))


def contrast_kernel(core_ref, uo_ref, us_ref, no_ref, ns_ref, o_ref):
    core = core_ref[0]
    for u_ref, n_ref, parity in ((uo_ref, no_ref, core), (us_ref, ns_ref, 1 - core)):
        column = jnp.transpose(jnp.broadcast_to(n_ref[...], (HD, 512)))
        for y in range(NY):
            a, b = y * REQ, ROWS + y * REQ
            shift = (1.0 + BETA) * column[a : a + REQ] - BETA * column[b : b + REQ]
            rows = pl.ds(pl.multiple_of((2 * y + parity) * REQ, REQ), REQ)
            for j in range(VOC // HD):
                lanes = slice(j * HD, (j + 1) * HD)
                o_ref[rows, lanes] = u_ref[y * REQ : (y + 1) * REQ, lanes] - shift


def contrast(core, u_own, u_sib, norm_own, norm_sib):
    near = pl.BlockSpec(memory_space=pltpu.VMEM)
    return pl.pallas_call(
        contrast_kernel,
        in_specs=[pl.BlockSpec(memory_space=pltpu.SMEM)] + [near] * 4,
        out_specs=near,
        out_shape=jax.ShapeDtypeStruct((512, VOC), F32),
        compiler_params=params(16),
        cost_estimate=pl.CostEstimate(flops=10**6, bytes_accessed=4 * MIB, transcendentals=65536),
    )(core, u_own, u_sib, norm_own, norm_sib)


TENSOR = ("x", "z")
SWAP = [(0, 1), (1, 0)]


def combine(lse):
    peak = lse[0]
    for part in lse[1:]:
        peak = jnp.maximum(peak, part)
    total = jnp.exp(lse[0] - peak)
    for part in lse[1:]:
        total = total + jnp.exp(part - peak)
    return peak + jnp.log(total)


def from_offset(array, axis, offset):
    return lax.ppermute(array, axis, [((i + offset) % 4, i) for i in range(4)])


def from_core_offset(array, axes, offset):
    pairs = []
    for c in range(2):
        for x in range(4):
            for z in range(4):
                far_x = (x + offset) % 4 if axes[c] == "x" else x
                far_z = (z + offset) % 4 if axes[c] == "z" else z
                pairs.append((c * 16 + far_x * 4 + far_z, c * 16 + x * 4 + z))
    return lax.ppermute(array, ("c", "x", "z"), pairs)


FIRST = ("x", "z")
SECOND = ("z", "x")


def opposite(after, before, axes):
    half = after.shape[0] // 2
    return from_core_offset(after[:half], axes, 1), from_core_offset(before[half:], axes, 3)


def per_device(
    queries,
    cached_key_rows,
    cached_value_rows,
    current_token_key,
    current_token_value,
    lengths,
    residual,
    output_projection_weight,
    request_adapter_index,
    lowrank_down_factors,
    lowrank_up_factors,
    final_norm_scale,
    vocabulary_head_matrix,
):
    core = lax.axis_index("c").astype(jnp.int32).reshape(1)
    place = jnp.stack([lax.axis_index(axis) for axis in ("y", "x", "z", "c")]).astype(jnp.int32)
    head_sib = lax.ppermute(vocabulary_head_matrix, "c", SWAP)
    down = lax.all_gather(lowrank_down_factors, ("y", "c"), axis=0, tiled=True)
    owner = request_adapter_index // HELD
    slots = ((owner // 2 - place[0]) % NY) * HELD + request_adapter_index % HELD
    slots = slots + jnp.where(owner % 2 == place[3], 0, NY * HELD)
    up_after = from_offset(lowrank_up_factors, "y", 1)
    up_before = from_offset(lowrank_up_factors, "y", 3)
    gain = lax.dynamic_slice(final_norm_scale, (lax.axis_index(TENSOR) * COLS,), (COLS,))
    gain = gain.reshape(1, COLS)
    inverse = 1.0 / final_norm_scale.astype(F32)
    inverse = (inverse * inverse).reshape(1, WIDTH)

    sent = attention(
        queries,
        cached_key_rows,
        cached_value_rows,
        current_token_key,
        current_token_value,
        lengths,
        residual,
    )
    got = lax.all_to_all(sent, TENSOR, split_axis=0, concat_axis=0, tiled=True)
    expert, amateur = projection(got, output_projection_weight)
    amateur = lax.all_to_all(amateur, TENSOR, split_axis=0, concat_axis=0, tiled=True)
    amateur = amateur_rows(amateur, got, gain)
    amateur, got = lax.optimization_barrier((amateur, got))
    gathered = lax.all_gather(amateur, ("y", "x", "z"), axis=0, tiled=False)
    gathered = gathered.reshape(NY, TEN, REQ, COLS)
    expert = with_rank_sums(request_adapter_index, got, down, expert)
    sums = lax.all_to_all(expert, TENSOR, split_axis=0, concat_axis=0, tiled=True)
    up_after, up_before, _ = lax.optimization_barrier((up_after, up_before, expert))
    half = HELD // 2
    up_far = (from_offset(up_after[:half], "y", 1), from_offset(up_before[half:], "y", 3))
    up_own = jnp.concatenate([lowrank_up_factors, up_after, *up_far, up_before], axis=0)
    up_sib = lax.ppermute(up_own, "c", SWAP)
    expert = expert_rows(slots, sums, got, gain, up_own, up_sib)

    plane = jnp.stack([expert] + [from_offset(expert, "y", d) for d in range(1, 4)])
    after = from_core_offset(plane, FIRST, 1)
    before = from_core_offset(plane, FIRST, 3)
    mine = jnp.stack([plane, after, from_core_offset(plane, FIRST, 2), before])
    after = from_core_offset(mine, SECOND, 1)
    before = from_core_offset(mine, SECOND, 3)
    weights = (inverse, vocabulary_head_matrix, head_sib)
    pieces = [(0, n, (n, 0)) for n in range(4)]
    partial = head_part(place, [mine], pieces, *weights)
    pieces = [(0, n, None) for n in range(TEN)]
    other = head_part(place, [gathered], pieces, *weights, amateur=True)
    after, before, *rest = lax.optimization_barrier((after, before, *partial, *other))
    partial, other = rest[:2], rest[2:]
    far = opposite(after, before, SECOND)
    pieces = [(n // 4, n % 4, (n % 4, 1 + 2 * (n // 4))) for n in range(8)]
    partial = head_part(place, [after, before], pieces, *weights, sums=partial)
    pieces = [(n // 2, n % 2, (n, 2)) for n in range(4)]
    u_own, u_send, lse = head_part(place, far, pieces, *weights, sums=partial, other=other)
    for axis in ("y", "x", "z"):
        lse = combine([lse] + [from_offset(lse, axis, d) for d in range(1, 4)])
        if axis == "y":
            u_send, lse = lax.optimization_barrier((u_send, lse))
            u_sib = lax.ppermute(u_send, "c", SWAP)
    return contrast(core, u_own, u_sib, lse, lax.ppermute(lse, "c", SWAP))


def solution(mesh):
    fine = Mesh(np.asarray(mesh.devices).reshape(NY, 2, 4, 4), ("y", "c", "x", "z"))
    every = ("y", "c", "x", "z")
    group = ("y", "c")
    in_specs = (
        P(every, None, None),
        P(every, None, None, None),
        P(every, None, None, None),
        P(every, None, None),
        P(every, None, None),
        P(every),
        P(every, None, None),
        P(TENSOR, None),
        P(group),
        P(group, None, TENSOR),
        P(group, None, TENSOR),
        P(),
        P(None, every),
    )
    return jax.shard_map(
        per_device, mesh=fine, in_specs=in_specs, out_specs=P(None, every), check_vma=False
    )
```

```python
import math

import jax
import jax.numpy as jnp
import numpy as np
from jax import lax
from jax.experimental import pallas as pl
from jax.experimental.pallas import tpu as pltpu
from jax.sharding import Mesh
from jax.sharding import PartitionSpec as P

WIDTH = 8192
HD = 128
CTX = 64
RANK = 16
HELD = 48
REQ = 64
TEN = 16
COLS = WIDTH // TEN
VOC = 768
NY = 4
BETA = 0.5
LOWRANK_SCALE = 2.0
EPS = 1e-05
MIB = 1 << 20
LAST = (((1,), (1,)), ((), ()))
F32 = jnp.float32
BF16 = jnp.bfloat16


def params(mib):
    return pltpu.CompilerParams(vmem_limit_bytes=mib * MIB)


GROUPS = 4


def attention_kernel(len_ref, q_ref, k_ref, v_ref, ck_ref, cv_ref, res_ref, o_ref, q_s, r_s, ck_s, cv_s):
    scale = 1.0 / math.sqrt(HD)
    for r in range(4):
        q_s[2 * r : 2 * r + 2, :] = q_ref[r].astype(F32)
        r_s[2 * r : 2 * r + 2, :] = res_ref[r].astype(F32)
        ck_s[2 * r : 2 * r + 2, :] = ck_ref[r].astype(F32)
        cv_s[2 * r : 2 * r + 2, :] = cv_ref[r].astype(F32)
    row = lax.broadcasted_iota(jnp.int32, (64, 8 * CTX), 0)
    col = lax.broadcasted_iota(jnp.int32, (64, 8 * CTX), 1)
    owner = col // CTX
    limit = jnp.zeros((64, 8 * CTX), jnp.int32)
    for r in range(4):
        limit = jnp.where(owner // 2 == r, len_ref[r], limit)
    valid = (row % 8 == owner) & (col % CTX < limit)
    for g in range(GROUPS):
        lanes = slice(g * HD, (g + 1) * HD)
        base = g * 8 * HD
        q = jnp.concatenate([q_s[:, base + h * HD : base + (h + 1) * HD] for h in range(8)], axis=0)
        keys = k_ref[:, :, :, lanes].reshape(8 * CTX, HD)
        values = v_ref[:, :, :, lanes].reshape(8 * CTX, HD)
        scores = lax.dot_general(q.astype(BF16), keys, LAST, preferred_element_type=F32) * scale
        fresh_key = jnp.concatenate([ck_s[:, lanes]] * 8, axis=0)
        fresh_value = jnp.concatenate([cv_s[:, lanes]] * 8, axis=0)
        own = jnp.sum(q * fresh_key, axis=1, keepdims=True) * scale
        highest = jnp.max(jnp.where(valid, scores, -1e30), axis=1, keepdims=True)
        highest = jnp.maximum(highest, own)
        powers = jnp.where(valid, jnp.exp(scores - highest), 0.0)
        fresh = jnp.exp(own - highest)
        summed = jnp.sum(powers, axis=1, keepdims=True) + fresh
        weights = (powers / summed).astype(BF16)
        fresh_weight = (fresh / summed).astype(BF16).astype(F32)
        mixed = jnp.dot(weights, values, preferred_element_type=F32) + fresh_weight * fresh_value
        for h in range(8):
            both = jnp.concatenate(
                [mixed[h * 8 : (h + 1) * 8, :], r_s[:, base + h * HD : base + (h + 1) * HD]], axis=0
            )
            o_ref[2 * g + h // 4, :, (h % 4) * HD : (h % 4 + 1) * HD] = both.astype(BF16)


def attention(queries, keys, values, fresh_key, fresh_value, lengths, residual):
    wide = pl.BlockSpec((4, 2, GROUPS * 1024), lambda g: (0, 0, g))
    cache = pl.BlockSpec((4, 2, CTX, GROUPS * HD), lambda g: (0, 0, 0, g))
    narrow = pl.BlockSpec((4, 2, GROUPS * HD), lambda g: (0, 0, g))
    return pl.pallas_call(
        attention_kernel,
        grid=(8 // GROUPS,),
        in_specs=[
            pl.BlockSpec(memory_space=pltpu.SMEM),
            wide,
            cache,
            cache,
            narrow,
            narrow,
            wide,
        ],
        out_specs=pl.BlockSpec((2 * GROUPS, 16, COLS), lambda g: (g, 0, 0)),
        out_shape=jax.ShapeDtypeStruct((TEN, 16, COLS), BF16),
        scratch_shapes=[
            pltpu.VMEM((8, GROUPS * 1024), F32),
            pltpu.VMEM((8, GROUPS * 1024), F32),
            pltpu.VMEM((8, GROUPS * HD), F32),
            pltpu.VMEM((8, GROUPS * HD), F32),
        ],
        compiler_params=params(56),
        cost_estimate=pl.CostEstimate(flops=3 * 10**8, bytes_accessed=3 * MIB, transcendentals=262144),
    )(lengths, queries, keys, values, fresh_key, fresh_value, residual)


def start_rows(slot_ref, tables, rows_s, sem):
    held = tables[0].shape[0]

    def one(r, carry):
        slot = slot_ref[r]
        for n, table_ref in enumerate(tables):

            @pl.when((slot >= n * held) & (slot < (n + 1) * held))
            def _():
                pltpu.make_async_copy(table_ref.at[slot - n * held], rows_s.at[r], sem).start()

        return carry

    lax.fori_loop(0, REQ, one, 0, unroll=4)


def wait_rows(table_ref, rows_s, sem):
    pltpu.make_async_copy(table_ref.at[pl.ds(0, REQ)], rows_s, sem).wait()


def own_lanes(rows, lanes, pitch, first=0):
    row = lax.broadcasted_iota(jnp.int32, (rows, lanes), 0)
    lane = lax.broadcasted_iota(jnp.int32, (rows, lanes), 1)
    return row == pitch * (lane // RANK + first)


def attended_rows(got_ref):
    return got_ref[...].astype(F32)[:, 0:8, :].reshape(128, COLS)


def split_kinds(rows, kinds_s):
    kinds = [[], []]
    for j in range(COLS // HD):
        kinds_s[j] = rows[:, j * HD : (j + 1) * HD]
        for kind in range(2):
            kinds[kind].append(kinds_s[j, pl.ds(kind, REQ, stride=2), :])
    return [jnp.concatenate(parts, axis=1) for parts in kinds]


WIDE = 4
SENT = REQ + 16


def projection_kernel(got_ref, w_ref, expert_ref, amateur_ref, att_s, kinds_s):
    @pl.when(pl.program_id(0) == 0)
    def _():
        att_s[...] = jnp.concatenate(split_kinds(attended_rows(got_ref), kinds_s), axis=0).astype(BF16)

    for t in range(WIDE):
        part = jnp.dot(
            att_s[...], w_ref[:, t * COLS : (t + 1) * COLS], preferred_element_type=F32
        )
        expert_ref[t, 0:REQ, :] = part[:REQ].astype(BF16)
        amateur_ref[t] = part[REQ:].astype(BF16)


def projection(got, weight):
    return pl.pallas_call(
        projection_kernel,
        grid=(TEN // WIDE,),
        in_specs=[
            pl.BlockSpec((TEN, 16, COLS), lambda j: (0, 0, 0)),
            pl.BlockSpec((COLS, WIDE * COLS), lambda j: (0, j)),
        ],
        out_specs=[pl.BlockSpec((WIDE, rows, COLS), lambda j: (j, 0, 0)) for rows in (SENT, REQ)],
        out_shape=[jax.ShapeDtypeStruct((TEN, rows, COLS), BF16) for rows in (SENT, REQ)],
        scratch_shapes=[
            pltpu.VMEM((128, COLS), BF16),
            pltpu.VMEM((COLS // HD, 128, HD), F32),
        ],
        compiler_params=params(56),
        cost_estimate=pl.CostEstimate(flops=11 * 10**8, bytes_accessed=11 * MIB, transcendentals=0),
    )(got, weight)


def rank_kernel(idx_ref, got_ref, table_ref, partial_ref, o_ref, rows_s, block_s, sem, out_sem):
    start_rows(idx_ref, [table_ref], rows_s, sem)
    attended = attended_rows(got_ref).astype(BF16)
    wait_rows(table_ref, rows_s, sem)
    rows = rows_s[...].reshape(REQ * RANK, COLS)
    product = lax.dot_general(attended, rows, LAST, preferred_element_type=F32)
    mask = own_lanes(128, REQ * RANK, 2)
    rank = jnp.sum(jnp.where(mask, product, 0.0), axis=0, keepdims=True)
    place = lax.broadcasted_iota(jnp.int32, (16, COLS), 0)
    block = jnp.zeros((16, COLS), F32)
    for n in range(2):
        half = rank[:, n * COLS : (n + 1) * COLS]
        high = half.astype(BF16).astype(F32)
        block = jnp.where(place == n, high, block)
        block = jnp.where(place == n + 2, half - high, block)
    block_s[...] = block.astype(BF16)
    copies = [
        pltpu.make_async_copy(block_s, o_ref.at[t, pl.ds(REQ, 16), :], out_sem.at[t])
        for t in range(TEN)
    ]
    for copy in copies:
        copy.start()
    for copy in copies:
        copy.wait()


def with_rank_sums(index, got, table, partial):
    far = pl.BlockSpec(memory_space=pl.ANY)
    return pl.pallas_call(
        rank_kernel,
        in_specs=[
            pl.BlockSpec(memory_space=pltpu.SMEM),
            pl.BlockSpec(memory_space=pltpu.VMEM),
            far,
            far,
        ],
        out_specs=far,
        out_shape=jax.ShapeDtypeStruct(partial.shape, BF16),
        input_output_aliases={3: 0},
        scratch_shapes=[
            pltpu.VMEM((REQ, RANK, COLS), BF16),
            pltpu.VMEM((16, COLS), BF16),
            pltpu.SemaphoreType.DMA,
            pltpu.SemaphoreType.DMA((TEN,)),
        ],
        compiler_params=params(56),
        cost_estimate=pl.CostEstimate(flops=14 * 10**7, bytes_accessed=2 * MIB, transcendentals=0),
    )(index, got, table, partial)


def add_all(sums_ref, first, last):
    total = sums_ref[0, first:last, :].astype(F32)
    for t in range(1, TEN):
        total = total + sums_ref[t, first:last, :].astype(F32)
    return total


def residual_rows(got_ref):
    return got_ref[...].astype(F32)[:, 8:16, :].reshape(128, COLS)


def amateur_kernel(sums_ref, got_ref, gain_ref, o_ref, kinds_s):
    base = split_kinds(residual_rows(got_ref), kinds_s)[1]
    hidden = (base + add_all(sums_ref, 0, REQ)).astype(BF16).astype(F32)
    o_ref[...] = (hidden * gain_ref[...].astype(F32)).astype(BF16)


def amateur_rows(sums, got, gain):
    near = pl.BlockSpec(memory_space=pltpu.VMEM)
    return pl.pallas_call(
        amateur_kernel,
        in_specs=[near] * 3,
        out_specs=near,
        out_shape=jax.ShapeDtypeStruct((REQ, COLS), BF16),
        scratch_shapes=[pltpu.VMEM((COLS // HD, 128, HD), F32)],
        compiler_params=params(16),
        cost_estimate=pl.CostEstimate(flops=10**6, bytes_accessed=2 * MIB, transcendentals=0),
    )(sums, got, gain)


def expert_kernel(
    slot_ref, sums_ref, got_ref, gain_ref, own_ref, sib_ref, o_ref, rows_s, kinds_s, sem
):
    start_rows(slot_ref, [own_ref, sib_ref], rows_s, sem)
    base = split_kinds(residual_rows(got_ref), kinds_s)[0] + add_all(sums_ref, 0, REQ)
    rank = add_all(sums_ref, REQ, SENT)
    wait_rows(own_ref, rows_s, sem)
    rows = rows_s[...].reshape(REQ * RANK, COLS)
    delta = jnp.zeros((REQ, COLS), F32)
    for n in range(2):
        vector = rank[n : n + 1, :] + rank[n + 2 : n + 3, :]
        spread = jnp.where(own_lanes(REQ, COLS, 1, n * (COLS // RANK)), vector, 0.0)
        high = spread.astype(BF16)
        low = (spread - high.astype(F32)).astype(BF16)
        part = rows[n * COLS : (n + 1) * COLS, :]
        delta = delta + jnp.dot(high, part, preferred_element_type=F32)
        delta = delta + jnp.dot(low, part, preferred_element_type=F32)
    hidden = (base + LOWRANK_SCALE * delta).astype(BF16).astype(F32)
    o_ref[...] = (hidden * gain_ref[...].astype(F32)).astype(BF16)


def expert_rows(slots, sums, got, gain, own, sib):
    near = pl.BlockSpec(memory_space=pltpu.VMEM)
    return pl.pallas_call(
        expert_kernel,
        in_specs=[pl.BlockSpec(memory_space=pltpu.SMEM)]
        + [near] * 3
        + [pl.BlockSpec(memory_space=pl.ANY)] * 2,
        out_specs=near,
        out_shape=jax.ShapeDtypeStruct((REQ, COLS), BF16),
        scratch_shapes=[
            pltpu.VMEM((REQ, RANK, COLS), BF16),
            pltpu.VMEM((COLS // HD, 128, HD), F32),
            pltpu.SemaphoreType.DMA,
        ],
        compiler_params=params(56),
        cost_estimate=pl.CostEstimate(flops=3 * 10**8, bytes_accessed=2 * MIB, transcendentals=0),
    )(slots, sums, got, gain, own, sib)


def tensor_index(at, first, second):
    along_x = jnp.where(at[3] == 0, first, second)
    along_z = jnp.where(at[3] == 0, second, first)
    return lax.rem(at[1] + along_x, 4) * 4 + lax.rem(at[2] + along_z, 4)


ROWS = NY * REQ
PAIR = 2 * COLS
BOTH = 2 * VOC


def head_kernel(pieces, first, last, amateur, at_ref, inv_ref, *refs):
    count = 1 + max(piece[0] for piece in pieces)
    x_refs, wo_ref, ws_ref, refs = refs[:count], refs[count], refs[count + 1], refs[count + 2 :]
    if not first:
        sums_ref, square_ref, refs = refs[0], refs[1], refs[2:]
    if last:
        other_ref, other_lse_ref, uo_ref, us_ref, lse_ref = refs[:5]
        x_s, w_s, acc_s, sq_s, x_sem, w_sem, in_sem, q_sem, other_s, o_sem = refs[5:]
    else:
        out_ref, squares_ref, x_s, w_s, acc_s, sq_s, x_sem, w_sem, in_sem, q_sem = refs

    starts = []
    for n, (which, block, offsets) in enumerate(pieces):
        index = block if offsets is None else tensor_index(at_ref, *offsets)
        start = pl.multiple_of(index * COLS, COLS)
        starts.append(start)
        run, part = n // 2, pl.ds(n % 2 * COLS, COLS)
        for y in range(NY):
            if offsets is None:
                source = x_refs[which].at[y, block]
                place = y
            else:
                source = x_refs[which].at[block, y]
                place = lax.rem(at_ref[0] + y, NY)
            pltpu.make_async_copy(source, x_s.at[run, place, :, part], x_sem.at[run]).start()
        for side, w_ref in enumerate((wo_ref, ws_ref)):
            pltpu.make_async_copy(
                w_ref.at[pl.ds(start, COLS), :],
                w_s.at[run, part, pl.ds(side * VOC, VOC)],
                w_sem.at[run],
            ).start()
    if not first:
        pltpu.make_async_copy(sums_ref, acc_s, in_sem).start()
        pltpu.make_async_copy(square_ref, sq_s, q_sem).start()
        pltpu.make_async_copy(square_ref, sq_s, q_sem).wait()
        pltpu.make_async_copy(sums_ref, acc_s, in_sem).wait()
    else:
        acc_s[...] = jnp.zeros((ROWS, BOTH), F32)
        sq_s[...] = jnp.zeros((ROWS, HD), F32)
    if last:
        pltpu.make_async_copy(other_ref, other_s, o_sem).start()

    def one(run, carry):
        pltpu.make_async_copy(x_s.at[run], x_s.at[run], x_sem.at[run]).wait()
        pltpu.make_async_copy(w_s.at[run], w_s.at[run], w_sem.at[run]).wait()
        x = x_s[run].reshape(ROWS, PAIR)
        acc_s[...] += jnp.dot(x, w_s[run], preferred_element_type=F32)
        return carry

    lax.fori_loop(0, len(pieces) // 2, one, 0)

    square = sq_s[...]
    for n, start in enumerate(starts):
        for j in range(COLS // HD):
            lanes = slice(n % 2 * COLS + j * HD, n % 2 * COLS + (j + 1) * HD)
            piece = x_s[n // 2, :, :, lanes].reshape(ROWS, HD).astype(F32)
            inverse = inv_ref[:, pl.ds(pl.multiple_of(start + j * HD, HD), HD)]
            square = square + piece * piece * inverse
    if not (last or amateur):
        sq_s[...] = square
        pltpu.make_async_copy(sq_s, squares_ref, q_sem).start()
        pltpu.make_async_copy(acc_s, out_ref, in_sem).start()
        pltpu.make_async_copy(sq_s, squares_ref, q_sem).wait()
        pltpu.make_async_copy(acc_s, out_ref, in_sem).wait()
        return

    factor = lax.rsqrt(jnp.sum(square, axis=1, keepdims=True) * (1.0 / WIDTH) + EPS)
    logits = acc_s[...] * factor
    peak = jnp.max(logits, axis=1, keepdims=True)
    lse = peak + jnp.log(jnp.sum(jnp.exp(logits - peak), axis=1, keepdims=True))
    sq_s[...] = jnp.broadcast_to(lse, (ROWS, HD))
    lse = jnp.transpose(sq_s[...])[0:1, :]
    if amateur:
        acc_s[...] = logits
        squares_ref[...] = lse
        pltpu.make_async_copy(acc_s, out_ref, in_sem).start()
        pltpu.make_async_copy(acc_s, out_ref, in_sem).wait()
        return
    lse_ref[:, 0:ROWS] = lse
    lse_ref[:, ROWS:] = other_lse_ref[...]
    pltpu.make_async_copy(other_ref, other_s, o_sem).wait()
    mixed = (1.0 + BETA) * logits - BETA * other_s[...]
    uo_ref[...] = mixed[:, :VOC]
    us_ref[...] = mixed[:, VOC:]


def head_part(place, arrays, pieces, inverse, w_own, w_sib, sums=None, other=None, amateur=False):
    first, last = sums is None, other is not None
    depth = len(pieces) * COLS
    runs = len(pieces) // 2
    near = pl.BlockSpec(memory_space=pltpu.VMEM)
    far = pl.BlockSpec(memory_space=pl.ANY)
    if last:
        shapes, out_specs = [(ROWS, VOC), (ROWS, VOC), (1, 2 * ROWS)], [near] * 3
    elif amateur:
        shapes, out_specs = [(ROWS, BOTH), (1, ROWS)], [far, near]
    else:
        shapes, out_specs = [(ROWS, BOTH), (ROWS, HD)], [far, far]
    dma = pltpu.SemaphoreType.DMA
    return pl.pallas_call(
        lambda *refs: head_kernel(pieces, first, last, amateur, *refs),
        in_specs=[pl.BlockSpec(memory_space=pltpu.SMEM), near]
        + [far] * (len(arrays) + 2 + (0 if first else 2))
        + ([far, near] if last else []),
        out_specs=out_specs,
        out_shape=[jax.ShapeDtypeStruct(shape, F32) for shape in shapes],
        scratch_shapes=[
            pltpu.VMEM((runs, NY, REQ, PAIR), BF16),
            pltpu.VMEM((runs, PAIR, BOTH), BF16),
            pltpu.VMEM((ROWS, BOTH), F32),
            pltpu.VMEM((ROWS, HD), F32),
            dma((runs,)),
            dma((runs,)),
            dma,
            dma,
        ]
        + ([pltpu.VMEM((ROWS, BOTH), F32), dma] if last else []),
        compiler_params=params(56),
        cost_estimate=pl.CostEstimate(
            flops=ROWS * depth,
            bytes_accessed=depth * 64,
            transcendentals=0,
        ),
    )(place, inverse, *arrays, w_own, w_sib, *(sums or ()), *(other or ()))


def contrast_kernel(core_ref, uo_ref, us_ref, no_ref, ns_ref, o_ref):
    core = core_ref[0]
    for u_ref, n_ref, parity in ((uo_ref, no_ref, core), (us_ref, ns_ref, 1 - core)):
        column = jnp.transpose(jnp.broadcast_to(n_ref[...], (HD, 512)))
        for y in range(NY):
            a, b = y * REQ, ROWS + y * REQ
            shift = (1.0 + BETA) * column[a : a + REQ] - BETA * column[b : b + REQ]
            rows = pl.ds(pl.multiple_of((2 * y + parity) * REQ, REQ), REQ)
            for j in range(VOC // HD):
                lanes = slice(j * HD, (j + 1) * HD)
                o_ref[rows, lanes] = u_ref[y * REQ : (y + 1) * REQ, lanes] - shift


def contrast(core, u_own, u_sib, norm_own, norm_sib):
    near = pl.BlockSpec(memory_space=pltpu.VMEM)
    return pl.pallas_call(
        contrast_kernel,
        in_specs=[pl.BlockSpec(memory_space=pltpu.SMEM)] + [near] * 4,
        out_specs=near,
        out_shape=jax.ShapeDtypeStruct((512, VOC), F32),
        compiler_params=params(16),
        cost_estimate=pl.CostEstimate(flops=10**6, bytes_accessed=4 * MIB, transcendentals=65536),
    )(core, u_own, u_sib, norm_own, norm_sib)


TENSOR = ("x", "z")
SWAP = [(0, 1), (1, 0)]


def combine(lse):
    peak = lse[0]
    for part in lse[1:]:
        peak = jnp.maximum(peak, part)
    total = jnp.exp(lse[0] - peak)
    for part in lse[1:]:
        total = total + jnp.exp(part - peak)
    return peak + jnp.log(total)


def from_offset(array, axis, offset):
    return lax.ppermute(array, axis, [((i + offset) % 4, i) for i in range(4)])


def from_core_offset(array, axes, offset):
    pairs = []
    for c in range(2):
        for x in range(4):
            for z in range(4):
                far_x = (x + offset) % 4 if axes[c] == "x" else x
                far_z = (z + offset) % 4 if axes[c] == "z" else z
                pairs.append((c * 16 + far_x * 4 + far_z, c * 16 + x * 4 + z))
    return lax.ppermute(array, ("c", "x", "z"), pairs)


FIRST = ("x", "z")
SECOND = ("z", "x")


def opposite(after, before, axes):
    half = after.shape[0] // 2
    return from_core_offset(after[:half], axes, 1), from_core_offset(before[half:], axes, 3)


def per_device(
    queries,
    cached_key_rows,
    cached_value_rows,
    current_token_key,
    current_token_value,
    lengths,
    residual,
    output_projection_weight,
    request_adapter_index,
    lowrank_down_factors,
    lowrank_up_factors,
    final_norm_scale,
    vocabulary_head_matrix,
):
    core = lax.axis_index("c").astype(jnp.int32).reshape(1)
    place = jnp.stack([lax.axis_index(axis) for axis in ("y", "x", "z", "c")]).astype(jnp.int32)
    head_sib = lax.ppermute(vocabulary_head_matrix, "c", SWAP)
    down = lax.all_gather(lowrank_down_factors, ("y", "c"), axis=0, tiled=True)
    owner = request_adapter_index // HELD
    slots = ((owner // 2 - place[0]) % NY) * HELD + request_adapter_index % HELD
    slots = slots + jnp.where(owner % 2 == place[3], 0, NY * HELD)
    up_after = from_offset(lowrank_up_factors, "y", 1)
    up_before = from_offset(lowrank_up_factors, "y", 3)
    gain = lax.dynamic_slice(final_norm_scale, (lax.axis_index(TENSOR) * COLS,), (COLS,))
    gain = gain.reshape(1, COLS)
    inverse = 1.0 / final_norm_scale.astype(F32)
    inverse = (inverse * inverse).reshape(1, WIDTH)

    sent = attention(
        queries,
        cached_key_rows,
        cached_value_rows,
        current_token_key,
        current_token_value,
        lengths,
        residual,
    )
    got = lax.all_to_all(sent, TENSOR, split_axis=0, concat_axis=0, tiled=True)
    expert, amateur = projection(got, output_projection_weight)
    up_after, up_before, amateur = lax.optimization_barrier((up_after, up_before, amateur))
    amateur = lax.all_to_all(amateur, TENSOR, split_axis=0, concat_axis=0, tiled=True)
    half = HELD // 2
    up_far = (from_offset(up_after[:half], "y", 1), from_offset(up_before[half:], "y", 3))
    up_own = jnp.concatenate([lowrank_up_factors, up_after, *up_far, up_before], axis=0)
    up_own, amateur = lax.optimization_barrier((up_own, amateur))
    up_sib = lax.ppermute(up_own, "c", SWAP)
    amateur = amateur_rows(amateur, got, gain)
    amateur, got = lax.optimization_barrier((amateur, got))
    gathered = lax.all_gather(amateur, ("y", "x", "z"), axis=0, tiled=False)
    gathered = gathered.reshape(NY, TEN, REQ, COLS)
    expert = with_rank_sums(request_adapter_index, got, down, expert)
    sums = lax.all_to_all(expert, TENSOR, split_axis=0, concat_axis=0, tiled=True)
    expert = expert_rows(slots, sums, got, gain, up_own, up_sib)

    plane = jnp.stack([expert] + [from_offset(expert, "y", d) for d in range(1, 4)])
    after = from_core_offset(plane, FIRST, 1)
    before = from_core_offset(plane, FIRST, 3)
    mine = jnp.stack([plane, after, from_core_offset(plane, FIRST, 2), before])
    after = from_core_offset(mine, SECOND, 1)
    before = from_core_offset(mine, SECOND, 3)
    weights = (inverse, vocabulary_head_matrix, head_sib)
    pieces = [(0, n, (n, 0)) for n in range(4)]
    partial = head_part(place, [mine], pieces, *weights)
    pieces = [(0, n, None) for n in range(TEN)]
    other = head_part(place, [gathered], pieces, *weights, amateur=True)
    after, before, *rest = lax.optimization_barrier((after, before, *partial, *other))
    partial, other = rest[:2], rest[2:]
    far = opposite(after, before, SECOND)
    pieces = [(n // 4, n % 4, (n % 4, 1 + 2 * (n // 4))) for n in range(8)]
    partial = head_part(place, [after, before], pieces, *weights, sums=partial)
    pieces = [(n // 2, n % 2, (n, 2)) for n in range(4)]
    u_own, u_send, lse = head_part(place, far, pieces, *weights, sums=partial, other=other)
    for axis in ("y", "x", "z"):
        lse = combine([lse] + [from_offset(lse, axis, d) for d in range(1, 4)])
        if axis == "y":
            u_send, lse = lax.optimization_barrier((u_send, lse))
            u_sib = lax.ppermute(u_send, "c", SWAP)
    return contrast(core, u_own, u_sib, lse, lax.ppermute(lse, "c", SWAP))


def solution(mesh):
    fine = Mesh(np.asarray(mesh.devices).reshape(NY, 2, 4, 4), ("y", "c", "x", "z"))
    every = ("y", "c", "x", "z")
    group = ("y", "c")
    in_specs = (
        P(every, None, None),
        P(every, None, None, None),
        P(every, None, None, None),
        P(every, None, None),
        P(every, None, None),
        P(every),
        P(every, None, None),
        P(TENSOR, None),
        P(group),
        P(group, None, TENSOR),
        P(group, None, TENSOR),
        P(),
        P(None, every),
    )
    return jax.shard_map(
        per_device, mesh=fine, in_specs=in_specs, out_specs=P(None, every), check_vma=False
    )
```

```python
import math

import jax
import jax.numpy as jnp
import numpy as np
from jax import lax
from jax.experimental import pallas as pl
from jax.experimental.pallas import tpu as pltpu
from jax.sharding import Mesh
from jax.sharding import PartitionSpec as P

WIDTH = 8192
HD = 128
CTX = 64
RANK = 16
REQ = 64
TEN = 16
COLS = WIDTH // TEN
VOC = 768
NY = 4
BETA = 0.5
LOWRANK_SCALE = 2.0
EPS = 1e-05
MIB = 1 << 20
LAST = (((1,), (1,)), ((), ()))
F32 = jnp.float32
BF16 = jnp.bfloat16


def params(mib):
    return pltpu.CompilerParams(vmem_limit_bytes=mib * MIB)


GROUPS = 4


def attention_kernel(len_ref, q_ref, k_ref, v_ref, ck_ref, cv_ref, res_ref, o_ref, q_s, r_s, ck_s, cv_s):
    scale = 1.0 / math.sqrt(HD)
    for r in range(4):
        q_s[2 * r : 2 * r + 2, :] = q_ref[r].astype(F32)
        r_s[2 * r : 2 * r + 2, :] = res_ref[r].astype(F32)
        ck_s[2 * r : 2 * r + 2, :] = ck_ref[r].astype(F32)
        cv_s[2 * r : 2 * r + 2, :] = cv_ref[r].astype(F32)
    row = lax.broadcasted_iota(jnp.int32, (64, 8 * CTX), 0)
    col = lax.broadcasted_iota(jnp.int32, (64, 8 * CTX), 1)
    owner = col // CTX
    limit = jnp.zeros((64, 8 * CTX), jnp.int32)
    for r in range(4):
        limit = jnp.where(owner // 2 == r, len_ref[r], limit)
    valid = (row % 8 == owner) & (col % CTX < limit)
    for g in range(GROUPS):
        lanes = slice(g * HD, (g + 1) * HD)
        base = g * 8 * HD
        q = jnp.concatenate([q_s[:, base + h * HD : base + (h + 1) * HD] for h in range(8)], axis=0)
        keys = k_ref[:, :, :, lanes].reshape(8 * CTX, HD)
        values = v_ref[:, :, :, lanes].reshape(8 * CTX, HD)
        scores = lax.dot_general(q.astype(BF16), keys, LAST, preferred_element_type=F32) * scale
        fresh_key = jnp.concatenate([ck_s[:, lanes]] * 8, axis=0)
        fresh_value = jnp.concatenate([cv_s[:, lanes]] * 8, axis=0)
        own = jnp.sum(q * fresh_key, axis=1, keepdims=True) * scale
        highest = jnp.max(jnp.where(valid, scores, -1e30), axis=1, keepdims=True)
        highest = jnp.maximum(highest, own)
        powers = jnp.where(valid, jnp.exp(scores - highest), 0.0)
        fresh = jnp.exp(own - highest)
        summed = jnp.sum(powers, axis=1, keepdims=True) + fresh
        weights = (powers / summed).astype(BF16)
        fresh_weight = (fresh / summed).astype(BF16).astype(F32)
        mixed = jnp.dot(weights, values, preferred_element_type=F32) + fresh_weight * fresh_value
        for h in range(8):
            both = jnp.concatenate(
                [mixed[h * 8 : (h + 1) * 8, :], r_s[:, base + h * HD : base + (h + 1) * HD]], axis=0
            )
            o_ref[2 * g + h // 4, :, (h % 4) * HD : (h % 4 + 1) * HD] = both.astype(BF16)


def attention(queries, keys, values, fresh_key, fresh_value, lengths, residual):
    wide = pl.BlockSpec((4, 2, GROUPS * 1024), lambda g: (0, 0, g))
    cache = pl.BlockSpec((4, 2, CTX, GROUPS * HD), lambda g: (0, 0, 0, g))
    narrow = pl.BlockSpec((4, 2, GROUPS * HD), lambda g: (0, 0, g))
    return pl.pallas_call(
        attention_kernel,
        grid=(8 // GROUPS,),
        in_specs=[
            pl.BlockSpec(memory_space=pltpu.SMEM),
            wide,
            cache,
            cache,
            narrow,
            narrow,
            wide,
        ],
        out_specs=pl.BlockSpec((2 * GROUPS, 16, COLS), lambda g: (g, 0, 0)),
        out_shape=jax.ShapeDtypeStruct((TEN, 16, COLS), BF16),
        scratch_shapes=[
            pltpu.VMEM((8, GROUPS * 1024), F32),
            pltpu.VMEM((8, GROUPS * 1024), F32),
            pltpu.VMEM((8, GROUPS * HD), F32),
            pltpu.VMEM((8, GROUPS * HD), F32),
        ],
        compiler_params=params(56),
        cost_estimate=pl.CostEstimate(flops=3 * 10**8, bytes_accessed=3 * MIB, transcendentals=262144),
    )(lengths, queries, keys, values, fresh_key, fresh_value, residual)


def start_rows(slot_ref, table_ref, rows_s, sem):
    def one(r, carry):
        pltpu.make_async_copy(table_ref.at[slot_ref[r]], rows_s.at[r], sem).start()
        return carry

    lax.fori_loop(0, REQ, one, 0, unroll=8)


def wait_rows(table_ref, rows_s, sem):
    pltpu.make_async_copy(table_ref.at[pl.ds(0, REQ)], rows_s, sem).wait()


def own_lanes(rows, lanes, pitch, first=0):
    row = lax.broadcasted_iota(jnp.int32, (rows, lanes), 0)
    lane = lax.broadcasted_iota(jnp.int32, (rows, lanes), 1)
    return row == pitch * (lane // RANK + first)


def attended_rows(got_ref):
    return got_ref[...].astype(F32)[:, 0:8, :].reshape(128, COLS)


def split_kinds(rows, kinds_s):
    kinds = [[], []]
    for j in range(COLS // HD):
        kinds_s[j] = rows[:, j * HD : (j + 1) * HD]
        for kind in range(2):
            kinds[kind].append(kinds_s[j, pl.ds(kind, REQ, stride=2), :])
    return [jnp.concatenate(parts, axis=1) for parts in kinds]


WIDE = 4
SENT = REQ + 16


def projection_kernel(got_ref, w_ref, expert_ref, amateur_ref, att_s, kinds_s):
    @pl.when(pl.program_id(0) == 0)
    def _():
        att_s[...] = jnp.concatenate(split_kinds(attended_rows(got_ref), kinds_s), axis=0).astype(BF16)

    for t in range(WIDE):
        part = jnp.dot(
            att_s[...], w_ref[:, t * COLS : (t + 1) * COLS], preferred_element_type=F32
        )
        expert_ref[t, 0:REQ, :] = part[:REQ].astype(BF16)
        amateur_ref[t] = part[REQ:].astype(BF16)


def projection(got, weight):
    return pl.pallas_call(
        projection_kernel,
        grid=(TEN // WIDE,),
        in_specs=[
            pl.BlockSpec((TEN, 16, COLS), lambda j: (0, 0, 0)),
            pl.BlockSpec((COLS, WIDE * COLS), lambda j: (0, j)),
        ],
        out_specs=[pl.BlockSpec((WIDE, rows, COLS), lambda j: (j, 0, 0)) for rows in (SENT, REQ)],
        out_shape=[jax.ShapeDtypeStruct((TEN, rows, COLS), BF16) for rows in (SENT, REQ)],
        scratch_shapes=[
            pltpu.VMEM((128, COLS), BF16),
            pltpu.VMEM((COLS // HD, 128, HD), F32),
        ],
        compiler_params=params(56),
        cost_estimate=pl.CostEstimate(flops=11 * 10**8, bytes_accessed=11 * MIB, transcendentals=0),
    )(got, weight)


def rank_kernel(idx_ref, got_ref, table_ref, partial_ref, o_ref, rows_s, block_s, sem, out_sem):
    start_rows(idx_ref, table_ref, rows_s, sem)
    attended = attended_rows(got_ref).astype(BF16)
    wait_rows(table_ref, rows_s, sem)
    rows = rows_s[...].reshape(REQ * RANK, COLS)
    product = lax.dot_general(attended, rows, LAST, preferred_element_type=F32)
    mask = own_lanes(128, REQ * RANK, 2)
    rank = jnp.sum(jnp.where(mask, product, 0.0), axis=0, keepdims=True)
    place = lax.broadcasted_iota(jnp.int32, (16, COLS), 0)
    block = jnp.zeros((16, COLS), F32)
    for n in range(2):
        half = rank[:, n * COLS : (n + 1) * COLS]
        high = half.astype(BF16).astype(F32)
        block = jnp.where(place == n, high, block)
        block = jnp.where(place == n + 2, half - high, block)
    block_s[...] = block.astype(BF16)
    copies = [
        pltpu.make_async_copy(block_s, o_ref.at[t, pl.ds(REQ, 16), :], out_sem.at[t])
        for t in range(TEN)
    ]
    for copy in copies:
        copy.start()
    for copy in copies:
        copy.wait()


def with_rank_sums(index, got, table, partial):
    far = pl.BlockSpec(memory_space=pl.ANY)
    return pl.pallas_call(
        rank_kernel,
        in_specs=[
            pl.BlockSpec(memory_space=pltpu.SMEM),
            pl.BlockSpec(memory_space=pltpu.VMEM),
            far,
            far,
        ],
        out_specs=far,
        out_shape=jax.ShapeDtypeStruct(partial.shape, BF16),
        input_output_aliases={3: 0},
        scratch_shapes=[
            pltpu.VMEM((REQ, RANK, COLS), BF16),
            pltpu.VMEM((16, COLS), BF16),
            pltpu.SemaphoreType.DMA,
            pltpu.SemaphoreType.DMA((TEN,)),
        ],
        compiler_params=params(56),
        cost_estimate=pl.CostEstimate(flops=14 * 10**7, bytes_accessed=2 * MIB, transcendentals=0),
    )(index, got, table, partial)


def add_all(sums_ref, first, last):
    total = sums_ref[0, first:last, :].astype(F32)
    for t in range(1, TEN):
        total = total + sums_ref[t, first:last, :].astype(F32)
    return total


def residual_rows(got_ref):
    return got_ref[...].astype(F32)[:, 8:16, :].reshape(128, COLS)


def amateur_kernel(sums_ref, got_ref, gain_ref, o_ref, kinds_s):
    base = split_kinds(residual_rows(got_ref), kinds_s)[1]
    hidden = (base + add_all(sums_ref, 0, REQ)).astype(BF16).astype(F32)
    o_ref[...] = (hidden * gain_ref[...].astype(F32)).astype(BF16)


def amateur_rows(sums, got, gain):
    near = pl.BlockSpec(memory_space=pltpu.VMEM)
    return pl.pallas_call(
        amateur_kernel,
        in_specs=[near] * 3,
        out_specs=near,
        out_shape=jax.ShapeDtypeStruct((REQ, COLS), BF16),
        scratch_shapes=[pltpu.VMEM((COLS // HD, 128, HD), F32)],
        compiler_params=params(16),
        cost_estimate=pl.CostEstimate(flops=10**6, bytes_accessed=2 * MIB, transcendentals=0),
    )(sums, got, gain)


def expert_kernel(idx_ref, sums_ref, got_ref, gain_ref, table_ref, o_ref, rows_s, kinds_s, sem):
    start_rows(idx_ref, table_ref, rows_s, sem)
    base = split_kinds(residual_rows(got_ref), kinds_s)[0] + add_all(sums_ref, 0, REQ)
    rank = add_all(sums_ref, REQ, SENT)
    wait_rows(table_ref, rows_s, sem)
    rows = rows_s[...].reshape(REQ * RANK, COLS)
    delta = jnp.zeros((REQ, COLS), F32)
    for n in range(2):
        vector = rank[n : n + 1, :] + rank[n + 2 : n + 3, :]
        spread = jnp.where(own_lanes(REQ, COLS, 1, n * (COLS // RANK)), vector, 0.0)
        high = spread.astype(BF16)
        low = (spread - high.astype(F32)).astype(BF16)
        part = rows[n * COLS : (n + 1) * COLS, :]
        delta = delta + jnp.dot(high, part, preferred_element_type=F32)
        delta = delta + jnp.dot(low, part, preferred_element_type=F32)
    hidden = (base + LOWRANK_SCALE * delta).astype(BF16).astype(F32)
    o_ref[...] = (hidden * gain_ref[...].astype(F32)).astype(BF16)


def expert_rows(index, sums, got, gain, table):
    near = pl.BlockSpec(memory_space=pltpu.VMEM)
    return pl.pallas_call(
        expert_kernel,
        in_specs=[pl.BlockSpec(memory_space=pltpu.SMEM)]
        + [near] * 3
        + [pl.BlockSpec(memory_space=pl.ANY)],
        out_specs=near,
        out_shape=jax.ShapeDtypeStruct((REQ, COLS), BF16),
        scratch_shapes=[
            pltpu.VMEM((REQ, RANK, COLS), BF16),
            pltpu.VMEM((COLS // HD, 128, HD), F32),
            pltpu.SemaphoreType.DMA,
        ],
        compiler_params=params(56),
        cost_estimate=pl.CostEstimate(flops=3 * 10**8, bytes_accessed=2 * MIB, transcendentals=0),
    )(index, sums, got, gain, table)


def tensor_index(at, first, second):
    along_x = jnp.where(at[3] == 0, first, second)
    along_z = jnp.where(at[3] == 0, second, first)
    return lax.rem(at[1] + along_x, 4) * 4 + lax.rem(at[2] + along_z, 4)


ROWS = NY * REQ
PAIR = 2 * COLS
BOTH = 2 * VOC


def head_kernel(pieces, first, last, amateur, at_ref, inv_ref, *refs):
    count = 1 + max(piece[0] for piece in pieces)
    x_refs, wo_ref, ws_ref, refs = refs[:count], refs[count], refs[count + 1], refs[count + 2 :]
    if not first:
        sums_ref, square_ref, refs = refs[0], refs[1], refs[2:]
    if last:
        other_ref, other_lse_ref, uo_ref, us_ref, lse_ref = refs[:5]
        x_s, w_s, acc_s, sq_s, x_sem, w_sem, in_sem, q_sem, other_s, o_sem = refs[5:]
    else:
        out_ref, squares_ref, x_s, w_s, acc_s, sq_s, x_sem, w_sem, in_sem, q_sem = refs

    starts = []
    for n, (which, block, offsets) in enumerate(pieces):
        index = tensor_index(at_ref, *offsets)
        start = pl.multiple_of(index * COLS, COLS)
        starts.append(start)
        run, part = n // 2, pl.ds(n % 2 * COLS, COLS)
        for y in range(NY):
            source = x_refs[which].at[block, y]
            place = lax.rem(at_ref[0] + y, NY)
            pltpu.make_async_copy(source, x_s.at[run, place, :, part], x_sem.at[run]).start()
        for side, w_ref in enumerate((wo_ref, ws_ref)):
            pltpu.make_async_copy(
                w_ref.at[pl.ds(start, COLS), :],
                w_s.at[run, part, pl.ds(side * VOC, VOC)],
                w_sem.at[run],
            ).start()
    if not first:
        pltpu.make_async_copy(sums_ref, acc_s, in_sem).start()
        pltpu.make_async_copy(square_ref, sq_s, q_sem).start()
        pltpu.make_async_copy(square_ref, sq_s, q_sem).wait()
        pltpu.make_async_copy(sums_ref, acc_s, in_sem).wait()
    else:
        acc_s[...] = jnp.zeros((ROWS, BOTH), F32)
        sq_s[...] = jnp.zeros((ROWS, HD), F32)
    if last:
        pltpu.make_async_copy(other_ref, other_s, o_sem).start()

    def one(run, carry):
        pltpu.make_async_copy(x_s.at[run], x_s.at[run], x_sem.at[run]).wait()
        pltpu.make_async_copy(w_s.at[run], w_s.at[run], w_sem.at[run]).wait()
        x = x_s[run].reshape(ROWS, PAIR)
        acc_s[...] += jnp.dot(x, w_s[run], preferred_element_type=F32)
        return carry

    lax.fori_loop(0, len(pieces) // 2, one, 0)

    square = sq_s[...]
    for n, start in enumerate(starts):
        for j in range(COLS // HD):
            lanes = slice(n % 2 * COLS + j * HD, n % 2 * COLS + (j + 1) * HD)
            piece = x_s[n // 2, :, :, lanes].reshape(ROWS, HD).astype(F32)
            inverse = inv_ref[:, pl.ds(pl.multiple_of(start + j * HD, HD), HD)]
            square = square + piece * piece * inverse
    if not (last or amateur):
        sq_s[...] = square
        pltpu.make_async_copy(sq_s, squares_ref, q_sem).start()
        pltpu.make_async_copy(acc_s, out_ref, in_sem).start()
        pltpu.make_async_copy(sq_s, squares_ref, q_sem).wait()
        pltpu.make_async_copy(acc_s, out_ref, in_sem).wait()
        return

    factor = lax.rsqrt(jnp.sum(square, axis=1, keepdims=True) * (1.0 / WIDTH) + EPS)
    logits = acc_s[...] * factor
    peak = jnp.max(logits, axis=1, keepdims=True)
    lse = peak + jnp.log(jnp.sum(jnp.exp(logits - peak), axis=1, keepdims=True))
    sq_s[...] = jnp.broadcast_to(lse, (ROWS, HD))
    lse = jnp.transpose(sq_s[...])[0:1, :]
    if amateur:
        acc_s[...] = logits
        squares_ref[...] = lse
        pltpu.make_async_copy(acc_s, out_ref, in_sem).start()
        pltpu.make_async_copy(acc_s, out_ref, in_sem).wait()
        return
    lse_ref[:, 0:ROWS] = lse
    lse_ref[:, ROWS:] = other_lse_ref[...]
    pltpu.make_async_copy(other_ref, other_s, o_sem).wait()
    mixed = (1.0 + BETA) * logits - BETA * other_s[...]
    uo_ref[...] = mixed[:, :VOC]
    us_ref[...] = mixed[:, VOC:]


def head_part(place, arrays, pieces, inverse, w_own, w_sib, sums=None, other=None, amateur=False):
    first, last = sums is None, other is not None
    depth = len(pieces) * COLS
    runs = len(pieces) // 2
    near = pl.BlockSpec(memory_space=pltpu.VMEM)
    far = pl.BlockSpec(memory_space=pl.ANY)
    if last:
        shapes, out_specs = [(ROWS, VOC), (ROWS, VOC), (1, 2 * ROWS)], [near] * 3
    elif amateur:
        shapes, out_specs = [(ROWS, BOTH), (1, ROWS)], [far, near]
    else:
        shapes, out_specs = [(ROWS, BOTH), (ROWS, HD)], [far, far]
    dma = pltpu.SemaphoreType.DMA
    return pl.pallas_call(
        lambda *refs: head_kernel(pieces, first, last, amateur, *refs),
        in_specs=[pl.BlockSpec(memory_space=pltpu.SMEM), near]
        + [far] * (len(arrays) + 2 + (0 if first else 2))
        + ([far, near] if last else []),
        out_specs=out_specs,
        out_shape=[jax.ShapeDtypeStruct(shape, F32) for shape in shapes],
        scratch_shapes=[
            pltpu.VMEM((runs, NY, REQ, PAIR), BF16),
            pltpu.VMEM((runs, PAIR, BOTH), BF16),
            pltpu.VMEM((ROWS, BOTH), F32),
            pltpu.VMEM((ROWS, HD), F32),
            dma((runs,)),
            dma((runs,)),
            dma,
            dma,
        ]
        + ([pltpu.VMEM((ROWS, BOTH), F32), dma] if last else []),
        compiler_params=params(56),
        cost_estimate=pl.CostEstimate(
            flops=ROWS * depth,
            bytes_accessed=depth * 64,
            transcendentals=0,
        ),
    )(place, inverse, *arrays, w_own, w_sib, *(sums or ()), *(other or ()))


def contrast_kernel(core_ref, uo_ref, us_ref, no_ref, ns_ref, o_ref):
    core = core_ref[0]
    for u_ref, n_ref, parity in ((uo_ref, no_ref, core), (us_ref, ns_ref, 1 - core)):
        column = jnp.transpose(jnp.broadcast_to(n_ref[...], (HD, 512)))
        for y in range(NY):
            a, b = y * REQ, ROWS + y * REQ
            shift = (1.0 + BETA) * column[a : a + REQ] - BETA * column[b : b + REQ]
            rows = pl.ds(pl.multiple_of((2 * y + parity) * REQ, REQ), REQ)
            for j in range(VOC // HD):
                lanes = slice(j * HD, (j + 1) * HD)
                o_ref[rows, lanes] = u_ref[y * REQ : (y + 1) * REQ, lanes] - shift


def contrast(core, u_own, u_sib, norm_own, norm_sib):
    near = pl.BlockSpec(memory_space=pltpu.VMEM)
    return pl.pallas_call(
        contrast_kernel,
        in_specs=[pl.BlockSpec(memory_space=pltpu.SMEM)] + [near] * 4,
        out_specs=near,
        out_shape=jax.ShapeDtypeStruct((512, VOC), F32),
        compiler_params=params(16),
        cost_estimate=pl.CostEstimate(flops=10**6, bytes_accessed=4 * MIB, transcendentals=65536),
    )(core, u_own, u_sib, norm_own, norm_sib)


TENSOR = ("x", "z")
SWAP = [(0, 1), (1, 0)]


def combine(lse):
    peak = lse[0]
    for part in lse[1:]:
        peak = jnp.maximum(peak, part)
    total = jnp.exp(lse[0] - peak)
    for part in lse[1:]:
        total = total + jnp.exp(part - peak)
    return peak + jnp.log(total)


def from_offset(array, axis, offset):
    return lax.ppermute(array, axis, [((i + offset) % 4, i) for i in range(4)])


def from_core_offset(array, axes, offset):
    pairs = []
    for c in range(2):
        for x in range(4):
            for z in range(4):
                far_x = (x + offset) % 4 if axes[c] == "x" else x
                far_z = (z + offset) % 4 if axes[c] == "z" else z
                pairs.append((c * 16 + far_x * 4 + far_z, c * 16 + x * 4 + z))
    return lax.ppermute(array, ("c", "x", "z"), pairs)


FIRST = ("x", "z")
SECOND = ("z", "x")


def plane_of(rows):
    return jnp.stack([rows] + [from_offset(rows, "y", d) for d in range(1, 4)])


def block_of(plane):
    return jnp.stack([plane] + [from_core_offset(plane, FIRST, d) for d in range(1, 4)])


def opposite(after, before, axes):
    half = after.shape[0] // 2
    return from_core_offset(after[:half], axes, 1), from_core_offset(before[half:], axes, 3)


def per_device(
    queries,
    cached_key_rows,
    cached_value_rows,
    current_token_key,
    current_token_value,
    lengths,
    residual,
    output_projection_weight,
    request_adapter_index,
    lowrank_down_factors,
    lowrank_up_factors,
    final_norm_scale,
    vocabulary_head_matrix,
):
    core = lax.axis_index("c").astype(jnp.int32).reshape(1)
    place = jnp.stack([lax.axis_index(axis) for axis in ("y", "x", "z", "c")]).astype(jnp.int32)
    head_sib = lax.ppermute(vocabulary_head_matrix, "c", SWAP)
    down = lax.all_gather(lowrank_down_factors, ("y", "c"), axis=0, tiled=True)
    up = lax.all_gather(lowrank_up_factors, ("y", "c"), axis=0, tiled=True)
    gain = lax.dynamic_slice(final_norm_scale, (lax.axis_index(TENSOR) * COLS,), (COLS,))
    gain = gain.reshape(1, COLS)
    inverse = 1.0 / final_norm_scale.astype(F32)
    inverse = (inverse * inverse).reshape(1, WIDTH)

    sent = attention(
        queries,
        cached_key_rows,
        cached_value_rows,
        current_token_key,
        current_token_value,
        lengths,
        residual,
    )
    got = lax.all_to_all(sent, TENSOR, split_axis=0, concat_axis=0, tiled=True)
    expert, amateur = projection(got, output_projection_weight)
    amateur = lax.all_to_all(amateur, TENSOR, split_axis=0, concat_axis=0, tiled=True)
    amateur = amateur_rows(amateur, got, gain)
    amateur, got = lax.optimization_barrier((amateur, got))
    expert = with_rank_sums(request_adapter_index, got, down, expert)
    sums = lax.all_to_all(expert, TENSOR, split_axis=0, concat_axis=0, tiled=True)
    amateur, _ = lax.optimization_barrier((amateur, expert))
    amateur, sums = lax.optimization_barrier((plane_of(amateur), sums))
    amateur, sums = lax.optimization_barrier((block_of(amateur), sums))
    amateur_after = from_core_offset(amateur, SECOND, 1)
    amateur_before = from_core_offset(amateur, SECOND, 3)
    expert = block_of(plane_of(expert_rows(request_adapter_index, sums, got, gain, up)))
    expert, amateur_after, amateur_before = lax.optimization_barrier(
        (expert, amateur_after, amateur_before)
    )
    after = from_core_offset(expert, SECOND, 1)
    before = from_core_offset(expert, SECOND, 3)
    amateur_far = opposite(amateur_after, amateur_before, SECOND)
    weights = (inverse, vocabulary_head_matrix, head_sib)
    own = [(0, n, (n, 0)) for n in range(4)]
    beside = [(n // 4, n % 4, (n % 4, 1 + 2 * (n // 4))) for n in range(8)]
    across = [(n // 2, n % 2, (n, 2)) for n in range(4)]
    partial = head_part(place, [expert], own, *weights)
    pieces = own + [(1 + n, b, o) for n, b, o in beside] + [(3 + n, b, o) for n, b, o in across]
    arrays = [amateur, amateur_after, amateur_before, *amateur_far]
    other = head_part(place, arrays, pieces, *weights, amateur=True)
    after, before, *rest = lax.optimization_barrier((after, before, *partial, *other))
    partial, other = rest[:2], rest[2:]
    far = opposite(after, before, SECOND)
    partial = head_part(place, [after, before], beside, *weights, sums=partial)
    u_own, u_send, lse = head_part(place, far, across, *weights, sums=partial, other=other)
    for axis in ("y", "x", "z"):
        lse = combine([lse] + [from_offset(lse, axis, d) for d in range(1, 4)])
        if axis == "y":
            u_send, lse = lax.optimization_barrier((u_send, lse))
            u_sib = lax.ppermute(u_send, "c", SWAP)
    return contrast(core, u_own, u_sib, lse, lax.ppermute(lse, "c", SWAP))


def solution(mesh):
    fine = Mesh(np.asarray(mesh.devices).reshape(NY, 2, 4, 4), ("y", "c", "x", "z"))
    every = ("y", "c", "x", "z")
    group = ("y", "c")
    in_specs = (
        P(every, None, None),
        P(every, None, None, None),
        P(every, None, None, None),
        P(every, None, None),
        P(every, None, None),
        P(every),
        P(every, None, None),
        P(TENSOR, None),
        P(group),
        P(group, None, TENSOR),
        P(group, None, TENSOR),
        P(),
        P(None, every),
    )
    return jax.shard_map(
        per_device, mesh=fine, in_specs=in_specs, out_specs=P(None, every), check_vma=False
    )
```

```python
import math

import jax
import jax.numpy as jnp
import numpy as np
from jax import lax
from jax.experimental import pallas as pl
from jax.experimental.pallas import tpu as pltpu
from jax.sharding import Mesh
from jax.sharding import PartitionSpec as P

WIDTH = 8192
HD = 128
CTX = 64
RANK = 16
REQ = 64
TEN = 16
COLS = WIDTH // TEN
VOC = 768
NY = 4
BETA = 0.5
LOWRANK_SCALE = 2.0
EPS = 1e-05
MIB = 1 << 20
LAST = (((1,), (1,)), ((), ()))
F32 = jnp.float32
BF16 = jnp.bfloat16


def params(mib):
    return pltpu.CompilerParams(vmem_limit_bytes=mib * MIB)


GROUPS = 4


def attention_kernel(len_ref, q_ref, k_ref, v_ref, ck_ref, cv_ref, res_ref, o_ref, q_s, r_s, ck_s, cv_s):
    scale = 1.0 / math.sqrt(HD)
    for r in range(4):
        q_s[2 * r : 2 * r + 2, :] = q_ref[r].astype(F32)
        r_s[2 * r : 2 * r + 2, :] = res_ref[r].astype(F32)
        ck_s[2 * r : 2 * r + 2, :] = ck_ref[r].astype(F32)
        cv_s[2 * r : 2 * r + 2, :] = cv_ref[r].astype(F32)
    row = lax.broadcasted_iota(jnp.int32, (64, 8 * CTX), 0)
    col = lax.broadcasted_iota(jnp.int32, (64, 8 * CTX), 1)
    owner = col // CTX
    limit = jnp.zeros((64, 8 * CTX), jnp.int32)
    for r in range(4):
        limit = jnp.where(owner // 2 == r, len_ref[r], limit)
    valid = (row % 8 == owner) & (col % CTX < limit)
    for g in range(GROUPS):
        lanes = slice(g * HD, (g + 1) * HD)
        base = g * 8 * HD
        q = jnp.concatenate([q_s[:, base + h * HD : base + (h + 1) * HD] for h in range(8)], axis=0)
        keys = k_ref[:, :, :, lanes].reshape(8 * CTX, HD)
        values = v_ref[:, :, :, lanes].reshape(8 * CTX, HD)
        scores = lax.dot_general(q.astype(BF16), keys, LAST, preferred_element_type=F32) * scale
        fresh_key = jnp.concatenate([ck_s[:, lanes]] * 8, axis=0)
        fresh_value = jnp.concatenate([cv_s[:, lanes]] * 8, axis=0)
        own = jnp.sum(q * fresh_key, axis=1, keepdims=True) * scale
        highest = jnp.max(jnp.where(valid, scores, -1e30), axis=1, keepdims=True)
        highest = jnp.maximum(highest, own)
        powers = jnp.where(valid, jnp.exp(scores - highest), 0.0)
        fresh = jnp.exp(own - highest)
        summed = jnp.sum(powers, axis=1, keepdims=True) + fresh
        weights = (powers / summed).astype(BF16)
        fresh_weight = (fresh / summed).astype(BF16).astype(F32)
        mixed = jnp.dot(weights, values, preferred_element_type=F32) + fresh_weight * fresh_value
        for h in range(8):
            both = jnp.concatenate(
                [mixed[h * 8 : (h + 1) * 8, :], r_s[:, base + h * HD : base + (h + 1) * HD]], axis=0
            )
            o_ref[2 * g + h // 4, :, (h % 4) * HD : (h % 4 + 1) * HD] = both.astype(BF16)


def attention(queries, keys, values, fresh_key, fresh_value, lengths, residual):
    wide = pl.BlockSpec((4, 2, GROUPS * 1024), lambda g: (0, 0, g))
    cache = pl.BlockSpec((4, 2, CTX, GROUPS * HD), lambda g: (0, 0, 0, g))
    narrow = pl.BlockSpec((4, 2, GROUPS * HD), lambda g: (0, 0, g))
    return pl.pallas_call(
        attention_kernel,
        grid=(8 // GROUPS,),
        in_specs=[
            pl.BlockSpec(memory_space=pltpu.SMEM),
            wide,
            cache,
            cache,
            narrow,
            narrow,
            wide,
        ],
        out_specs=pl.BlockSpec((2 * GROUPS, 16, COLS), lambda g: (g, 0, 0)),
        out_shape=jax.ShapeDtypeStruct((TEN, 16, COLS), BF16),
        scratch_shapes=[
            pltpu.VMEM((8, GROUPS * 1024), F32),
            pltpu.VMEM((8, GROUPS * 1024), F32),
            pltpu.VMEM((8, GROUPS * HD), F32),
            pltpu.VMEM((8, GROUPS * HD), F32),
        ],
        compiler_params=params(56),
        cost_estimate=pl.CostEstimate(flops=3 * 10**8, bytes_accessed=3 * MIB, transcendentals=262144),
    )(lengths, queries, keys, values, fresh_key, fresh_value, residual)


def start_rows(slot_ref, table_ref, rows_s, sem):
    def one(r, carry):
        pltpu.make_async_copy(table_ref.at[slot_ref[r]], rows_s.at[r], sem).start()
        return carry

    lax.fori_loop(0, REQ, one, 0, unroll=8)


def wait_rows(table_ref, rows_s, sem):
    pltpu.make_async_copy(table_ref.at[pl.ds(0, REQ)], rows_s, sem).wait()


def own_lanes(rows, lanes, pitch, first=0):
    row = lax.broadcasted_iota(jnp.int32, (rows, lanes), 0)
    lane = lax.broadcasted_iota(jnp.int32, (rows, lanes), 1)
    return row == pitch * (lane // RANK + first)


def attended_rows(got_ref):
    return got_ref[...].astype(F32)[:, 0:8, :].reshape(128, COLS)


def split_kinds(rows, kinds_s):
    kinds = [[], []]
    for j in range(COLS // HD):
        kinds_s[j] = rows[:, j * HD : (j + 1) * HD]
        for kind in range(2):
            kinds[kind].append(kinds_s[j, pl.ds(kind, REQ, stride=2), :])
    return [jnp.concatenate(parts, axis=1) for parts in kinds]


WIDE = 4
SENT = REQ + 16


def projection_kernel(got_ref, w_ref, expert_ref, amateur_ref, att_s, kinds_s):
    @pl.when(pl.program_id(0) == 0)
    def _():
        att_s[...] = jnp.concatenate(split_kinds(attended_rows(got_ref), kinds_s), axis=0).astype(BF16)

    for t in range(WIDE):
        part = jnp.dot(
            att_s[...], w_ref[:, t * COLS : (t + 1) * COLS], preferred_element_type=F32
        )
        expert_ref[t, 0:REQ, :] = part[:REQ].astype(BF16)
        amateur_ref[t] = part[REQ:].astype(BF16)


def projection(got, weight):
    return pl.pallas_call(
        projection_kernel,
        grid=(TEN // WIDE,),
        in_specs=[
            pl.BlockSpec((TEN, 16, COLS), lambda j: (0, 0, 0)),
            pl.BlockSpec((COLS, WIDE * COLS), lambda j: (0, j)),
        ],
        out_specs=[pl.BlockSpec((WIDE, rows, COLS), lambda j: (j, 0, 0)) for rows in (SENT, REQ)],
        out_shape=[jax.ShapeDtypeStruct((TEN, rows, COLS), BF16) for rows in (SENT, REQ)],
        scratch_shapes=[
            pltpu.VMEM((128, COLS), BF16),
            pltpu.VMEM((COLS // HD, 128, HD), F32),
        ],
        compiler_params=params(56),
        cost_estimate=pl.CostEstimate(flops=11 * 10**8, bytes_accessed=11 * MIB, transcendentals=0),
    )(got, weight)


def rank_kernel(idx_ref, got_ref, table_ref, partial_ref, o_ref, rows_s, block_s, sem, out_sem):
    start_rows(idx_ref, table_ref, rows_s, sem)
    attended = attended_rows(got_ref).astype(BF16)
    wait_rows(table_ref, rows_s, sem)
    rows = rows_s[...].reshape(REQ * RANK, COLS)
    product = lax.dot_general(attended, rows, LAST, preferred_element_type=F32)
    mask = own_lanes(128, REQ * RANK, 2)
    rank = jnp.sum(jnp.where(mask, product, 0.0), axis=0, keepdims=True)
    place = lax.broadcasted_iota(jnp.int32, (16, COLS), 0)
    block = jnp.zeros((16, COLS), F32)
    for n in range(2):
        half = rank[:, n * COLS : (n + 1) * COLS]
        high = half.astype(BF16).astype(F32)
        block = jnp.where(place == n, high, block)
        block = jnp.where(place == n + 2, half - high, block)
    block_s[...] = block.astype(BF16)
    copies = [
        pltpu.make_async_copy(block_s, o_ref.at[t, pl.ds(REQ, 16), :], out_sem.at[t])
        for t in range(TEN)
    ]
    for copy in copies:
        copy.start()
    for copy in copies:
        copy.wait()


def with_rank_sums(index, got, table, partial):
    far = pl.BlockSpec(memory_space=pl.ANY)
    return pl.pallas_call(
        rank_kernel,
        in_specs=[
            pl.BlockSpec(memory_space=pltpu.SMEM),
            pl.BlockSpec(memory_space=pltpu.VMEM),
            far,
            far,
        ],
        out_specs=far,
        out_shape=jax.ShapeDtypeStruct(partial.shape, BF16),
        input_output_aliases={3: 0},
        scratch_shapes=[
            pltpu.VMEM((REQ, RANK, COLS), BF16),
            pltpu.VMEM((16, COLS), BF16),
            pltpu.SemaphoreType.DMA,
            pltpu.SemaphoreType.DMA((TEN,)),
        ],
        compiler_params=params(56),
        cost_estimate=pl.CostEstimate(flops=14 * 10**7, bytes_accessed=2 * MIB, transcendentals=0),
    )(index, got, table, partial)


def add_all(sums_ref, first, last):
    total = sums_ref[0, first:last, :].astype(F32)
    for t in range(1, TEN):
        total = total + sums_ref[t, first:last, :].astype(F32)
    return total


def residual_rows(got_ref):
    return got_ref[...].astype(F32)[:, 8:16, :].reshape(128, COLS)


def amateur_kernel(sums_ref, got_ref, gain_ref, o_ref, kinds_s):
    base = split_kinds(residual_rows(got_ref), kinds_s)[1]
    hidden = (base + add_all(sums_ref, 0, REQ)).astype(BF16).astype(F32)
    o_ref[...] = (hidden * gain_ref[...].astype(F32)).astype(BF16)


def amateur_rows(sums, got, gain):
    near = pl.BlockSpec(memory_space=pltpu.VMEM)
    return pl.pallas_call(
        amateur_kernel,
        in_specs=[near] * 3,
        out_specs=near,
        out_shape=jax.ShapeDtypeStruct((REQ, COLS), BF16),
        scratch_shapes=[pltpu.VMEM((COLS // HD, 128, HD), F32)],
        compiler_params=params(16),
        cost_estimate=pl.CostEstimate(flops=10**6, bytes_accessed=2 * MIB, transcendentals=0),
    )(sums, got, gain)


def expert_kernel(idx_ref, sums_ref, got_ref, gain_ref, table_ref, o_ref, rows_s, kinds_s, sem):
    start_rows(idx_ref, table_ref, rows_s, sem)
    base = split_kinds(residual_rows(got_ref), kinds_s)[0] + add_all(sums_ref, 0, REQ)
    rank = add_all(sums_ref, REQ, SENT)
    wait_rows(table_ref, rows_s, sem)
    rows = rows_s[...].reshape(REQ * RANK, COLS)
    delta = jnp.zeros((REQ, COLS), F32)
    for n in range(2):
        vector = rank[n : n + 1, :] + rank[n + 2 : n + 3, :]
        spread = jnp.where(own_lanes(REQ, COLS, 1, n * (COLS // RANK)), vector, 0.0)
        high = spread.astype(BF16)
        low = (spread - high.astype(F32)).astype(BF16)
        part = rows[n * COLS : (n + 1) * COLS, :]
        delta = delta + jnp.dot(high, part, preferred_element_type=F32)
        delta = delta + jnp.dot(low, part, preferred_element_type=F32)
    hidden = (base + LOWRANK_SCALE * delta).astype(BF16).astype(F32)
    o_ref[...] = (hidden * gain_ref[...].astype(F32)).astype(BF16)


def expert_rows(index, sums, got, gain, table):
    near = pl.BlockSpec(memory_space=pltpu.VMEM)
    return pl.pallas_call(
        expert_kernel,
        in_specs=[pl.BlockSpec(memory_space=pltpu.SMEM)]
        + [near] * 3
        + [pl.BlockSpec(memory_space=pl.ANY)],
        out_specs=near,
        out_shape=jax.ShapeDtypeStruct((REQ, COLS), BF16),
        scratch_shapes=[
            pltpu.VMEM((REQ, RANK, COLS), BF16),
            pltpu.VMEM((COLS // HD, 128, HD), F32),
            pltpu.SemaphoreType.DMA,
        ],
        compiler_params=params(56),
        cost_estimate=pl.CostEstimate(flops=3 * 10**8, bytes_accessed=2 * MIB, transcendentals=0),
    )(index, sums, got, gain, table)


def tensor_index(at, first, second):
    along_x = jnp.where(at[3] == 0, first, second)
    along_z = jnp.where(at[3] == 0, second, first)
    return lax.rem(at[1] + along_x, 4) * 4 + lax.rem(at[2] + along_z, 4)


ROWS = NY * REQ
PAIR = 2 * COLS
BOTH = 2 * VOC


def head_kernel(pieces, first, last, amateur, at_ref, inv_ref, *refs):
    count = 1 + max(piece[0] for piece in pieces)
    x_refs, wo_ref, ws_ref, refs = refs[:count], refs[count], refs[count + 1], refs[count + 2 :]
    if not first:
        sums_ref, square_ref, refs = refs[0], refs[1], refs[2:]
    if last:
        other_ref, other_lse_ref, uo_ref, us_ref, lse_ref = refs[:5]
        x_s, w_s, acc_s, sq_s, x_sem, w_sem, in_sem, q_sem, other_s, o_sem = refs[5:]
    else:
        out_ref, squares_ref, x_s, w_s, acc_s, sq_s, x_sem, w_sem, in_sem, q_sem = refs

    starts = []
    for n, (which, block, offsets) in enumerate(pieces):
        index = tensor_index(at_ref, *offsets)
        start = pl.multiple_of(index * COLS, COLS)
        starts.append(start)
        run, part = n // 2, pl.ds(n % 2 * COLS, COLS)
        for y in range(NY):
            source = x_refs[which].at[block, y]
            place = lax.rem(at_ref[0] + y, NY)
            pltpu.make_async_copy(source, x_s.at[run, place, :, part], x_sem.at[run]).start()
        for side, w_ref in enumerate((wo_ref, ws_ref)):
            pltpu.make_async_copy(
                w_ref.at[pl.ds(start, COLS), :],
                w_s.at[run, part, pl.ds(side * VOC, VOC)],
                w_sem.at[run],
            ).start()
    if not first:
        pltpu.make_async_copy(sums_ref, acc_s, in_sem).start()
        pltpu.make_async_copy(square_ref, sq_s, q_sem).start()
        pltpu.make_async_copy(square_ref, sq_s, q_sem).wait()
        pltpu.make_async_copy(sums_ref, acc_s, in_sem).wait()
    else:
        acc_s[...] = jnp.zeros((ROWS, BOTH), F32)
        sq_s[...] = jnp.zeros((ROWS, HD), F32)
    if last:
        pltpu.make_async_copy(other_ref, other_s, o_sem).start()

    def one(run, carry):
        pltpu.make_async_copy(x_s.at[run], x_s.at[run], x_sem.at[run]).wait()
        pltpu.make_async_copy(w_s.at[run], w_s.at[run], w_sem.at[run]).wait()
        x = x_s[run].reshape(ROWS, PAIR)
        acc_s[...] += jnp.dot(x, w_s[run], preferred_element_type=F32)
        return carry

    lax.fori_loop(0, len(pieces) // 2, one, 0)

    square = sq_s[...]
    for n, start in enumerate(starts):
        for j in range(COLS // HD):
            lanes = slice(n % 2 * COLS + j * HD, n % 2 * COLS + (j + 1) * HD)
            piece = x_s[n // 2, :, :, lanes].reshape(ROWS, HD).astype(F32)
            inverse = inv_ref[:, pl.ds(pl.multiple_of(start + j * HD, HD), HD)]
            square = square + piece * piece * inverse
    if not (last or amateur):
        sq_s[...] = square
        pltpu.make_async_copy(sq_s, squares_ref, q_sem).start()
        pltpu.make_async_copy(acc_s, out_ref, in_sem).start()
        pltpu.make_async_copy(sq_s, squares_ref, q_sem).wait()
        pltpu.make_async_copy(acc_s, out_ref, in_sem).wait()
        return

    factor = lax.rsqrt(jnp.sum(square, axis=1, keepdims=True) * (1.0 / WIDTH) + EPS)
    logits = acc_s[...] * factor
    peak = jnp.max(logits, axis=1, keepdims=True)
    lse = peak + jnp.log(jnp.sum(jnp.exp(logits - peak), axis=1, keepdims=True))
    sq_s[...] = jnp.broadcast_to(lse, (ROWS, HD))
    lse = jnp.transpose(sq_s[...])[0:1, :]
    if amateur:
        acc_s[...] = logits
        squares_ref[...] = lse
        pltpu.make_async_copy(acc_s, out_ref, in_sem).start()
        pltpu.make_async_copy(acc_s, out_ref, in_sem).wait()
        return
    lse_ref[:, 0:ROWS] = lse
    lse_ref[:, ROWS:] = other_lse_ref[...]
    pltpu.make_async_copy(other_ref, other_s, o_sem).wait()
    mixed = (1.0 + BETA) * logits - BETA * other_s[...]
    uo_ref[...] = mixed[:, :VOC]
    us_ref[...] = mixed[:, VOC:]


def head_part(place, arrays, pieces, inverse, w_own, w_sib, sums=None, other=None, amateur=False):
    first, last = sums is None, other is not None
    depth = len(pieces) * COLS
    runs = len(pieces) // 2
    near = pl.BlockSpec(memory_space=pltpu.VMEM)
    far = pl.BlockSpec(memory_space=pl.ANY)
    if last:
        shapes, out_specs = [(ROWS, VOC), (ROWS, VOC), (1, 2 * ROWS)], [near] * 3
    elif amateur:
        shapes, out_specs = [(ROWS, BOTH), (1, ROWS)], [far, near]
    else:
        shapes, out_specs = [(ROWS, BOTH), (ROWS, HD)], [far, far]
    dma = pltpu.SemaphoreType.DMA
    return pl.pallas_call(
        lambda *refs: head_kernel(pieces, first, last, amateur, *refs),
        in_specs=[pl.BlockSpec(memory_space=pltpu.SMEM), near]
        + [far] * (len(arrays) + 2 + (0 if first else 2))
        + ([far, near] if last else []),
        out_specs=out_specs,
        out_shape=[jax.ShapeDtypeStruct(shape, F32) for shape in shapes],
        scratch_shapes=[
            pltpu.VMEM((runs, NY, REQ, PAIR), BF16),
            pltpu.VMEM((runs, PAIR, BOTH), BF16),
            pltpu.VMEM((ROWS, BOTH), F32),
            pltpu.VMEM((ROWS, HD), F32),
            dma((runs,)),
            dma((runs,)),
            dma,
            dma,
        ]
        + ([pltpu.VMEM((ROWS, BOTH), F32), dma] if last else []),
        compiler_params=params(56),
        cost_estimate=pl.CostEstimate(
            flops=ROWS * depth,
            bytes_accessed=depth * 64,
            transcendentals=0,
        ),
    )(place, inverse, *arrays, w_own, w_sib, *(sums or ()), *(other or ()))


def contrast_kernel(core_ref, uo_ref, us_ref, no_ref, ns_ref, o_ref):
    core = core_ref[0]
    for u_ref, n_ref, parity in ((uo_ref, no_ref, core), (us_ref, ns_ref, 1 - core)):
        column = jnp.transpose(jnp.broadcast_to(n_ref[...], (HD, 512)))
        for y in range(NY):
            a, b = y * REQ, ROWS + y * REQ
            shift = (1.0 + BETA) * column[a : a + REQ] - BETA * column[b : b + REQ]
            rows = pl.ds(pl.multiple_of((2 * y + parity) * REQ, REQ), REQ)
            for j in range(VOC // HD):
                lanes = slice(j * HD, (j + 1) * HD)
                o_ref[rows, lanes] = u_ref[y * REQ : (y + 1) * REQ, lanes] - shift


def contrast(core, u_own, u_sib, norm_own, norm_sib):
    near = pl.BlockSpec(memory_space=pltpu.VMEM)
    return pl.pallas_call(
        contrast_kernel,
        in_specs=[pl.BlockSpec(memory_space=pltpu.SMEM)] + [near] * 4,
        out_specs=near,
        out_shape=jax.ShapeDtypeStruct((512, VOC), F32),
        compiler_params=params(16),
        cost_estimate=pl.CostEstimate(flops=10**6, bytes_accessed=4 * MIB, transcendentals=65536),
    )(core, u_own, u_sib, norm_own, norm_sib)


TENSOR = ("x", "z")
SWAP = [(0, 1), (1, 0)]


def combine(lse):
    peak = lse[0]
    for part in lse[1:]:
        peak = jnp.maximum(peak, part)
    total = jnp.exp(lse[0] - peak)
    for part in lse[1:]:
        total = total + jnp.exp(part - peak)
    return peak + jnp.log(total)


def from_offset(array, axis, offset):
    return lax.ppermute(array, axis, [((i + offset) % 4, i) for i in range(4)])


def from_core_offset(array, axes, offset):
    pairs = []
    for c in range(2):
        for x in range(4):
            for z in range(4):
                far_x = (x + offset) % 4 if axes[c] == "x" else x
                far_z = (z + offset) % 4 if axes[c] == "z" else z
                pairs.append((c * 16 + far_x * 4 + far_z, c * 16 + x * 4 + z))
    return lax.ppermute(array, ("c", "x", "z"), pairs)


FIRST = ("x", "z")
SECOND = ("z", "x")


def plane_of(rows):
    return jnp.stack([rows] + [from_offset(rows, "y", d) for d in range(1, 4)])


def block_of(plane):
    return jnp.stack([plane] + [from_core_offset(plane, FIRST, d) for d in range(1, 4)])


def opposite(after, before, axes):
    half = after.shape[0] // 2
    return from_core_offset(after[:half], axes, 1), from_core_offset(before[half:], axes, 3)


def per_device(
    queries,
    cached_key_rows,
    cached_value_rows,
    current_token_key,
    current_token_value,
    lengths,
    residual,
    output_projection_weight,
    request_adapter_index,
    lowrank_down_factors,
    lowrank_up_factors,
    final_norm_scale,
    vocabulary_head_matrix,
):
    core = lax.axis_index("c").astype(jnp.int32).reshape(1)
    place = jnp.stack([lax.axis_index(axis) for axis in ("y", "x", "z", "c")]).astype(jnp.int32)
    head_sib = lax.ppermute(vocabulary_head_matrix, "c", SWAP)
    down = lax.all_gather(lowrank_down_factors, ("y", "c"), axis=0, tiled=True)
    up = lax.all_gather(lowrank_up_factors, ("y", "c"), axis=0, tiled=True)
    gain = lax.dynamic_slice(final_norm_scale, (lax.axis_index(TENSOR) * COLS,), (COLS,))
    gain = gain.reshape(1, COLS)
    inverse = 1.0 / final_norm_scale.astype(F32)
    inverse = (inverse * inverse).reshape(1, WIDTH)

    sent = attention(
        queries,
        cached_key_rows,
        cached_value_rows,
        current_token_key,
        current_token_value,
        lengths,
        residual,
    )
    got = lax.all_to_all(sent, TENSOR, split_axis=0, concat_axis=0, tiled=True)
    expert, amateur = projection(got, output_projection_weight)
    amateur = lax.all_to_all(amateur, TENSOR, split_axis=0, concat_axis=0, tiled=True)
    amateur = amateur_rows(amateur, got, gain)
    amateur, got = lax.optimization_barrier((amateur, got))
    expert = with_rank_sums(request_adapter_index, got, down, expert)
    sums = lax.all_to_all(expert, TENSOR, split_axis=0, concat_axis=0, tiled=True)
    amateur, _ = lax.optimization_barrier((amateur, expert))
    amateur, sums = lax.optimization_barrier((plane_of(amateur), sums))
    amateur, sums = lax.optimization_barrier((block_of(amateur), sums))
    amateur_after = from_core_offset(amateur, SECOND, 1)
    amateur_before = from_core_offset(amateur, SECOND, 3)
    expert = plane_of(expert_rows(request_adapter_index, sums, got, gain, up))
    expert, amateur_after, amateur_before = lax.optimization_barrier(
        (expert, amateur_after, amateur_before)
    )
    amateur_far = opposite(amateur_after, amateur_before, SECOND)
    expert, *amateur_far = lax.optimization_barrier((block_of(expert), *amateur_far))
    after = from_core_offset(expert, SECOND, 1)
    before = from_core_offset(expert, SECOND, 3)
    weights = (inverse, vocabulary_head_matrix, head_sib)
    own = [(0, n, (n, 0)) for n in range(4)]
    beside = [(n // 4, n % 4, (n % 4, 1 + 2 * (n // 4))) for n in range(8)]
    across = [(n // 2, n % 2, (n, 2)) for n in range(4)]
    partial = head_part(place, [expert], own, *weights)
    pieces = own + [(1 + n, b, o) for n, b, o in beside] + [(3 + n, b, o) for n, b, o in across]
    arrays = [amateur, amateur_after, amateur_before, *amateur_far]
    other = head_part(place, arrays, pieces, *weights, amateur=True)
    after, before, *rest = lax.optimization_barrier((after, before, *partial, *other))
    partial, other = rest[:2], rest[2:]
    far = opposite(after, before, SECOND)
    partial = head_part(place, [after, before], beside, *weights, sums=partial)
    u_own, u_send, lse = head_part(place, far, across, *weights, sums=partial, other=other)
    for axis in ("y", "x", "z"):
        lse = combine([lse] + [from_offset(lse, axis, d) for d in range(1, 4)])
        if axis == "y":
            u_send, lse = lax.optimization_barrier((u_send, lse))
            u_sib = lax.ppermute(u_send, "c", SWAP)
    return contrast(core, u_own, u_sib, lse, lax.ppermute(lse, "c", SWAP))


def solution(mesh):
    fine = Mesh(np.asarray(mesh.devices).reshape(NY, 2, 4, 4), ("y", "c", "x", "z"))
    every = ("y", "c", "x", "z")
    group = ("y", "c")
    in_specs = (
        P(every, None, None),
        P(every, None, None, None),
        P(every, None, None, None),
        P(every, None, None),
        P(every, None, None),
        P(every),
        P(every, None, None),
        P(TENSOR, None),
        P(group),
        P(group, None, TENSOR),
        P(group, None, TENSOR),
        P(),
        P(None, every),
    )
    return jax.shard_map(
        per_device, mesh=fine, in_specs=in_specs, out_specs=P(None, every), check_vma=False
    )
```

```python
import math

import jax
import jax.numpy as jnp
import numpy as np
from jax import lax
from jax.experimental import pallas as pl
from jax.experimental.pallas import tpu as pltpu
from jax.sharding import Mesh
from jax.sharding import PartitionSpec as P

WIDTH = 8192
HD = 128
CTX = 64
RANK = 16
REQ = 64
TEN = 16
COLS = WIDTH // TEN
VOC = 768
NY = 4
BETA = 0.5
LOWRANK_SCALE = 2.0
EPS = 1e-05
MIB = 1 << 20
LAST = (((1,), (1,)), ((), ()))
F32 = jnp.float32
BF16 = jnp.bfloat16


def params(mib):
    return pltpu.CompilerParams(vmem_limit_bytes=mib * MIB)


GROUPS = 4


def attention_kernel(len_ref, q_ref, k_ref, v_ref, ck_ref, cv_ref, res_ref, o_ref, q_s, r_s, ck_s, cv_s):
    scale = 1.0 / math.sqrt(HD)
    for r in range(4):
        q_s[2 * r : 2 * r + 2, :] = q_ref[r].astype(F32)
        r_s[2 * r : 2 * r + 2, :] = res_ref[r].astype(F32)
        ck_s[2 * r : 2 * r + 2, :] = ck_ref[r].astype(F32)
        cv_s[2 * r : 2 * r + 2, :] = cv_ref[r].astype(F32)
    row = lax.broadcasted_iota(jnp.int32, (64, 8 * CTX), 0)
    col = lax.broadcasted_iota(jnp.int32, (64, 8 * CTX), 1)
    owner = col // CTX
    limit = jnp.zeros((64, 8 * CTX), jnp.int32)
    for r in range(4):
        limit = jnp.where(owner // 2 == r, len_ref[r], limit)
    valid = (row % 8 == owner) & (col % CTX < limit)
    for g in range(GROUPS):
        lanes = slice(g * HD, (g + 1) * HD)
        base = g * 8 * HD
        q = jnp.concatenate([q_s[:, base + h * HD : base + (h + 1) * HD] for h in range(8)], axis=0)
        keys = k_ref[:, :, :, lanes].reshape(8 * CTX, HD)
        values = v_ref[:, :, :, lanes].reshape(8 * CTX, HD)
        scores = lax.dot_general(q.astype(BF16), keys, LAST, preferred_element_type=F32) * scale
        fresh_key = jnp.concatenate([ck_s[:, lanes]] * 8, axis=0)
        fresh_value = jnp.concatenate([cv_s[:, lanes]] * 8, axis=0)
        own = jnp.sum(q * fresh_key, axis=1, keepdims=True) * scale
        highest = jnp.max(jnp.where(valid, scores, -1e30), axis=1, keepdims=True)
        highest = jnp.maximum(highest, own)
        powers = jnp.where(valid, jnp.exp(scores - highest), 0.0)
        fresh = jnp.exp(own - highest)
        summed = jnp.sum(powers, axis=1, keepdims=True) + fresh
        weights = (powers / summed).astype(BF16)
        fresh_weight = (fresh / summed).astype(BF16).astype(F32)
        mixed = jnp.dot(weights, values, preferred_element_type=F32) + fresh_weight * fresh_value
        for h in range(8):
            both = jnp.concatenate(
                [mixed[h * 8 : (h + 1) * 8, :], r_s[:, base + h * HD : base + (h + 1) * HD]], axis=0
            )
            o_ref[2 * g + h // 4, :, (h % 4) * HD : (h % 4 + 1) * HD] = both.astype(BF16)


def attention(queries, keys, values, fresh_key, fresh_value, lengths, residual):
    wide = pl.BlockSpec((4, 2, GROUPS * 1024), lambda g: (0, 0, g))
    cache = pl.BlockSpec((4, 2, CTX, GROUPS * HD), lambda g: (0, 0, 0, g))
    narrow = pl.BlockSpec((4, 2, GROUPS * HD), lambda g: (0, 0, g))
    return pl.pallas_call(
        attention_kernel,
        grid=(8 // GROUPS,),
        in_specs=[
            pl.BlockSpec(memory_space=pltpu.SMEM),
            wide,
            cache,
            cache,
            narrow,
            narrow,
            wide,
        ],
        out_specs=pl.BlockSpec((2 * GROUPS, 16, COLS), lambda g: (g, 0, 0)),
        out_shape=jax.ShapeDtypeStruct((TEN, 16, COLS), BF16),
        scratch_shapes=[
            pltpu.VMEM((8, GROUPS * 1024), F32),
            pltpu.VMEM((8, GROUPS * 1024), F32),
            pltpu.VMEM((8, GROUPS * HD), F32),
            pltpu.VMEM((8, GROUPS * HD), F32),
        ],
        compiler_params=params(56),
        cost_estimate=pl.CostEstimate(flops=3 * 10**8, bytes_accessed=3 * MIB, transcendentals=262144),
    )(lengths, queries, keys, values, fresh_key, fresh_value, residual)


def start_rows(slot_ref, table_ref, rows_s, sem):
    def one(r, carry):
        pltpu.make_async_copy(table_ref.at[slot_ref[r]], rows_s.at[r], sem).start()
        return carry

    lax.fori_loop(0, REQ, one, 0, unroll=8)


def wait_rows(table_ref, rows_s, sem):
    pltpu.make_async_copy(table_ref.at[pl.ds(0, REQ)], rows_s, sem).wait()


def own_lanes(rows, lanes, pitch, first=0):
    row = lax.broadcasted_iota(jnp.int32, (rows, lanes), 0)
    lane = lax.broadcasted_iota(jnp.int32, (rows, lanes), 1)
    return row == pitch * (lane // RANK + first)


def attended_rows(got_ref):
    return got_ref[...].astype(F32)[:, 0:8, :].reshape(128, COLS)


def split_kinds(rows, kinds_s):
    kinds = [[], []]
    for j in range(COLS // HD):
        kinds_s[j] = rows[:, j * HD : (j + 1) * HD]
        for kind in range(2):
            kinds[kind].append(kinds_s[j, pl.ds(kind, REQ, stride=2), :])
    return [jnp.concatenate(parts, axis=1) for parts in kinds]


WIDE = 4
SENT = REQ + 16


def projection_kernel(got_ref, w_ref, expert_ref, amateur_ref, att_s, kinds_s):
    @pl.when(pl.program_id(0) == 0)
    def _():
        att_s[...] = jnp.concatenate(split_kinds(attended_rows(got_ref), kinds_s), axis=0).astype(BF16)

    for t in range(WIDE):
        part = jnp.dot(
            att_s[...], w_ref[:, t * COLS : (t + 1) * COLS], preferred_element_type=F32
        )
        expert_ref[t, 0:REQ, :] = part[:REQ].astype(BF16)
        amateur_ref[t] = part[REQ:].astype(BF16)


def projection(got, weight):
    return pl.pallas_call(
        projection_kernel,
        grid=(TEN // WIDE,),
        in_specs=[
            pl.BlockSpec((TEN, 16, COLS), lambda j: (0, 0, 0)),
            pl.BlockSpec((COLS, WIDE * COLS), lambda j: (0, j)),
        ],
        out_specs=[pl.BlockSpec((WIDE, rows, COLS), lambda j: (j, 0, 0)) for rows in (SENT, REQ)],
        out_shape=[jax.ShapeDtypeStruct((TEN, rows, COLS), BF16) for rows in (SENT, REQ)],
        scratch_shapes=[
            pltpu.VMEM((128, COLS), BF16),
            pltpu.VMEM((COLS // HD, 128, HD), F32),
        ],
        compiler_params=params(56),
        cost_estimate=pl.CostEstimate(flops=11 * 10**8, bytes_accessed=11 * MIB, transcendentals=0),
    )(got, weight)


def rank_kernel(idx_ref, got_ref, table_ref, partial_ref, o_ref, rows_s, block_s, sem, out_sem):
    start_rows(idx_ref, table_ref, rows_s, sem)
    attended = attended_rows(got_ref).astype(BF16)
    wait_rows(table_ref, rows_s, sem)
    rows = rows_s[...].reshape(REQ * RANK, COLS)
    product = lax.dot_general(attended, rows, LAST, preferred_element_type=F32)
    mask = own_lanes(128, REQ * RANK, 2)
    rank = jnp.sum(jnp.where(mask, product, 0.0), axis=0, keepdims=True)
    place = lax.broadcasted_iota(jnp.int32, (16, COLS), 0)
    block = jnp.zeros((16, COLS), F32)
    for n in range(2):
        half = rank[:, n * COLS : (n + 1) * COLS]
        high = half.astype(BF16).astype(F32)
        block = jnp.where(place == n, high, block)
        block = jnp.where(place == n + 2, half - high, block)
    block_s[...] = block.astype(BF16)
    copies = [
        pltpu.make_async_copy(block_s, o_ref.at[t, pl.ds(REQ, 16), :], out_sem.at[t])
        for t in range(TEN)
    ]
    for copy in copies:
        copy.start()
    for copy in copies:
        copy.wait()


def with_rank_sums(index, got, table, partial):
    far = pl.BlockSpec(memory_space=pl.ANY)
    return pl.pallas_call(
        rank_kernel,
        in_specs=[
            pl.BlockSpec(memory_space=pltpu.SMEM),
            pl.BlockSpec(memory_space=pltpu.VMEM),
            far,
            far,
        ],
        out_specs=far,
        out_shape=jax.ShapeDtypeStruct(partial.shape, BF16),
        input_output_aliases={3: 0},
        scratch_shapes=[
            pltpu.VMEM((REQ, RANK, COLS), BF16),
            pltpu.VMEM((16, COLS), BF16),
            pltpu.SemaphoreType.DMA,
            pltpu.SemaphoreType.DMA((TEN,)),
        ],
        compiler_params=params(56),
        cost_estimate=pl.CostEstimate(flops=14 * 10**7, bytes_accessed=2 * MIB, transcendentals=0),
    )(index, got, table, partial)


def add_all(sums_ref, first, last):
    total = sums_ref[0, first:last, :].astype(F32)
    for t in range(1, TEN):
        total = total + sums_ref[t, first:last, :].astype(F32)
    return total


def residual_rows(got_ref):
    return got_ref[...].astype(F32)[:, 8:16, :].reshape(128, COLS)


def amateur_kernel(sums_ref, got_ref, gain_ref, o_ref, kinds_s):
    base = split_kinds(residual_rows(got_ref), kinds_s)[1]
    hidden = (base + add_all(sums_ref, 0, REQ)).astype(BF16).astype(F32)
    o_ref[...] = (hidden * gain_ref[...].astype(F32)).astype(BF16)


def amateur_rows(sums, got, gain):
    near = pl.BlockSpec(memory_space=pltpu.VMEM)
    return pl.pallas_call(
        amateur_kernel,
        in_specs=[near] * 3,
        out_specs=near,
        out_shape=jax.ShapeDtypeStruct((REQ, COLS), BF16),
        scratch_shapes=[pltpu.VMEM((COLS // HD, 128, HD), F32)],
        compiler_params=params(16),
        cost_estimate=pl.CostEstimate(flops=10**6, bytes_accessed=2 * MIB, transcendentals=0),
    )(sums, got, gain)


def expert_kernel(idx_ref, sums_ref, got_ref, gain_ref, table_ref, o_ref, rows_s, kinds_s, sem):
    start_rows(idx_ref, table_ref, rows_s, sem)
    base = split_kinds(residual_rows(got_ref), kinds_s)[0] + add_all(sums_ref, 0, REQ)
    rank = add_all(sums_ref, REQ, SENT)
    wait_rows(table_ref, rows_s, sem)
    rows = rows_s[...].reshape(REQ * RANK, COLS)
    delta = jnp.zeros((REQ, COLS), F32)
    for n in range(2):
        vector = rank[n : n + 1, :] + rank[n + 2 : n + 3, :]
        spread = jnp.where(own_lanes(REQ, COLS, 1, n * (COLS // RANK)), vector, 0.0)
        high = spread.astype(BF16)
        low = (spread - high.astype(F32)).astype(BF16)
        part = rows[n * COLS : (n + 1) * COLS, :]
        delta = delta + jnp.dot(high, part, preferred_element_type=F32)
        delta = delta + jnp.dot(low, part, preferred_element_type=F32)
    hidden = (base + LOWRANK_SCALE * delta).astype(BF16).astype(F32)
    o_ref[...] = (hidden * gain_ref[...].astype(F32)).astype(BF16)


def expert_rows(index, sums, got, gain, table):
    near = pl.BlockSpec(memory_space=pltpu.VMEM)
    return pl.pallas_call(
        expert_kernel,
        in_specs=[pl.BlockSpec(memory_space=pltpu.SMEM)]
        + [near] * 3
        + [pl.BlockSpec(memory_space=pl.ANY)],
        out_specs=near,
        out_shape=jax.ShapeDtypeStruct((REQ, COLS), BF16),
        scratch_shapes=[
            pltpu.VMEM((REQ, RANK, COLS), BF16),
            pltpu.VMEM((COLS // HD, 128, HD), F32),
            pltpu.SemaphoreType.DMA,
        ],
        compiler_params=params(56),
        cost_estimate=pl.CostEstimate(flops=3 * 10**8, bytes_accessed=2 * MIB, transcendentals=0),
    )(index, sums, got, gain, table)


def tensor_index(at, first, second):
    along_x = jnp.where(at[3] == 0, first, second)
    along_z = jnp.where(at[3] == 0, second, first)
    return lax.rem(at[1] + along_x, 4) * 4 + lax.rem(at[2] + along_z, 4)


ROWS = NY * REQ
PAIR = 2 * COLS
BOTH = 2 * VOC


def head_kernel(pieces, first, last, amateur, at_ref, inv_ref, *refs):
    count = 1 + max(piece[0] for piece in pieces)
    x_refs, wo_ref, ws_ref, refs = refs[:count], refs[count], refs[count + 1], refs[count + 2 :]
    if not first:
        sums_ref, square_ref, refs = refs[0], refs[1], refs[2:]
    if last:
        other_ref, other_lse_ref, uo_ref, us_ref, lse_ref = refs[:5]
        x_s, w_s, acc_s, sq_s, x_sem, w_sem, in_sem, q_sem, other_s, o_sem = refs[5:]
    else:
        out_ref, squares_ref, x_s, w_s, acc_s, sq_s, x_sem, w_sem, in_sem, q_sem = refs

    if not first:
        pltpu.make_async_copy(square_ref, sq_s, q_sem).start()
        pltpu.make_async_copy(sums_ref, acc_s, in_sem).start()
    starts = []
    for n, (which, block, offsets) in enumerate(pieces):
        index = tensor_index(at_ref, *offsets)
        start = pl.multiple_of(index * COLS, COLS)
        starts.append(start)
        run, part = n // 2, pl.ds(n % 2 * COLS, COLS)
        for y in range(NY):
            source = x_refs[which].at[block, y]
            place = lax.rem(at_ref[0] + y, NY)
            pltpu.make_async_copy(source, x_s.at[run, place, :, part], x_sem.at[run]).start()
        for side, w_ref in enumerate((wo_ref, ws_ref)):
            pltpu.make_async_copy(
                w_ref.at[pl.ds(start, COLS), :],
                w_s.at[run, part, pl.ds(side * VOC, VOC)],
                w_sem.at[run],
            ).start()
    if not first:
        pltpu.make_async_copy(square_ref, sq_s, q_sem).wait()
        pltpu.make_async_copy(sums_ref, acc_s, in_sem).wait()
    else:
        acc_s[...] = jnp.zeros((ROWS, BOTH), F32)
        sq_s[...] = jnp.zeros((ROWS, HD), F32)
    if last:
        pltpu.make_async_copy(other_ref, other_s, o_sem).start()

    def one(run, carry):
        pltpu.make_async_copy(x_s.at[run], x_s.at[run], x_sem.at[run]).wait()
        pltpu.make_async_copy(w_s.at[run], w_s.at[run], w_sem.at[run]).wait()
        x = x_s[run].reshape(ROWS, PAIR)
        acc_s[...] += jnp.dot(x, w_s[run], preferred_element_type=F32)
        return carry

    lax.fori_loop(0, len(pieces) // 2, one, 0)

    square = sq_s[...]
    for n, start in enumerate(starts):
        for j in range(COLS // HD):
            lanes = slice(n % 2 * COLS + j * HD, n % 2 * COLS + (j + 1) * HD)
            piece = x_s[n // 2, :, :, lanes].reshape(ROWS, HD).astype(F32)
            inverse = inv_ref[:, pl.ds(pl.multiple_of(start + j * HD, HD), HD)]
            square = square + piece * piece * inverse
    if not (last or amateur):
        sq_s[...] = square
        pltpu.make_async_copy(sq_s, squares_ref, q_sem).start()
        pltpu.make_async_copy(acc_s, out_ref, in_sem).start()
        pltpu.make_async_copy(sq_s, squares_ref, q_sem).wait()
        pltpu.make_async_copy(acc_s, out_ref, in_sem).wait()
        return

    factor = lax.rsqrt(jnp.sum(square, axis=1, keepdims=True) * (1.0 / WIDTH) + EPS)
    logits = acc_s[...] * factor
    peak = jnp.max(logits, axis=1, keepdims=True)
    lse = peak + jnp.log(jnp.sum(jnp.exp(logits - peak), axis=1, keepdims=True))
    sq_s[...] = jnp.broadcast_to(lse, (ROWS, HD))
    lse = jnp.transpose(sq_s[...])[0:1, :]
    if amateur:
        acc_s[...] = logits
        squares_ref[...] = lse
        pltpu.make_async_copy(acc_s, out_ref, in_sem).start()
        pltpu.make_async_copy(acc_s, out_ref, in_sem).wait()
        return
    lse_ref[:, 0:ROWS] = lse
    lse_ref[:, ROWS:] = other_lse_ref[...]
    pltpu.make_async_copy(other_ref, other_s, o_sem).wait()
    mixed = (1.0 + BETA) * logits - BETA * other_s[...]
    uo_ref[...] = mixed[:, :VOC]
    us_ref[...] = mixed[:, VOC:]


def head_part(place, arrays, pieces, inverse, w_own, w_sib, sums=None, other=None, amateur=False):
    first, last = sums is None, other is not None
    depth = len(pieces) * COLS
    runs = len(pieces) // 2
    near = pl.BlockSpec(memory_space=pltpu.VMEM)
    far = pl.BlockSpec(memory_space=pl.ANY)
    if last:
        shapes, out_specs = [(ROWS, VOC), (ROWS, VOC), (1, 2 * ROWS)], [near] * 3
    elif amateur:
        shapes, out_specs = [(ROWS, BOTH), (1, ROWS)], [far, near]
    else:
        shapes, out_specs = [(ROWS, BOTH), (ROWS, HD)], [far, far]
    dma = pltpu.SemaphoreType.DMA
    return pl.pallas_call(
        lambda *refs: head_kernel(pieces, first, last, amateur, *refs),
        in_specs=[pl.BlockSpec(memory_space=pltpu.SMEM), near]
        + [far] * (len(arrays) + 2 + (0 if first else 2))
        + ([far, near] if last else []),
        out_specs=out_specs,
        out_shape=[jax.ShapeDtypeStruct(shape, F32) for shape in shapes],
        scratch_shapes=[
            pltpu.VMEM((runs, NY, REQ, PAIR), BF16),
            pltpu.VMEM((runs, PAIR, BOTH), BF16),
            pltpu.VMEM((ROWS, BOTH), F32),
            pltpu.VMEM((ROWS, HD), F32),
            dma((runs,)),
            dma((runs,)),
            dma,
            dma,
        ]
        + ([pltpu.VMEM((ROWS, BOTH), F32), dma] if last else []),
        compiler_params=params(56),
        cost_estimate=pl.CostEstimate(
            flops=ROWS * depth,
            bytes_accessed=depth * 64,
            transcendentals=0,
        ),
    )(place, inverse, *arrays, w_own, w_sib, *(sums or ()), *(other or ()))


def contrast_kernel(core_ref, uo_ref, us_ref, no_ref, ns_ref, o_ref):
    core = core_ref[0]
    for u_ref, n_ref, parity in ((uo_ref, no_ref, core), (us_ref, ns_ref, 1 - core)):
        column = jnp.transpose(jnp.broadcast_to(n_ref[...], (HD, 512)))
        for y in range(NY):
            a, b = y * REQ, ROWS + y * REQ
            shift = (1.0 + BETA) * column[a : a + REQ] - BETA * column[b : b + REQ]
            rows = pl.ds(pl.multiple_of((2 * y + parity) * REQ, REQ), REQ)
            for j in range(VOC // HD):
                lanes = slice(j * HD, (j + 1) * HD)
                o_ref[rows, lanes] = u_ref[y * REQ : (y + 1) * REQ, lanes] - shift


def contrast(core, u_own, u_sib, norm_own, norm_sib):
    near = pl.BlockSpec(memory_space=pltpu.VMEM)
    return pl.pallas_call(
        contrast_kernel,
        in_specs=[pl.BlockSpec(memory_space=pltpu.SMEM)] + [near] * 4,
        out_specs=near,
        out_shape=jax.ShapeDtypeStruct((512, VOC), F32),
        compiler_params=params(16),
        cost_estimate=pl.CostEstimate(flops=10**6, bytes_accessed=4 * MIB, transcendentals=65536),
    )(core, u_own, u_sib, norm_own, norm_sib)


TENSOR = ("x", "z")
SWAP = [(0, 1), (1, 0)]


def combine(lse):
    peak = lse[0]
    for part in lse[1:]:
        peak = jnp.maximum(peak, part)
    total = jnp.exp(lse[0] - peak)
    for part in lse[1:]:
        total = total + jnp.exp(part - peak)
    return peak + jnp.log(total)


def from_offset(array, axis, offset):
    return lax.ppermute(array, axis, [((i + offset) % 4, i) for i in range(4)])


def from_core_offset(array, axes, offset):
    pairs = []
    for c in range(2):
        for x in range(4):
            for z in range(4):
                far_x = (x + offset) % 4 if axes[c] == "x" else x
                far_z = (z + offset) % 4 if axes[c] == "z" else z
                pairs.append((c * 16 + far_x * 4 + far_z, c * 16 + x * 4 + z))
    return lax.ppermute(array, ("c", "x", "z"), pairs)


FIRST = ("x", "z")
SECOND = ("z", "x")


def plane_of(rows):
    return jnp.stack([rows] + [from_offset(rows, "y", d) for d in range(1, 4)])


def block_of(plane):
    return jnp.stack([plane] + [from_core_offset(plane, FIRST, d) for d in range(1, 4)])


def opposite(after, before, axes):
    half = after.shape[0] // 2
    return from_core_offset(after[:half], axes, 1), from_core_offset(before[half:], axes, 3)


def per_device(
    queries,
    cached_key_rows,
    cached_value_rows,
    current_token_key,
    current_token_value,
    lengths,
    residual,
    output_projection_weight,
    request_adapter_index,
    lowrank_down_factors,
    lowrank_up_factors,
    final_norm_scale,
    vocabulary_head_matrix,
):
    core = lax.axis_index("c").astype(jnp.int32).reshape(1)
    place = jnp.stack([lax.axis_index(axis) for axis in ("y", "x", "z", "c")]).astype(jnp.int32)
    head_sib = lax.ppermute(vocabulary_head_matrix, "c", SWAP)
    down = lax.all_gather(lowrank_down_factors, ("y", "c"), axis=0, tiled=True)
    up = lax.all_gather(lowrank_up_factors, ("y", "c"), axis=0, tiled=True)
    gain = lax.dynamic_slice(final_norm_scale, (lax.axis_index(TENSOR) * COLS,), (COLS,))
    gain = gain.reshape(1, COLS)
    inverse = 1.0 / final_norm_scale.astype(F32)
    inverse = (inverse * inverse).reshape(1, WIDTH)

    sent = attention(
        queries,
        cached_key_rows,
        cached_value_rows,
        current_token_key,
        current_token_value,
        lengths,
        residual,
    )
    got = lax.all_to_all(sent, TENSOR, split_axis=0, concat_axis=0, tiled=True)
    expert, amateur = projection(got, output_projection_weight)
    amateur = lax.all_to_all(amateur, TENSOR, split_axis=0, concat_axis=0, tiled=True)
    amateur = amateur_rows(amateur, got, gain)
    amateur, got = lax.optimization_barrier((amateur, got))
    expert = with_rank_sums(request_adapter_index, got, down, expert)
    sums = lax.all_to_all(expert, TENSOR, split_axis=0, concat_axis=0, tiled=True)
    amateur, _ = lax.optimization_barrier((amateur, expert))
    amateur, sums = lax.optimization_barrier((plane_of(amateur), sums))
    amateur, sums = lax.optimization_barrier((block_of(amateur), sums))
    amateur_after = from_core_offset(amateur, SECOND, 1)
    amateur_before = from_core_offset(amateur, SECOND, 3)
    expert = plane_of(expert_rows(request_adapter_index, sums, got, gain, up))
    expert, amateur_after, amateur_before = lax.optimization_barrier(
        (expert, amateur_after, amateur_before)
    )
    amateur_far = opposite(amateur_after, amateur_before, SECOND)
    expert, *amateur_far = lax.optimization_barrier((block_of(expert), *amateur_far))
    after = from_core_offset(expert, SECOND, 1)
    before = from_core_offset(expert, SECOND, 3)
    weights = (inverse, vocabulary_head_matrix, head_sib)
    own = [(0, n, (n, 0)) for n in range(4)]
    beside = [(n // 4, n % 4, (n % 4, 1 + 2 * (n // 4))) for n in range(8)]
    across = [(n // 2, n % 2, (n, 2)) for n in range(4)]
    pieces = own + [(1 + n, b, o) for n, b, o in beside] + [(3 + n, b, o) for n, b, o in across]
    arrays = [amateur, amateur_after, amateur_before, *amateur_far]
    other = head_part(place, arrays, pieces, *weights, amateur=True)
    after, before, *other = lax.optimization_barrier((after, before, *other))
    far = opposite(after, before, SECOND)
    pieces = own + [(1 + n, b, o) for n, b, o in beside]
    partial = head_part(place, [expert, after, before], pieces, *weights)
    u_own, u_send, lse = head_part(place, far, across, *weights, sums=partial, other=other)
    for axis in ("y", "x", "z"):
        lse = combine([lse] + [from_offset(lse, axis, d) for d in range(1, 4)])
        if axis == "y":
            u_send, lse = lax.optimization_barrier((u_send, lse))
            u_sib = lax.ppermute(u_send, "c", SWAP)
    return contrast(core, u_own, u_sib, lse, lax.ppermute(lse, "c", SWAP))


def solution(mesh):
    fine = Mesh(np.asarray(mesh.devices).reshape(NY, 2, 4, 4), ("y", "c", "x", "z"))
    every = ("y", "c", "x", "z")
    group = ("y", "c")
    in_specs = (
        P(every, None, None),
        P(every, None, None, None),
        P(every, None, None, None),
        P(every, None, None),
        P(every, None, None),
        P(every),
        P(every, None, None),
        P(TENSOR, None),
        P(group),
        P(group, None, TENSOR),
        P(group, None, TENSOR),
        P(),
        P(None, every),
    )
    return jax.shard_map(
        per_device, mesh=fine, in_specs=in_specs, out_specs=P(None, every), check_vma=False
    )
```

```python
import math

import jax
import jax.numpy as jnp
import numpy as np
from jax import lax
from jax.experimental import pallas as pl
from jax.experimental.pallas import tpu as pltpu
from jax.sharding import Mesh
from jax.sharding import PartitionSpec as P

WIDTH = 8192
HD = 128
CTX = 64
RANK = 16
REQ = 64
TEN = 16
COLS = WIDTH // TEN
VOC = 768
NY = 4
BETA = 0.5
LOWRANK_SCALE = 2.0
EPS = 1e-05
MIB = 1 << 20
LAST = (((1,), (1,)), ((), ()))
F32 = jnp.float32
BF16 = jnp.bfloat16


def params(mib):
    return pltpu.CompilerParams(vmem_limit_bytes=mib * MIB)


GROUPS = 4


def attention_kernel(len_ref, q_ref, k_ref, v_ref, ck_ref, cv_ref, res_ref, o_ref, q_s, r_s, ck_s, cv_s):
    scale = 1.0 / math.sqrt(HD)
    for r in range(4):
        q_s[2 * r : 2 * r + 2, :] = q_ref[r].astype(F32)
        r_s[2 * r : 2 * r + 2, :] = res_ref[r].astype(F32)
        ck_s[2 * r : 2 * r + 2, :] = ck_ref[r].astype(F32)
        cv_s[2 * r : 2 * r + 2, :] = cv_ref[r].astype(F32)
    row = lax.broadcasted_iota(jnp.int32, (64, 8 * CTX), 0)
    col = lax.broadcasted_iota(jnp.int32, (64, 8 * CTX), 1)
    owner = col // CTX
    limit = jnp.zeros((64, 8 * CTX), jnp.int32)
    for r in range(4):
        limit = jnp.where(owner // 2 == r, len_ref[r], limit)
    valid = (row % 8 == owner) & (col % CTX < limit)
    for g in range(GROUPS):
        lanes = slice(g * HD, (g + 1) * HD)
        base = g * 8 * HD
        q = jnp.concatenate([q_s[:, base + h * HD : base + (h + 1) * HD] for h in range(8)], axis=0)
        keys = k_ref[:, :, :, lanes].reshape(8 * CTX, HD)
        values = v_ref[:, :, :, lanes].reshape(8 * CTX, HD)
        scores = lax.dot_general(q.astype(BF16), keys, LAST, preferred_element_type=F32) * scale
        fresh_key = jnp.concatenate([ck_s[:, lanes]] * 8, axis=0)
        fresh_value = jnp.concatenate([cv_s[:, lanes]] * 8, axis=0)
        own = jnp.sum(q * fresh_key, axis=1, keepdims=True) * scale
        highest = jnp.max(jnp.where(valid, scores, -1e30), axis=1, keepdims=True)
        highest = jnp.maximum(highest, own)
        powers = jnp.where(valid, jnp.exp(scores - highest), 0.0)
        fresh = jnp.exp(own - highest)
        summed = jnp.sum(powers, axis=1, keepdims=True) + fresh
        weights = (powers / summed).astype(BF16)
        fresh_weight = (fresh / summed).astype(BF16).astype(F32)
        mixed = jnp.dot(weights, values, preferred_element_type=F32) + fresh_weight * fresh_value
        for h in range(8):
            both = jnp.concatenate(
                [mixed[h * 8 : (h + 1) * 8, :], r_s[:, base + h * HD : base + (h + 1) * HD]], axis=0
            )
            o_ref[2 * g + h // 4, :, (h % 4) * HD : (h % 4 + 1) * HD] = both.astype(BF16)


def attention(queries, keys, values, fresh_key, fresh_value, lengths, residual):
    wide = pl.BlockSpec((4, 2, GROUPS * 1024), lambda g: (0, 0, g))
    cache = pl.BlockSpec((4, 2, CTX, GROUPS * HD), lambda g: (0, 0, 0, g))
    narrow = pl.BlockSpec((4, 2, GROUPS * HD), lambda g: (0, 0, g))
    return pl.pallas_call(
        attention_kernel,
        grid=(8 // GROUPS,),
        in_specs=[
            pl.BlockSpec(memory_space=pltpu.SMEM),
            wide,
            cache,
            cache,
            narrow,
            narrow,
            wide,
        ],
        out_specs=pl.BlockSpec((2 * GROUPS, 16, COLS), lambda g: (g, 0, 0)),
        out_shape=jax.ShapeDtypeStruct((TEN, 16, COLS), BF16),
        scratch_shapes=[
            pltpu.VMEM((8, GROUPS * 1024), F32),
            pltpu.VMEM((8, GROUPS * 1024), F32),
            pltpu.VMEM((8, GROUPS * HD), F32),
            pltpu.VMEM((8, GROUPS * HD), F32),
        ],
        compiler_params=params(56),
        cost_estimate=pl.CostEstimate(flops=3 * 10**8, bytes_accessed=3 * MIB, transcendentals=262144),
    )(lengths, queries, keys, values, fresh_key, fresh_value, residual)


def start_rows(slot_ref, table_ref, rows_s, sem):
    def one(r, carry):
        pltpu.make_async_copy(table_ref.at[slot_ref[r]], rows_s.at[r], sem).start()
        return carry

    lax.fori_loop(0, REQ, one, 0, unroll=8)


def wait_rows(table_ref, rows_s, sem):
    pltpu.make_async_copy(table_ref.at[pl.ds(0, REQ)], rows_s, sem).wait()


def own_lanes(rows, lanes, pitch, first=0):
    row = lax.broadcasted_iota(jnp.int32, (rows, lanes), 0)
    lane = lax.broadcasted_iota(jnp.int32, (rows, lanes), 1)
    return row == pitch * (lane // RANK + first)


def attended_rows(got_ref):
    return got_ref[...].astype(F32)[:, 0:8, :].reshape(128, COLS)


def split_kinds(rows, kinds_s):
    kinds = [[], []]
    for j in range(COLS // HD):
        kinds_s[j] = rows[:, j * HD : (j + 1) * HD]
        for kind in range(2):
            kinds[kind].append(kinds_s[j, pl.ds(kind, REQ, stride=2), :])
    return [jnp.concatenate(parts, axis=1) for parts in kinds]


WIDE = 4
SENT = REQ + 16


def projection_kernel(got_ref, w_ref, expert_ref, amateur_ref, att_s, kinds_s):
    @pl.when(pl.program_id(0) == 0)
    def _():
        att_s[...] = jnp.concatenate(split_kinds(attended_rows(got_ref), kinds_s), axis=0).astype(BF16)

    for t in range(WIDE):
        part = jnp.dot(
            att_s[...], w_ref[:, t * COLS : (t + 1) * COLS], preferred_element_type=F32
        )
        expert_ref[t, 0:REQ, :] = part[:REQ].astype(BF16)
        amateur_ref[t] = part[REQ:].astype(BF16)


def projection(got, weight):
    return pl.pallas_call(
        projection_kernel,
        grid=(TEN // WIDE,),
        in_specs=[
            pl.BlockSpec((TEN, 16, COLS), lambda j: (0, 0, 0)),
            pl.BlockSpec((COLS, WIDE * COLS), lambda j: (0, j)),
        ],
        out_specs=[pl.BlockSpec((WIDE, rows, COLS), lambda j: (j, 0, 0)) for rows in (SENT, REQ)],
        out_shape=[jax.ShapeDtypeStruct((TEN, rows, COLS), BF16) for rows in (SENT, REQ)],
        scratch_shapes=[
            pltpu.VMEM((128, COLS), BF16),
            pltpu.VMEM((COLS // HD, 128, HD), F32),
        ],
        compiler_params=params(56),
        cost_estimate=pl.CostEstimate(flops=11 * 10**8, bytes_accessed=11 * MIB, transcendentals=0),
    )(got, weight)


def rank_kernel(idx_ref, got_ref, table_ref, partial_ref, o_ref, rows_s, block_s, sem, out_sem):
    start_rows(idx_ref, table_ref, rows_s, sem)
    attended = attended_rows(got_ref).astype(BF16)
    wait_rows(table_ref, rows_s, sem)
    rows = rows_s[...].reshape(REQ * RANK, COLS)
    product = lax.dot_general(attended, rows, LAST, preferred_element_type=F32)
    mask = own_lanes(128, REQ * RANK, 2)
    rank = jnp.sum(jnp.where(mask, product, 0.0), axis=0, keepdims=True)
    place = lax.broadcasted_iota(jnp.int32, (16, COLS), 0)
    block = jnp.zeros((16, COLS), F32)
    for n in range(2):
        half = rank[:, n * COLS : (n + 1) * COLS]
        high = half.astype(BF16).astype(F32)
        block = jnp.where(place == n, high, block)
        block = jnp.where(place == n + 2, half - high, block)
    block_s[...] = block.astype(BF16)
    copies = [
        pltpu.make_async_copy(block_s, o_ref.at[t, pl.ds(REQ, 16), :], out_sem.at[t])
        for t in range(TEN)
    ]
    for copy in copies:
        copy.start()
    for copy in copies:
        copy.wait()


def with_rank_sums(index, got, table, partial):
    far = pl.BlockSpec(memory_space=pl.ANY)
    return pl.pallas_call(
        rank_kernel,
        in_specs=[
            pl.BlockSpec(memory_space=pltpu.SMEM),
            pl.BlockSpec(memory_space=pltpu.VMEM),
            far,
            far,
        ],
        out_specs=far,
        out_shape=jax.ShapeDtypeStruct(partial.shape, BF16),
        input_output_aliases={3: 0},
        scratch_shapes=[
            pltpu.VMEM((REQ, RANK, COLS), BF16),
            pltpu.VMEM((16, COLS), BF16),
            pltpu.SemaphoreType.DMA,
            pltpu.SemaphoreType.DMA((TEN,)),
        ],
        compiler_params=params(56),
        cost_estimate=pl.CostEstimate(flops=14 * 10**7, bytes_accessed=2 * MIB, transcendentals=0),
    )(index, got, table, partial)


def add_all(sums_ref, first, last):
    total = sums_ref[0, first:last, :].astype(F32)
    for t in range(1, TEN):
        total = total + sums_ref[t, first:last, :].astype(F32)
    return total


def residual_rows(got_ref):
    return got_ref[...].astype(F32)[:, 8:16, :].reshape(128, COLS)


def amateur_kernel(sums_ref, got_ref, gain_ref, o_ref, kinds_s):
    base = split_kinds(residual_rows(got_ref), kinds_s)[1]
    hidden = (base + add_all(sums_ref, 0, REQ)).astype(BF16).astype(F32)
    o_ref[...] = (hidden * gain_ref[...].astype(F32)).astype(BF16)


def amateur_rows(sums, got, gain):
    near = pl.BlockSpec(memory_space=pltpu.VMEM)
    return pl.pallas_call(
        amateur_kernel,
        in_specs=[near] * 3,
        out_specs=near,
        out_shape=jax.ShapeDtypeStruct((REQ, COLS), BF16),
        scratch_shapes=[pltpu.VMEM((COLS // HD, 128, HD), F32)],
        compiler_params=params(16),
        cost_estimate=pl.CostEstimate(flops=10**6, bytes_accessed=2 * MIB, transcendentals=0),
    )(sums, got, gain)


def expert_kernel(idx_ref, sums_ref, got_ref, gain_ref, table_ref, o_ref, rows_s, kinds_s, sem):
    start_rows(idx_ref, table_ref, rows_s, sem)
    base = split_kinds(residual_rows(got_ref), kinds_s)[0] + add_all(sums_ref, 0, REQ)
    rank = add_all(sums_ref, REQ, SENT)
    wait_rows(table_ref, rows_s, sem)
    rows = rows_s[...].reshape(REQ * RANK, COLS)
    delta = jnp.zeros((REQ, COLS), F32)
    for n in range(2):
        vector = rank[n : n + 1, :] + rank[n + 2 : n + 3, :]
        spread = jnp.where(own_lanes(REQ, COLS, 1, n * (COLS // RANK)), vector, 0.0)
        high = spread.astype(BF16)
        low = (spread - high.astype(F32)).astype(BF16)
        part = rows[n * COLS : (n + 1) * COLS, :]
        delta = delta + jnp.dot(high, part, preferred_element_type=F32)
        delta = delta + jnp.dot(low, part, preferred_element_type=F32)
    hidden = (base + LOWRANK_SCALE * delta).astype(BF16).astype(F32)
    o_ref[...] = (hidden * gain_ref[...].astype(F32)).astype(BF16)


def expert_rows(index, sums, got, gain, table):
    near = pl.BlockSpec(memory_space=pltpu.VMEM)
    return pl.pallas_call(
        expert_kernel,
        in_specs=[pl.BlockSpec(memory_space=pltpu.SMEM)]
        + [near] * 3
        + [pl.BlockSpec(memory_space=pl.ANY)],
        out_specs=near,
        out_shape=jax.ShapeDtypeStruct((REQ, COLS), BF16),
        scratch_shapes=[
            pltpu.VMEM((REQ, RANK, COLS), BF16),
            pltpu.VMEM((COLS // HD, 128, HD), F32),
            pltpu.SemaphoreType.DMA,
        ],
        compiler_params=params(56),
        cost_estimate=pl.CostEstimate(flops=3 * 10**8, bytes_accessed=2 * MIB, transcendentals=0),
    )(index, sums, got, gain, table)


def tensor_index(at, first, second):
    along_x = jnp.where(at[3] == 0, first, second)
    along_z = jnp.where(at[3] == 0, second, first)
    return lax.rem(at[1] + along_x, 4) * 4 + lax.rem(at[2] + along_z, 4)


ROWS = NY * REQ
PAIR = 2 * COLS
BOTH = 2 * VOC


def head_kernel(pieces, first, last, amateur, at_ref, inv_ref, *refs):
    count = 1 + max(piece[0] for piece in pieces)
    x_refs, wo_ref, ws_ref, refs = refs[:count], refs[count], refs[count + 1], refs[count + 2 :]
    if not first:
        sums_ref, square_ref, refs = refs[0], refs[1], refs[2:]
    if last:
        other_ref, other_lse_ref, uo_ref, us_ref, lse_ref = refs[:5]
        x_s, w_s, acc_s, sq_s, x_sem, w_sem, in_sem, q_sem, other_s, o_sem = refs[5:]
    else:
        out_ref, squares_ref, x_s, w_s, acc_s, sq_s, x_sem, w_sem, in_sem, q_sem = refs

    if not first:
        pltpu.make_async_copy(square_ref, sq_s, q_sem).start()
        pltpu.make_async_copy(sums_ref, acc_s, in_sem).start()
    starts = []
    for n, (which, block, offsets) in enumerate(pieces):
        index = tensor_index(at_ref, *offsets)
        start = pl.multiple_of(index * COLS, COLS)
        starts.append(start)
        run, part = n // 2, pl.ds(n % 2 * COLS, COLS)
        for y in range(NY):
            source = x_refs[which].at[block, y]
            place = lax.rem(at_ref[0] + y, NY)
            pltpu.make_async_copy(source, x_s.at[run, place, :, part], x_sem.at[run]).start()
        for side, w_ref in enumerate((wo_ref, ws_ref)):
            pltpu.make_async_copy(
                w_ref.at[pl.ds(start, COLS), :],
                w_s.at[run, part, pl.ds(side * VOC, VOC)],
                w_sem.at[run],
            ).start()
    if not first:
        pltpu.make_async_copy(square_ref, sq_s, q_sem).wait()
        pltpu.make_async_copy(sums_ref, acc_s, in_sem).wait()
    else:
        acc_s[...] = jnp.zeros((ROWS, BOTH), F32)
        sq_s[...] = jnp.zeros((ROWS, HD), F32)
    if last:
        pltpu.make_async_copy(other_ref, other_s, o_sem).start()

    def one(run, carry):
        pltpu.make_async_copy(x_s.at[run], x_s.at[run], x_sem.at[run]).wait()
        pltpu.make_async_copy(w_s.at[run], w_s.at[run], w_sem.at[run]).wait()
        x = x_s[run].reshape(ROWS, PAIR)
        acc_s[...] += jnp.dot(x, w_s[run], preferred_element_type=F32)
        return carry

    lax.fori_loop(0, len(pieces) // 2, one, 0)

    square = sq_s[...]
    for n, start in enumerate(starts):
        for j in range(COLS // HD):
            lanes = slice(n % 2 * COLS + j * HD, n % 2 * COLS + (j + 1) * HD)
            piece = x_s[n // 2, :, :, lanes].reshape(ROWS, HD).astype(F32)
            inverse = inv_ref[:, pl.ds(pl.multiple_of(start + j * HD, HD), HD)]
            square = square + piece * piece * inverse
    if not (last or amateur):
        sq_s[...] = square
        pltpu.make_async_copy(sq_s, squares_ref, q_sem).start()
        pltpu.make_async_copy(acc_s, out_ref, in_sem).start()
        pltpu.make_async_copy(sq_s, squares_ref, q_sem).wait()
        pltpu.make_async_copy(acc_s, out_ref, in_sem).wait()
        return

    factor = lax.rsqrt(jnp.sum(square, axis=1, keepdims=True) * (1.0 / WIDTH) + EPS)
    logits = acc_s[...] * factor
    peak = jnp.max(logits, axis=1, keepdims=True)
    lse = peak + jnp.log(jnp.sum(jnp.exp(logits - peak), axis=1, keepdims=True))
    sq_s[...] = jnp.broadcast_to(lse, (ROWS, HD))
    lse = jnp.transpose(sq_s[...])[0:1, :]
    if amateur:
        acc_s[...] = logits
        squares_ref[...] = lse
        pltpu.make_async_copy(acc_s, out_ref, in_sem).start()
        pltpu.make_async_copy(acc_s, out_ref, in_sem).wait()
        return
    lse_ref[:, 0:ROWS] = lse
    lse_ref[:, ROWS:] = other_lse_ref[...]
    pltpu.make_async_copy(other_ref, other_s, o_sem).wait()
    mixed = (1.0 + BETA) * logits - BETA * other_s[...]
    uo_ref[...] = mixed[:, :VOC]
    us_ref[...] = mixed[:, VOC:]


def head_part(place, arrays, pieces, inverse, w_own, w_sib, sums=None, other=None, amateur=False):
    first, last = sums is None, other is not None
    depth = len(pieces) * COLS
    runs = len(pieces) // 2
    near = pl.BlockSpec(memory_space=pltpu.VMEM)
    far = pl.BlockSpec(memory_space=pl.ANY)
    if last:
        shapes, out_specs = [(ROWS, VOC), (ROWS, VOC), (1, 2 * ROWS)], [near] * 3
    elif amateur:
        shapes, out_specs = [(ROWS, BOTH), (1, ROWS)], [far, near]
    else:
        shapes, out_specs = [(ROWS, BOTH), (ROWS, HD)], [far, far]
    dma = pltpu.SemaphoreType.DMA
    return pl.pallas_call(
        lambda *refs: head_kernel(pieces, first, last, amateur, *refs),
        in_specs=[pl.BlockSpec(memory_space=pltpu.SMEM), near]
        + [far] * (len(arrays) + 2 + (0 if first else 2))
        + ([far, near] if last else []),
        out_specs=out_specs,
        out_shape=[jax.ShapeDtypeStruct(shape, F32) for shape in shapes],
        scratch_shapes=[
            pltpu.VMEM((runs, NY, REQ, PAIR), BF16),
            pltpu.VMEM((runs, PAIR, BOTH), BF16),
            pltpu.VMEM((ROWS, BOTH), F32),
            pltpu.VMEM((ROWS, HD), F32),
            dma((runs,)),
            dma((runs,)),
            dma,
            dma,
        ]
        + ([pltpu.VMEM((ROWS, BOTH), F32), dma] if last else []),
        compiler_params=params(56),
        cost_estimate=pl.CostEstimate(
            flops=ROWS * depth,
            bytes_accessed=depth * 64,
            transcendentals=0,
        ),
    )(place, inverse, *arrays, w_own, w_sib, *(sums or ()), *(other or ()))


def contrast_kernel(core_ref, uo_ref, us_ref, no_ref, ns_ref, o_ref):
    core = core_ref[0]
    for u_ref, n_ref, parity in ((uo_ref, no_ref, core), (us_ref, ns_ref, 1 - core)):
        column = jnp.transpose(jnp.broadcast_to(n_ref[...], (HD, 512)))
        for y in range(NY):
            a, b = y * REQ, ROWS + y * REQ
            shift = (1.0 + BETA) * column[a : a + REQ] - BETA * column[b : b + REQ]
            rows = pl.ds(pl.multiple_of((2 * y + parity) * REQ, REQ), REQ)
            for j in range(VOC // HD):
                lanes = slice(j * HD, (j + 1) * HD)
                o_ref[rows, lanes] = u_ref[y * REQ : (y + 1) * REQ, lanes] - shift


def contrast(core, u_own, u_sib, norm_own, norm_sib):
    near = pl.BlockSpec(memory_space=pltpu.VMEM)
    return pl.pallas_call(
        contrast_kernel,
        in_specs=[pl.BlockSpec(memory_space=pltpu.SMEM)] + [near] * 4,
        out_specs=near,
        out_shape=jax.ShapeDtypeStruct((512, VOC), F32),
        compiler_params=params(16),
        cost_estimate=pl.CostEstimate(flops=10**6, bytes_accessed=4 * MIB, transcendentals=65536),
    )(core, u_own, u_sib, norm_own, norm_sib)


TENSOR = ("x", "z")
SWAP = [(0, 1), (1, 0)]


def combine(lse):
    peak = lse[0]
    for part in lse[1:]:
        peak = jnp.maximum(peak, part)
    total = jnp.exp(lse[0] - peak)
    for part in lse[1:]:
        total = total + jnp.exp(part - peak)
    return peak + jnp.log(total)


def from_offset(array, axis, offset):
    return lax.ppermute(array, axis, [((i + offset) % 4, i) for i in range(4)])


def from_core_offset(array, axes, offset):
    pairs = []
    for c in range(2):
        for x in range(4):
            for z in range(4):
                far_x = (x + offset) % 4 if axes[c] == "x" else x
                far_z = (z + offset) % 4 if axes[c] == "z" else z
                pairs.append((c * 16 + far_x * 4 + far_z, c * 16 + x * 4 + z))
    return lax.ppermute(array, ("c", "x", "z"), pairs)


FIRST = ("x", "z")
SECOND = ("z", "x")


def plane_of(rows):
    return jnp.stack([rows] + [from_offset(rows, "y", d) for d in range(1, 4)])


def block_of(plane):
    return jnp.stack([plane] + [from_core_offset(plane, FIRST, d) for d in range(1, 4)])


def opposite(after, before, axes):
    half = after.shape[0] // 2
    return from_core_offset(after[:half], axes, 1), from_core_offset(before[half:], axes, 3)


def per_device(
    queries,
    cached_key_rows,
    cached_value_rows,
    current_token_key,
    current_token_value,
    lengths,
    residual,
    output_projection_weight,
    request_adapter_index,
    lowrank_down_factors,
    lowrank_up_factors,
    final_norm_scale,
    vocabulary_head_matrix,
):
    core = lax.axis_index("c").astype(jnp.int32).reshape(1)
    place = jnp.stack([lax.axis_index(axis) for axis in ("y", "x", "z", "c")]).astype(jnp.int32)
    head_sib = lax.ppermute(vocabulary_head_matrix, "c", SWAP)
    down = lax.all_gather(lowrank_down_factors, ("y", "c"), axis=0, tiled=True)
    up = lax.all_gather(lowrank_up_factors, ("y", "c"), axis=0, tiled=True)
    gain = lax.dynamic_slice(final_norm_scale, (lax.axis_index(TENSOR) * COLS,), (COLS,))
    gain = gain.reshape(1, COLS)
    inverse = 1.0 / final_norm_scale.astype(F32)
    inverse = (inverse * inverse).reshape(1, WIDTH)

    sent = attention(
        queries,
        cached_key_rows,
        cached_value_rows,
        current_token_key,
        current_token_value,
        lengths,
        residual,
    )
    got = lax.all_to_all(sent, TENSOR, split_axis=0, concat_axis=0, tiled=True)
    expert, amateur = projection(got, output_projection_weight)
    amateur = lax.all_to_all(amateur, TENSOR, split_axis=0, concat_axis=0, tiled=True)
    amateur = amateur_rows(amateur, got, gain)
    expert = with_rank_sums(request_adapter_index, got, down, expert)
    sums = lax.all_to_all(expert, TENSOR, split_axis=0, concat_axis=0, tiled=True)
    amateur, _ = lax.optimization_barrier((amateur, expert))
    amateur, sums = lax.optimization_barrier((plane_of(amateur), sums))
    amateur, sums = lax.optimization_barrier((block_of(amateur), sums))
    amateur_after = from_core_offset(amateur, SECOND, 1)
    amateur_before = from_core_offset(amateur, SECOND, 3)
    expert = plane_of(expert_rows(request_adapter_index, sums, got, gain, up))
    expert, amateur_after, amateur_before = lax.optimization_barrier(
        (expert, amateur_after, amateur_before)
    )
    amateur_far = opposite(amateur_after, amateur_before, SECOND)
    expert, *amateur_far = lax.optimization_barrier((block_of(expert), *amateur_far))
    after = from_core_offset(expert, SECOND, 1)
    before = from_core_offset(expert, SECOND, 3)
    weights = (inverse, vocabulary_head_matrix, head_sib)
    own = [(0, n, (n, 0)) for n in range(4)]
    beside = [(n // 4, n % 4, (n % 4, 1 + 2 * (n // 4))) for n in range(8)]
    across = [(n // 2, n % 2, (n, 2)) for n in range(4)]
    pieces = own + [(1 + n, b, o) for n, b, o in beside] + [(3 + n, b, o) for n, b, o in across]
    arrays = [amateur, amateur_after, amateur_before, *amateur_far]
    other = head_part(place, arrays, pieces, *weights, amateur=True)
    after, before, *other = lax.optimization_barrier((after, before, *other))
    far = opposite(after, before, SECOND)
    pieces = own + [(1 + n, b, o) for n, b, o in beside]
    partial = head_part(place, [expert, after, before], pieces, *weights)
    u_own, u_send, lse = head_part(place, far, across, *weights, sums=partial, other=other)
    for axis in ("y", "x", "z"):
        lse = combine([lse] + [from_offset(lse, axis, d) for d in range(1, 4)])
        if axis == "y":
            u_send, lse = lax.optimization_barrier((u_send, lse))
            u_sib = lax.ppermute(u_send, "c", SWAP)
    return contrast(core, u_own, u_sib, lse, lax.ppermute(lse, "c", SWAP))


def solution(mesh):
    fine = Mesh(np.asarray(mesh.devices).reshape(NY, 2, 4, 4), ("y", "c", "x", "z"))
    every = ("y", "c", "x", "z")
    group = ("y", "c")
    in_specs = (
        P(every, None, None),
        P(every, None, None, None),
        P(every, None, None, None),
        P(every, None, None),
        P(every, None, None),
        P(every),
        P(every, None, None),
        P(TENSOR, None),
        P(group),
        P(group, None, TENSOR),
        P(group, None, TENSOR),
        P(),
        P(None, every),
    )
    return jax.shard_map(
        per_device, mesh=fine, in_specs=in_specs, out_specs=P(None, every), check_vma=False
    )
```
